32 devices in a mesh: groups: 2 (over y), dp: 8 (over z, x), sub: 2 (over core).
Axes of the slice: x: 2, y: 2, z: 4, core: 2. Of those that a mesh axis runs over, the one named last changes fastest.
Arguments:
- queries: bfloat16 [32, 128, 576], P(('groups', 'dp', 'sub')), parts along dimension 0, may hold values from -100 to 100
- new_latent: bfloat16 [32, 576], P(('groups', 'dp', 'sub')), parts along dimension 0, may hold values from -4 to 4
- cache: bfloat16 [32, 384, 576], P(('groups', 'dp', 'sub')), parts along dimension 0, may hold values from -4 to 4
- lengths: int32 [32], P('groups'), parts along dimension 0, may hold values from 2 to 383
- moves: int32 [4, 3], P('groups'), parts along dimension 0, may hold values from 0 to 15, as said below
- resid: bfloat16 [32, 7168], P(('groups', 'dp', 'sub')), parts along dimension 0, may hold values from -6 to 6
- w_uv: bfloat16 [128, 512, 128], P('dp'), may hold values from -0.25 to 0.25
- w_out: bfloat16 [16384, 7168], P('dp'), may hold values from -0.1875 to 0.1875
- norm_gain: bfloat16 [7168], replicated, may hold values from 0.099609375 to 1.8984375
- w_gate: bfloat16 [7168, 9216], P(None, ('dp', 'sub')), may hold values from -0.0625 to 0.0625
- w_up: bfloat16 [7168, 9216], P(None, ('dp', 'sub')), may hold values from -0.0625 to 0.0625
- w_down: bfloat16 [9216, 7168], P(None, ('dp', 'sub')), may hold values from -0.0625 to 0.0625
Outputs:
- cache_out: bfloat16 [32, 384, 576], P(('groups', 'dp', 'sub')), parts along dimension 0
- spare_out: bfloat16 [32, 192, 576], P(('groups', 'dp', 'sub')), parts along dimension 0
- mixed: bfloat16 [32, 7168], P('groups', ('dp', 'sub')), parts along dimension 0
The draws below stay inside these ranges and needn't reach their ends.
There are 2 independent parts, one for each index of `groups`. The reference program is written for one: setup_inputs(seed, part) draws one part's arguments, and reference() takes and returns one part's arrays. A program takes and returns all parts, laid end to end along the dimension named above; an argument that names none is the same for every part. Nothing has to cross between parts.
Inputs may be any that keep to these rules, and one draw needn't show every extreme that they name: `moves`: each row is (request, source rank, destination rank) with request = source rank * 2 + the request's sub index; rows s * (1) to (s + 1) * 1 - 1 are those of sub index s; a request slot is the source of at most one row and the destination of at most one, never both; every migrated request is longer than 192.
All inputs are finite; a program needn't handle non-finite values.
Results may differ from the reference program's by a relative error of at most 0.0067.
Values may be sent and summed in bfloat16 or wider, within the bound.
No kernel may reach another device: no remote copies, remote signals or barrier semaphores. Data moves between devices by JAX's collectives and lax.ppermute only.
A program may use at most 128 MiB of HBM per device.

```python
import jax
import jax.numpy as jnp
from jax import lax

D = 7168
HEADS = 128
LAT = 512
ROPE = 64
VH = 128
FF = 9216
CAP = 384
RQ = 16
N_DP = 8
N_SUB = 2


def plan(key):
    perm_keys = jax.random.split(jax.random.fold_in(key, 1), N_SUB)
    perms = jax.vmap(lambda k: jax.random.permutation(k, N_DP))(perm_keys)
    place = jnp.argsort(perms, axis=1)
    long_len = jax.random.randint(jax.random.fold_in(key, 2), (N_SUB, N_DP), CAP // 2 + 1, CAP)
    short_len = jax.random.randint(jax.random.fold_in(key, 3), (N_SUB, N_DP), 2, CAP // 4 + 1)
    lens = jnp.where(place < N_DP // 4, long_len, short_len)
    sub_ids = jnp.arange(N_SUB, dtype=jnp.int32)[:, None]
    ranks = jnp.arange(N_DP, dtype=jnp.int32)[None, :]
    lens = jnp.where((sub_ids == N_SUB - 1) & (ranks == N_DP - 1), CAP - 1, lens)
    lens = jnp.where((sub_ids == 0) & (ranks == 0), 2, lens)
    score = lens * (2 * N_DP) + ranks
    ranked = jnp.argsort(-score, axis=1)
    count = N_DP // 8
    heavy = ranked[:, :count]
    light = ranked[:, ::-1][:, :count]
    request = heavy * N_SUB + sub_ids
    moves = jnp.stack([request, heavy, light], axis=-1).reshape(-1, 3)
    lengths = lens.T.reshape(-1)
    return (lengths.astype(jnp.int32), moves.astype(jnp.int32))


def draw_lengths(key, part):
    lengths, moves = plan(key)
    return lengths


def draw_moves(key, part):
    lengths, moves = plan(key)
    return moves


def draw_cache(key, part):
    key = jax.random.fold_in(key, 3)
    vals = jax.random.truncated_normal(key, -4.0, 4.0, (RQ, CAP, LAT + ROPE), jnp.float32)
    return vals.astype(jnp.bfloat16)


def draw_queries(key, part):
    key = jax.random.fold_in(key, 5)
    vals = jax.random.truncated_normal(key, -4.0, 4.0, (RQ, HEADS, LAT + ROPE), jnp.float32)
    return vals.astype(jnp.bfloat16)


def block_scale(stream_key, shape, cuts, low, high):
    gain, own = 1.0, jax.random.fold_in(stream_key, 6)
    for axis_at, shards_of in cuts:
        heights = jnp.exp(jax.random.uniform(jax.random.fold_in(own, axis_at), (shards_of,), jnp.float32, low / len(cuts), high / len(cuts)))
        gain = gain * jnp.repeat(heights, shape[axis_at] // shards_of).reshape([-1 if axis == axis_at else 1 for axis in range(len(shape))])
    return gain


def scatter_about(rng, extent, width, limit, cuts=(), held_as=jnp.bfloat16):
    entries = jax.random.normal(rng, extent, jnp.float32) * width
    if len(cuts) > 0:
        entries = block_scale(rng, extent, cuts, -0.22, 0.18) * entries
    return jnp.clip(entries, min=-limit, max=limit).astype(held_as)


def setup_inputs(seed: int = 0, part: int = 0) -> dict:
    key_of = jax.random.split(jax.random.key(seed), 13)
    part_keys = jax.random.split(jax.random.fold_in(key_of[12], part), 13)
    return {
        "queries": draw_queries(jax.random.fold_in(jax.random.fold_in(key_of[12], part), 71), part),
        "new_latent": scatter_about(part_keys[1], (RQ, LAT + ROPE), 1.0, 4.0, ((0, 16),)),
        "cache": draw_cache(jax.random.fold_in(jax.random.fold_in(key_of[12], part), 71), part),
        "lengths": draw_lengths(jax.random.fold_in(jax.random.fold_in(key_of[12], part), 71), part),
        "moves": draw_moves(jax.random.fold_in(jax.random.fold_in(key_of[12], part), 71), part),
        "resid": scatter_about(part_keys[5], (RQ, D), 1.0, 6.0, ((0, 16),)),
        "w_uv": scatter_about(key_of[6], (HEADS, LAT, VH), LAT ** -0.5, 0.25, ((0, 8),)),
        "w_out": scatter_about(key_of[7], (HEADS * VH, D), (8 * VH) ** -0.5, 0.1875, ((0, 8),)),
        "norm_gain": jnp.clip(1.0 + 0.18 * jax.random.normal(key_of[8], (D,), jnp.float32), 0.099609375, 1.8984375).astype(jnp.bfloat16),
        "w_gate": scatter_about(key_of[9], (D, FF), D ** -0.5, 0.0625, ((1, 16),)),
        "w_up": scatter_about(key_of[10], (D, FF), D ** -0.5, 0.0625, ((1, 16),)),
        "w_down": scatter_about(key_of[11], (FF, D), FF ** -0.5, 0.0625, ((1, 16),)),
    }


def attend(query, keys, length):
    positions = jnp.arange(CAP, dtype=jnp.int32)
    live = positions <= length
    scale = (VH + ROPE) ** (-0.5)
    scores = jnp.dot(query, keys.T, preferred_element_type=jnp.float32) * scale
    scores = jnp.where(live[None, :], scores, -1e+30)
    top = lax.optimization_barrier(jnp.max(scores, axis=1))
    weights = jnp.where(live[None, :], jnp.exp(scores - top[:, None]), 0.0)
    total = lax.optimization_barrier(jnp.sum(weights, axis=1))
    acc = jnp.dot(weights.astype(jnp.bfloat16), keys[:, :LAT], preferred_element_type=jnp.float32)
    return (acc / total[:, None]).astype(jnp.bfloat16)

def reference(queries, new_latent, cache, lengths, moves, resid, w_uv, w_out, norm_gain, w_gate, w_up, w_down):
    half = CAP // 2
    positions = jnp.arange(CAP, dtype=jnp.int32)
    appended = jnp.where(positions[None, :, None] == lengths[:, None, None], new_latent[:, None, :], cache)
    requests = jnp.arange(RQ, dtype=jnp.int32)
    moved = jnp.any(requests[:, None] == moves[None, :, 0], axis=1)
    upper = (positions >= half)[None, :, None]
    cache_out = jnp.where(moved[:, None, None] & upper, jnp.zeros((), jnp.bfloat16), appended)
    target_req = moves[:, 2] * N_SUB + moves[:, 0] % N_SUB
    match = requests[:, None] == target_req[None, :]
    source_idx = lax.optimization_barrier(jnp.sum(jnp.where(match, moves[None, :, 0], 0), axis=1)).astype(jnp.int32)
    has = jnp.any(match, axis=1)
    spare_out = jnp.where(has[:, None, None], appended[source_idx, half:], jnp.zeros((), jnp.bfloat16))
    o_lat = lax.map(lambda a: attend(a[0], a[1], a[2]), (queries, appended, lengths))
    values = jnp.einsum('rhl,hlv->rhv', o_lat.astype(jnp.float32), w_uv.astype(jnp.float32)).astype(jnp.bfloat16)
    attn = jnp.dot(values.reshape(RQ, HEADS * VH), w_out, preferred_element_type=jnp.float32)
    x_rows = (resid.astype(jnp.float32) + attn).astype(jnp.bfloat16)
    xf = x_rows.astype(jnp.float32)
    normed = (xf * lax.rsqrt(lax.optimization_barrier(jnp.mean(xf * xf, axis=1, keepdims=True)) + 1e-06) * norm_gain.astype(jnp.float32)).astype(jnp.bfloat16)
    gate = jnp.dot(normed, w_gate, preferred_element_type=jnp.float32)
    up_part = jnp.dot(normed, w_up, preferred_element_type=jnp.float32)
    hidden = (jax.nn.silu(gate) * up_part).astype(jnp.bfloat16)
    down = jnp.dot(hidden, w_down, preferred_element_type=jnp.float32)
    mixed = (xf + down).astype(jnp.bfloat16)
    return (cache_out, spare_out, mixed)
```

```python
import functools

import jax
import jax.numpy as jnp
from jax import lax
from jax.experimental import pallas as pl
from jax.experimental.pallas import tpu as pltpu
from jax.sharding import PartitionSpec as P


def partial_attend(query, keys, live, scale, latent):
    scores = jnp.einsum("hw,pw->hp", query, keys, preferred_element_type=jnp.float32) * scale
    scores = jnp.where(live[None, :], scores, -1e30)
    top = jnp.max(scores, axis=1)
    weights = jnp.where(live[None, :], jnp.exp(scores - top[:, None]), 0.0)
    total = jnp.sum(weights, axis=1)
    acc = jnp.dot(
        weights.astype(jnp.bfloat16), keys[:, :latent], preferred_element_type=jnp.float32
    )
    return (top, total, acc)


def route(spread, partner, present):
    shape = (spread.shape[0],) + (1,) * (spread.ndim - 1)
    picked = jnp.take(spread, partner, axis=0)
    return jnp.where(present.reshape(shape), picked, jnp.zeros((), spread.dtype))


def per_device_any(
    queries, new_latent, cache, lengths, moves, resid, w_uv, w_out, norm_gain, w_gate, w_up, w_down
):
    n_dp = lax.axis_size("dp")
    n_sub = lax.axis_size("sub")
    rank = lax.axis_index("dp")
    core = lax.axis_index("sub")
    device = rank * n_sub + core
    cap = cache.shape[1]
    half = cap // 2
    width = cache.shape[2]
    heads = queries.shape[1]
    latent = w_uv.shape[1]
    scale = (w_uv.shape[2] + width - latent) ** (-0.5)
    length = lax.dynamic_index_in_dim(lengths, device, 0, keepdims=False)
    positions = jnp.arange(cap, dtype=jnp.int32)
    appended = jnp.where((positions == length)[:, None], new_latent[0][None, :], cache[0])
    moved_req = moves[:, 0]
    sources = moves[:, 1]
    targets = moves[:, 2]
    same_core = moved_req % n_sub == core
    sending = jnp.any(moved_req == device)
    peers = jnp.arange(n_dp, dtype=jnp.int32)
    to_match = same_core[None, :] & (peers[:, None] == targets[None, :])
    from_of = jnp.sum(jnp.where(to_match, sources[None, :], 0), axis=1)
    to_has = jnp.any(to_match, axis=1)
    zero_bf = jnp.zeros((), jnp.bfloat16)
    upper = jnp.where(sending, appended[half:], zero_bf).reshape(n_dp, -1)
    spread = lax.all_to_all(upper, "dp", split_axis=0, concat_axis=0, tiled=True)
    landed = lax.all_to_all(
        route(spread, from_of, to_has), "dp", split_axis=0, concat_axis=0, tiled=True
    )
    spare = landed.reshape(half, width)
    kept = jnp.where(sending & (positions >= half)[:, None], zero_bf, appended)
    top, total, acc = partial_attend(queries[0], appended, positions <= length, scale, latent)
    o_lat = (acc / total[:, None]).astype(jnp.bfloat16)
    owners = lax.all_to_all(
        o_lat.reshape(n_dp, heads // n_dp, latent), "dp", split_axis=0, concat_axis=0, tiled=True
    )
    values = jnp.einsum("rhl,hlv->rhv", owners, w_uv, preferred_element_type=jnp.float32).astype(
        jnp.bfloat16
    )
    values = values.reshape(n_dp, -1)
    cols = w_down.shape[1]
    units = w_gate.shape[1]
    col_start = device * cols
    gain = norm_gain.astype(jnp.float32)
    summed = lax.psum_scatter(
        jnp.dot(values, w_out, preferred_element_type=jnp.float32),
        "dp",
        scatter_dimension=0,
        tiled=True,
    )
    x_rows = (resid.astype(jnp.float32) + summed).astype(jnp.bfloat16)
    piece = lax.all_gather(x_rows, ("dp", "sub"), axis=0, tiled=True)
    xf = piece.astype(jnp.float32)
    normed = (xf * lax.rsqrt(jnp.mean(xf * xf, axis=1, keepdims=True) + 1e-06) * gain).astype(
        jnp.bfloat16
    )
    gate = jnp.dot(normed, w_gate, preferred_element_type=jnp.float32)
    up_part = jnp.dot(normed, w_up, preferred_element_type=jnp.float32)
    hidden_part = (jax.nn.silu(gate) * up_part).astype(jnp.bfloat16)
    own_cols = lax.dynamic_slice_in_dim(piece, col_start, cols, 1)
    joined = jnp.concatenate([hidden_part, own_cols], axis=1)
    hidden = joined[:, :units]
    base = joined[:, units:]
    down = jnp.dot(
        lax.all_gather(hidden, ("dp", "sub"), axis=1, tiled=True),
        w_down,
        preferred_element_type=jnp.float32,
    )
    mixed = (base.astype(jnp.float32) + down).astype(jnp.bfloat16)
    return (kept[None], spare[None], mixed)


VMEM = pl.BlockSpec(memory_space=pltpu.VMEM)
SMEM = pl.BlockSpec(memory_space=pltpu.SMEM)
HBM = pl.BlockSpec(memory_space=pl.ANY)
NT = (((1,), (1,)), ((), ()))
TN = (((0,), (0,)), ((), ()))


def params(mib):
    return pltpu.CompilerParams(vmem_limit_bytes=mib << 20)


def place(n_sub):
    rank = lax.axis_index("dp")
    core = lax.axis_index("sub")
    return jnp.stack([rank, core, rank * n_sub + core]).astype(jnp.int32)


def attend_kernel(
    scale, n_dp, n_sub, at, lengths, moves, q_ref, fresh_ref, cache_ref, kept_ref, out_ref
):
    width, cap = cache_ref.shape
    half = cap // 2
    latent = 512
    heads = q_ref.shape[1]
    device = at[2]
    length = lengths[device]
    sending = moves[0, 0] == device
    for row in range(1, moves.shape[0]):
        sending = sending | (moves[row, 0] == device)
    fresh = jnp.broadcast_to(fresh_ref[...].astype(jnp.float32), (128, width)).T
    fresh = jnp.concatenate([fresh] * (cap // 128), axis=1)
    positions = lax.broadcasted_iota(jnp.int32, (width, cap), 1)
    appended = jnp.where(positions == length, fresh, cache_ref[...].astype(jnp.float32))
    drop = jnp.where(sending, half, cap)
    kept_ref[...] = jnp.where(positions >= drop, 0.0, appended).astype(jnp.bfloat16)
    keys = appended.astype(jnp.bfloat16)
    scores = lax.dot_general(q_ref[...], keys, TN, preferred_element_type=jnp.float32) * scale
    live = lax.broadcasted_iota(jnp.int32, (heads, cap), 1) <= length
    scores = jnp.where(live, scores, -1e30)
    top = jnp.max(scores, axis=1, keepdims=True)
    weights = jnp.where(live, jnp.exp(scores - top), 0.0)
    total = jnp.sum(weights, axis=1, keepdims=True)
    acc = lax.dot_general(
        weights.astype(jnp.bfloat16), keys[:latent], NT, preferred_element_type=jnp.float32
    )
    o_lat = (acc / total).astype(jnp.bfloat16)
    share = heads // n_dp
    rows = half // n_dp
    upper = jnp.where(sending, appended.T[half:], 0.0)
    for peer in range(n_dp):
        out_ref[peer, 0:share, 0:latent] = o_lat[peer * share : (peer + 1) * share]
        out_ref[peer, 0:share, latent:width] = jnp.zeros((share, width - latent), jnp.bfloat16)
        out_ref[peer, share : share + rows, :] = upper[peer * rows : (peer + 1) * rows].astype(
            jnp.bfloat16
        )


def values_kernel(got_ref, uv_ref, out_ref, wide):
    n_dp = got_ref.shape[0]
    share, latent, vh = uv_ref.shape
    for src in range(n_dp):
        for k in range(latent // 128):
            wide[k, src * share : (src + 1) * share, :] = got_ref[
                src, 0:share, 128 * k : 128 * (k + 1)
            ].astype(jnp.float32)
    for head in range(share):
        rows = jnp.concatenate(
            [wide[k, pl.ds(head, n_dp, stride=share), :] for k in range(latent // 128)], axis=1
        ).astype(jnp.bfloat16)
        out_ref[:, head * vh : (head + 1) * vh] = jnp.dot(
            rows, uv_ref[head], preferred_element_type=jnp.float32
        ).astype(jnp.bfloat16)


def interleave(first, second):
    n = first.shape[0]
    row = lax.broadcasted_iota(jnp.int32, (2 * n, 2 * n), 0)
    col = lax.broadcasted_iota(jnp.int32, (2 * n, 2 * n), 1)
    pick = (col == (row % 2) * n + row // 2).astype(jnp.bfloat16)
    both = jnp.concatenate([first, second], axis=0)
    return jnp.dot(pick, both, preferred_element_type=jnp.float32).astype(jnp.bfloat16)


def project_kernel(at, own_ref, peer_ref, w_ref, out_ref, weights, sems):
    chunks = sems.shape[0]
    n_dp = out_ref.shape[0]
    per = out_ref.shape[1]
    half = out_ref.shape[2]
    wide = half // chunks
    core = at[1]

    def fetch(i):
        start = pl.multiple_of(core * half + i * wide, 128)
        return pltpu.make_async_copy(
            w_ref.at[:, pl.ds(start, wide)], weights.at[i], sems.at[i]
        )

    for i in range(chunks):
        fetch(i).start()
    own = own_ref[...].astype(jnp.float32)
    peer = peer_ref[...].astype(jnp.float32)
    first = jnp.where(core == 0, own, peer).astype(jnp.bfloat16)
    second = jnp.where(core == 0, peer, own).astype(jnp.bfloat16)
    values = interleave(first, second)
    for i in range(chunks):
        fetch(i).wait()
        part = jnp.dot(values, weights[i], preferred_element_type=jnp.float32)
        for dst in range(n_dp):
            out_ref[dst, :, i * wide : (i + 1) * wide] = part[dst * per : (dst + 1) * per]


def sum_kernel(n_sub, at, moves, part_ref, resid_ref, got_ref, out_ref):
    n_dp, per, half = part_ref.shape
    rows_at = 16
    rows = out_ref.shape[1] - rows_at
    total = resid_ref[...].astype(jnp.float32)
    for src in range(n_dp):
        total = total + part_ref[src]
    x = total.astype(jnp.bfloat16)
    core = at[1]
    for dst in range(n_dp):
        for k in range(half // 512):
            out_ref[dst, per * k : per * (k + 1), 0:512] = x[:, 512 * k : 512 * (k + 1)]
        source = jnp.int32(0)
        found = jnp.int32(0)
        for row in range(moves.shape[0]):
            hit = (moves[row, 2] == dst) & (moves[row, 0] % n_sub == core)
            source = jnp.where(hit, moves[row, 1], source)
            found = jnp.where(hit, 1, found)

        @pl.when(found == 1)
        def _():
            out_ref[dst, rows_at : rows_at + rows, :] = got_ref[source, rows_at : rows_at + rows, :]

        @pl.when(found == 0)
        def _():
            out_ref[dst, rows_at : rows_at + rows, :] = jnp.zeros(
                (rows, out_ref.shape[2]), jnp.bfloat16
            )


def gate_up_kernel(x_ref, gain_ref, gate_ref, up_ref, out_ref, weights, sems):
    chunks = sems.shape[0] // 2
    tall = weights.shape[1]

    def fetch(i):
        ref = gate_ref if i % 2 == 0 else up_ref
        return pltpu.make_async_copy(
            ref.at[pl.ds((i // 2) * tall, tall), :], weights.at[i], sems.at[i]
        )

    for i in range(2 * chunks):
        fetch(i).start()
    xf = x_ref[...].astype(jnp.float32)
    inverse = lax.rsqrt(jnp.mean(xf * xf, axis=1, keepdims=True) + 1e-06)
    normed = (xf * inverse * gain_ref[...].astype(jnp.float32)).astype(jnp.bfloat16)
    for i in range(chunks):
        fetch(2 * i).wait()
        gate = lax.dot_general(weights[2 * i], normed, NT, preferred_element_type=jnp.float32)
        fetch(2 * i + 1).wait()
        up = lax.dot_general(weights[2 * i + 1], normed, NT, preferred_element_type=jnp.float32)
        out_ref[i * tall : (i + 1) * tall, :] = (gate * jax.nn.sigmoid(gate) * up).astype(
            jnp.bfloat16
        )


def down_kernel(hidden_ref, down_ref, out_ref, weights, sems):
    chunks = sems.shape[0]
    tall = weights.shape[1]

    def fetch(i):
        return pltpu.make_async_copy(
            down_ref.at[pl.ds(i * tall, tall), :], weights.at[i], sems.at[i]
        )

    for i in range(chunks):
        fetch(i).start()
    hidden = hidden_ref[...]
    for i in range(chunks):
        fetch(i).wait()
        out_ref[i * tall : (i + 1) * tall, :] = lax.dot_general(
            weights[i], hidden, NT, preferred_element_type=jnp.float32
        )


def swap(x, n_sub):
    return lax.ppermute(x, "sub", [(i, (i + 1) % n_sub) for i in range(n_sub)])


def exchange(x):
    return lax.all_to_all(x, "dp", split_axis=0, concat_axis=0, tiled=True)


def per_device_fast(
    queries, new_latent, cache, lengths, moves, resid, w_uv, w_out, norm_gain, w_gate, w_up, w_down
):
    n_dp = lax.axis_size("dp")
    n_sub = lax.axis_size("sub")
    cap, width = cache.shape[1:]
    heads = queries.shape[1]
    share, latent, vh = w_uv.shape
    half = cap // 2
    rows = half // n_dp
    dim = w_out.shape[1]
    requests = n_dp * n_sub
    units = w_gate.shape[1]
    cols = w_down.shape[1]
    scale = (vh + width - latent) ** (-0.5)
    bf16, f32 = jnp.bfloat16, jnp.float32
    at = place(n_sub)
    core = lax.axis_index("sub")

    kept, sent = pl.pallas_call(
        functools.partial(attend_kernel, scale, n_dp, n_sub),
        out_shape=(
            jax.ShapeDtypeStruct((width, cap), bf16),
            jax.ShapeDtypeStruct((n_dp, share + rows, width), bf16),
        ),
        in_specs=[SMEM] * 3 + [VMEM] * 3,
        out_specs=(VMEM, VMEM),
        compiler_params=params(16),
        name="attend",
    )(at, lengths, moves, queries[0].T, new_latent, cache[0].T)
    got = exchange(sent)
    wide_half = dim // n_sub
    mine = lax.dynamic_slice_in_dim(resid, core * wide_half, wide_half, 1)
    other = lax.dynamic_slice_in_dim(resid, (1 - core) * wide_half, wide_half, 1)
    theirs = swap(other, n_sub)
    resid_pair = jnp.where(
        core == 0, jnp.concatenate([mine, theirs]), jnp.concatenate([theirs, mine])
    )
    values = pl.pallas_call(
        values_kernel,
        out_shape=jax.ShapeDtypeStruct((n_dp, share * vh), bf16),
        in_specs=[VMEM] * 2,
        out_specs=VMEM,
        scratch_shapes=[pltpu.VMEM((latent // 128, n_dp * share, 128), f32)],
        compiler_params=params(16),
        name="values",
    )(got, w_uv)
    chunks = 4
    partial = pl.pallas_call(
        project_kernel,
        out_shape=jax.ShapeDtypeStruct((n_dp, n_sub, wide_half), f32),
        in_specs=[SMEM, VMEM, VMEM, HBM],
        out_specs=VMEM,
        scratch_shapes=[
            pltpu.VMEM((chunks, share * vh, wide_half // chunks), bf16),
            pltpu.SemaphoreType.DMA((chunks,)),
        ],
        compiler_params=params(32),
        name="project",
    )(at, values, swap(values, n_sub), w_out)
    summed = exchange(partial)
    routed = pl.pallas_call(
        functools.partial(sum_kernel, n_sub),
        out_shape=jax.ShapeDtypeStruct((n_dp, 16 + rows, width), bf16),
        in_specs=[SMEM] * 2 + [VMEM] * 3,
        out_specs=VMEM,
        compiler_params=params(16),
        name="sum",
    )(at, moves, summed, resid_pair, got)
    landed = exchange(routed)
    spare = landed[:, 16:, :].reshape(half, width)
    x_half = (
        landed[:, : wide_half // 512 * n_sub, :latent]
        .reshape(n_dp, wide_half // 512, n_sub, 512)
        .transpose(0, 2, 1, 3)
        .reshape(requests, wide_half)
    )
    x_peer = swap(x_half, n_sub)
    x = jnp.where(
        core == 0,
        jnp.concatenate([x_half, x_peer], axis=1),
        jnp.concatenate([x_peer, x_half], axis=1),
    )
    chunks = 6
    hidden = pl.pallas_call(
        gate_up_kernel,
        out_shape=jax.ShapeDtypeStruct((units, requests), bf16),
        in_specs=[VMEM, VMEM, HBM, HBM],
        out_specs=VMEM,
        scratch_shapes=[
            pltpu.VMEM((2 * chunks, units // chunks, dim), bf16),
            pltpu.SemaphoreType.DMA((2 * chunks,)),
        ],
        compiler_params=params(40),
        name="gate_up",
    )(x, norm_gain[None], w_gate.T, w_up.T)
    every = exchange(jnp.broadcast_to(hidden.T[None], (n_dp, requests, units)))
    every_peer = swap(every, n_sub)
    pair = jnp.where(
        core == 0,
        jnp.concatenate([every, every_peer], axis=2),
        jnp.concatenate([every_peer, every], axis=2),
    )
    all_hidden = pair.transpose(1, 0, 2).reshape(requests, n_dp * n_sub * units)
    chunks = 4
    down = pl.pallas_call(
        down_kernel,
        out_shape=jax.ShapeDtypeStruct((cols, requests), f32),
        in_specs=[VMEM, HBM],
        out_specs=VMEM,
        scratch_shapes=[
            pltpu.VMEM((chunks, cols // chunks, w_down.shape[0]), bf16),
            pltpu.SemaphoreType.DMA((chunks,)),
        ],
        compiler_params=params(24),
        name="down",
    )(all_hidden, w_down.T)
    base = lax.dynamic_slice_in_dim(x, at[2] * cols, cols, 1)
    mixed = (base.astype(f32) + down.T).astype(bf16)
    return (kept.T[None], spare[None], mixed)


def per_device(*args):
    queries, cache, w_uv, w_out = args[0], args[2], args[6], args[7]
    w_gate, w_down = args[9], args[11]
    n_dp = lax.axis_size("dp")
    n_sub = lax.axis_size("sub")
    fits = (
        n_sub == 2
        and n_dp == 8
        and cache.shape[1] % (2 * 8 * n_dp) == 0
        and queries.shape[1] // n_dp == 16
        and w_uv.shape[1] == 512
        and w_out.shape[1] % (n_sub * 4 * 128) == 0
        and w_gate.shape[1] % 96 == 0
        and w_down.shape[1] % 64 == 0
    )
    return per_device_fast(*args) if fits else per_device_any(*args)


def solution(mesh):
    return jax.shard_map(
        per_device,
        mesh=mesh,
        in_specs=(
            P(("groups", "dp", "sub"), None, None),
            P(("groups", "dp", "sub"), None),
            P(("groups", "dp", "sub"), None, None),
            P("groups"),
            P("groups", None),
            P(("groups", "dp", "sub"), None),
            P("dp", None, None),
            P("dp", None),
            P(),
            P(None, ("dp", "sub")),
            P(None, ("dp", "sub")),
            P(None, ("dp", "sub")),
        ),
        out_specs=(
            P(("groups", "dp", "sub"), None, None),
            P(("groups", "dp", "sub"), None, None),
            P("groups", ("dp", "sub")),
        ),
        check_vma=False,
    )
```

```python
import functools

import jax
import jax.numpy as jnp
from jax import lax
from jax.experimental import pallas as pl
from jax.experimental.pallas import tpu as pltpu
from jax.sharding import PartitionSpec as P


def partial_attend(query, keys, live, scale, latent):
    scores = jnp.einsum("hw,pw->hp", query, keys, preferred_element_type=jnp.float32) * scale
    scores = jnp.where(live[None, :], scores, -1e30)
    top = jnp.max(scores, axis=1)
    weights = jnp.where(live[None, :], jnp.exp(scores - top[:, None]), 0.0)
    total = jnp.sum(weights, axis=1)
    acc = jnp.dot(
        weights.astype(jnp.bfloat16), keys[:, :latent], preferred_element_type=jnp.float32
    )
    return (top, total, acc)


def route(spread, partner, present):
    shape = (spread.shape[0],) + (1,) * (spread.ndim - 1)
    picked = jnp.take(spread, partner, axis=0)
    return jnp.where(present.reshape(shape), picked, jnp.zeros((), spread.dtype))


def per_device_any(
    queries, new_latent, cache, lengths, moves, resid, w_uv, w_out, norm_gain, w_gate, w_up, w_down
):
    n_dp = lax.axis_size("dp")
    n_sub = lax.axis_size("sub")
    rank = lax.axis_index("dp")
    core = lax.axis_index("sub")
    device = rank * n_sub + core
    cap = cache.shape[1]
    half = cap // 2
    width = cache.shape[2]
    heads = queries.shape[1]
    latent = w_uv.shape[1]
    scale = (w_uv.shape[2] + width - latent) ** (-0.5)
    length = lax.dynamic_index_in_dim(lengths, device, 0, keepdims=False)
    positions = jnp.arange(cap, dtype=jnp.int32)
    appended = jnp.where((positions == length)[:, None], new_latent[0][None, :], cache[0])
    moved_req = moves[:, 0]
    sources = moves[:, 1]
    targets = moves[:, 2]
    same_core = moved_req % n_sub == core
    sending = jnp.any(moved_req == device)
    peers = jnp.arange(n_dp, dtype=jnp.int32)
    to_match = same_core[None, :] & (peers[:, None] == targets[None, :])
    from_of = jnp.sum(jnp.where(to_match, sources[None, :], 0), axis=1)
    to_has = jnp.any(to_match, axis=1)
    zero_bf = jnp.zeros((), jnp.bfloat16)
    upper = jnp.where(sending, appended[half:], zero_bf).reshape(n_dp, -1)
    spread = lax.all_to_all(upper, "dp", split_axis=0, concat_axis=0, tiled=True)
    landed = lax.all_to_all(
        route(spread, from_of, to_has), "dp", split_axis=0, concat_axis=0, tiled=True
    )
    spare = landed.reshape(half, width)
    kept = jnp.where(sending & (positions >= half)[:, None], zero_bf, appended)
    top, total, acc = partial_attend(queries[0], appended, positions <= length, scale, latent)
    o_lat = (acc / total[:, None]).astype(jnp.bfloat16)
    owners = lax.all_to_all(
        o_lat.reshape(n_dp, heads // n_dp, latent), "dp", split_axis=0, concat_axis=0, tiled=True
    )
    values = jnp.einsum("rhl,hlv->rhv", owners, w_uv, preferred_element_type=jnp.float32).astype(
        jnp.bfloat16
    )
    values = values.reshape(n_dp, -1)
    cols = w_down.shape[1]
    units = w_gate.shape[1]
    col_start = device * cols
    gain = norm_gain.astype(jnp.float32)
    summed = lax.psum_scatter(
        jnp.dot(values, w_out, preferred_element_type=jnp.float32),
        "dp",
        scatter_dimension=0,
        tiled=True,
    )
    x_rows = (resid.astype(jnp.float32) + summed).astype(jnp.bfloat16)
    piece = lax.all_gather(x_rows, ("dp", "sub"), axis=0, tiled=True)
    xf = piece.astype(jnp.float32)
    normed = (xf * lax.rsqrt(jnp.mean(xf * xf, axis=1, keepdims=True) + 1e-06) * gain).astype(
        jnp.bfloat16
    )
    gate = jnp.dot(normed, w_gate, preferred_element_type=jnp.float32)
    up_part = jnp.dot(normed, w_up, preferred_element_type=jnp.float32)
    hidden_part = (jax.nn.silu(gate) * up_part).astype(jnp.bfloat16)
    own_cols = lax.dynamic_slice_in_dim(piece, col_start, cols, 1)
    joined = jnp.concatenate([hidden_part, own_cols], axis=1)
    hidden = joined[:, :units]
    base = joined[:, units:]
    down = jnp.dot(
        lax.all_gather(hidden, ("dp", "sub"), axis=1, tiled=True),
        w_down,
        preferred_element_type=jnp.float32,
    )
    mixed = (base.astype(jnp.float32) + down).astype(jnp.bfloat16)
    return (kept[None], spare[None], mixed)


VMEM = pl.BlockSpec(memory_space=pltpu.VMEM)
SMEM = pl.BlockSpec(memory_space=pltpu.SMEM)
HBM = pl.BlockSpec(memory_space=pl.ANY)
NT = (((1,), (1,)), ((), ()))
TN = (((0,), (0,)), ((), ()))


def params(mib):
    return pltpu.CompilerParams(vmem_limit_bytes=mib << 20)


def place(n_sub):
    rank = lax.axis_index("dp")
    core = lax.axis_index("sub")
    return rank, core, rank * n_sub + core


def attend_kernel(
    scale, n_dp, n_sub, latent, lengths, moves, q_ref, fresh_ref, cache_ref, kept_ref, out_ref
):
    width, cap = cache_ref.shape
    half = cap // 2
    heads = q_ref.shape[1]
    _, _, device = place(n_sub)
    length = lengths[device]
    sending = moves[0, 0] == device
    for row in range(1, moves.shape[0]):
        sending = sending | (moves[row, 0] == device)
    fresh = jnp.broadcast_to(fresh_ref[...].astype(jnp.float32), (128, width)).T
    fresh = jnp.concatenate([fresh] * (cap // 128), axis=1)
    positions = lax.broadcasted_iota(jnp.int32, (width, cap), 1)
    appended = jnp.where(positions == length, fresh, cache_ref[...].astype(jnp.float32))
    drop = jnp.where(sending, half, cap)
    kept_ref[...] = jnp.where(positions >= drop, 0.0, appended).astype(jnp.bfloat16)
    keys = appended.astype(jnp.bfloat16)
    scores = lax.dot_general(q_ref[...], keys, TN, preferred_element_type=jnp.float32) * scale
    live = lax.broadcasted_iota(jnp.int32, (heads, cap), 1) <= length
    scores = jnp.where(live, scores, -1e30)
    top = jnp.max(scores, axis=1, keepdims=True)
    weights = jnp.where(live, jnp.exp(scores - top), 0.0)
    total = jnp.sum(weights, axis=1, keepdims=True)
    acc = lax.dot_general(
        weights.astype(jnp.bfloat16), keys[:latent], NT, preferred_element_type=jnp.float32
    )
    o_lat = (acc / total).astype(jnp.bfloat16)
    share = heads // n_dp
    rows = half // n_dp
    upper = jnp.where(sending, appended.T[half:], 0.0)
    for peer in range(n_dp):
        out_ref[peer, 0:share, 0:latent] = o_lat[peer * share : (peer + 1) * share]
        out_ref[peer, 0:share, latent:width] = jnp.zeros((share, width - latent), jnp.bfloat16)
        out_ref[peer, share : share + rows, :] = upper[peer * rows : (peer + 1) * rows].astype(
            jnp.bfloat16
        )


def values_kernel(got_ref, uv_ref, out_ref, wide):
    n_dp = got_ref.shape[0]
    share, latent, vh = uv_ref.shape
    for src in range(n_dp):
        for k in range(latent // 128):
            wide[k, src * share : (src + 1) * share, :] = got_ref[
                src, 0:share, 128 * k : 128 * (k + 1)
            ].astype(jnp.float32)
    for head in range(share):
        rows = jnp.concatenate(
            [wide[k, pl.ds(head, n_dp, stride=share), :] for k in range(latent // 128)], axis=1
        ).astype(jnp.bfloat16)
        out_ref[:, head * vh : (head + 1) * vh] = jnp.dot(
            rows, uv_ref[head], preferred_element_type=jnp.float32
        ).astype(jnp.bfloat16)


def interleave(first, second):
    n = first.shape[0]
    row = lax.broadcasted_iota(jnp.int32, (2 * n, 2 * n), 0)
    col = lax.broadcasted_iota(jnp.int32, (2 * n, 2 * n), 1)
    pick = (col == (row % 2) * n + row // 2).astype(jnp.bfloat16)
    both = jnp.concatenate([first, second], axis=0)
    return jnp.dot(pick, both, preferred_element_type=jnp.float32).astype(jnp.bfloat16)


def project_kernel(n_sub, own_ref, peer_ref, w_ref, out_ref, weights, sems):
    chunks = sems.shape[0]
    n_dp = out_ref.shape[0]
    per = out_ref.shape[1]
    half = out_ref.shape[2]
    wide = half // chunks
    _, core, _ = place(n_sub)

    def fetch(i):
        start = pl.multiple_of(core * half + i * wide, 128)
        return pltpu.make_async_copy(
            w_ref.at[:, pl.ds(start, wide)], weights.at[i], sems.at[i]
        )

    for i in range(chunks):
        fetch(i).start()
    own = own_ref[...].astype(jnp.float32)
    peer = peer_ref[...].astype(jnp.float32)
    first = jnp.where(core == 0, own, peer).astype(jnp.bfloat16)
    second = jnp.where(core == 0, peer, own).astype(jnp.bfloat16)
    values = interleave(first, second)
    for i in range(chunks):
        fetch(i).wait()
        part = jnp.dot(values, weights[i], preferred_element_type=jnp.float32)
        for dst in range(n_dp):
            out_ref[dst, :, i * wide : (i + 1) * wide] = part[dst * per : (dst + 1) * per]


def sum_kernel(n_sub, moves, part_ref, resid_ref, theirs_ref, got_ref, out_ref):
    n_dp, per, half = part_ref.shape
    rows_at = 16
    rows = out_ref.shape[1] - rows_at
    _, core, _ = place(n_sub)
    mine = resid_ref[...].astype(jnp.float32)
    theirs = theirs_ref[...].astype(jnp.float32)
    mine = jnp.where(core == 0, mine[:, :half], mine[:, half:])
    theirs = jnp.where(core == 0, theirs[:, :half], theirs[:, half:])
    row = lax.broadcasted_iota(jnp.int32, (per, half), 0)
    total = jnp.where(row == core, mine, theirs)
    for src in range(n_dp):
        total = total + part_ref[src]
    x = total.astype(jnp.bfloat16)
    for dst in range(n_dp):
        for k in range(half // 512):
            out_ref[dst, per * k : per * (k + 1), 0:512] = x[:, 512 * k : 512 * (k + 1)]
        source = jnp.int32(0)
        found = jnp.int32(0)
        for row in range(moves.shape[0]):
            hit = (moves[row, 2] == dst) & (moves[row, 0] % n_sub == core)
            source = jnp.where(hit, moves[row, 1], source)
            found = jnp.where(hit, 1, found)

        @pl.when(found == 1)
        def _():
            out_ref[dst, rows_at : rows_at + rows, :] = got_ref[source, rows_at : rows_at + rows, :]

        @pl.when(found == 0)
        def _():
            out_ref[dst, rows_at : rows_at + rows, :] = jnp.zeros(
                (rows, out_ref.shape[2]), jnp.bfloat16
            )


def unpack_kernel(n_sub, got_ref, x_ref, spare_ref):
    n_dp = got_ref.shape[0]
    rows = spare_ref.shape[0] // n_dp
    half = x_ref.shape[1]
    for k in range(half // 512):
        x_ref[:, 512 * k : 512 * (k + 1)] = jnp.concatenate(
            [
                got_ref[src, n_sub * k : n_sub * (k + 1), 0:512].astype(jnp.float32)
                for src in range(n_dp)
            ],
            axis=0,
        ).astype(jnp.bfloat16)
    for src in range(n_dp):
        spare_ref[src * rows : (src + 1) * rows, :] = got_ref[src, 16 : 16 + rows, :]


def gate_up_kernel(
    n_sub, own_ref, peer_ref, gain_ref, gate_ref, up_ref, out_ref, base_ref, whole, weights, sems
):
    chunks = sems.shape[0] // 2
    tall = weights.shape[1]
    half = own_ref.shape[1]
    cols = base_ref.shape[1]
    rank, core, _ = place(n_sub)

    def fetch(i):
        ref = gate_ref if i % 2 == 0 else up_ref
        return pltpu.make_async_copy(
            ref.at[pl.ds((i // 2) * tall, tall), :], weights.at[i], sems.at[i]
        )

    for i in range(2 * chunks):
        fetch(i).start()
    own = own_ref[...].astype(jnp.float32)
    peer = peer_ref[...].astype(jnp.float32)
    whole[:, :half] = jnp.where(core == 0, own, peer)
    whole[:, half:] = jnp.where(core == 0, peer, own)
    xf = whole[...]
    inverse = lax.rsqrt(jnp.mean(xf * xf, axis=1, keepdims=True) + 1e-06)
    normed = (xf * inverse * gain_ref[...].astype(jnp.float32)).astype(jnp.bfloat16)
    start = pl.multiple_of(rank * n_sub * cols + core * (cols // 128 * 128), 128)
    near = whole[:, pl.ds(start, cols + 64)]
    base_ref[...] = jnp.where(core == 0, near[:, :cols], near[:, 64:]).astype(jnp.bfloat16)
    parts = []
    for i in range(chunks):
        fetch(2 * i).wait()
        gate = lax.dot_general(weights[2 * i], normed, NT, preferred_element_type=jnp.float32)
        fetch(2 * i + 1).wait()
        up = lax.dot_general(weights[2 * i + 1], normed, NT, preferred_element_type=jnp.float32)
        parts.append(gate * jax.nn.sigmoid(gate) * up)
    hidden = jnp.concatenate(parts, axis=0).T.astype(jnp.bfloat16)
    for dst in range(out_ref.shape[0]):
        out_ref[dst] = hidden


def down_kernel(n_sub, own_ref, peer_ref, base_ref, down_ref, out_ref, hidden, weights, sems):
    chunks = sems.shape[0]
    tall = weights.shape[1]
    units = own_ref.shape[2]
    _, core, _ = place(n_sub)

    def fetch(i):
        return pltpu.make_async_copy(
            down_ref.at[pl.ds(i * tall, tall), :], weights.at[i], sems.at[i]
        )

    for i in range(chunks):
        fetch(i).start()
    for src in range(own_ref.shape[0]):
        own = own_ref[src].astype(jnp.float32)
        peer = peer_ref[src].astype(jnp.float32)
        first = jnp.where(core == 0, own, peer)
        second = jnp.where(core == 0, peer, own)
        hidden[:, src * n_sub * units : (src + 1) * n_sub * units] = jnp.concatenate(
            [first, second], axis=1
        ).astype(jnp.bfloat16)
    every = hidden[...]
    parts = []
    for i in range(chunks):
        fetch(i).wait()
        parts.append(
            lax.dot_general(weights[i], every, NT, preferred_element_type=jnp.float32)
        )
    down = jnp.concatenate(parts, axis=0).T
    out_ref[...] = (base_ref[...].astype(jnp.float32) + down).astype(jnp.bfloat16)


def swap(x, n_sub):
    return lax.ppermute(x, "sub", [(i, (i + 1) % n_sub) for i in range(n_sub)])


def exchange(x):
    return lax.all_to_all(x, "dp", split_axis=0, concat_axis=0, tiled=True)


def per_device_fast(
    queries, new_latent, cache, lengths, moves, resid, w_uv, w_out, norm_gain, w_gate, w_up, w_down
):
    n_dp = lax.axis_size("dp")
    n_sub = lax.axis_size("sub")
    cap, width = cache.shape[1:]
    heads = queries.shape[1]
    share, latent, vh = w_uv.shape
    half = cap // 2
    rows = half // n_dp
    dim = w_out.shape[1]
    requests = n_dp * n_sub
    units = w_gate.shape[1]
    cols = w_down.shape[1]
    scale = (vh + width - latent) ** (-0.5)
    bf16, f32 = jnp.bfloat16, jnp.float32

    kept, sent = pl.pallas_call(
        functools.partial(attend_kernel, scale, n_dp, n_sub, latent),
        out_shape=(
            jax.ShapeDtypeStruct((width, cap), bf16),
            jax.ShapeDtypeStruct((n_dp, share + rows, width), bf16),
        ),
        in_specs=[SMEM] * 2 + [VMEM] * 3,
        out_specs=(VMEM, VMEM),
        compiler_params=params(60),
        name="attend",
    )(lengths, moves, queries[0].T, new_latent, cache[0].T)
    got = exchange(sent)
    wide_half = dim // n_sub
    theirs = swap(resid, n_sub)
    values = pl.pallas_call(
        values_kernel,
        out_shape=jax.ShapeDtypeStruct((n_dp, share * vh), bf16),
        in_specs=[VMEM] * 2,
        out_specs=VMEM,
        scratch_shapes=[pltpu.VMEM((latent // 128, n_dp * share, 128), f32)],
        compiler_params=params(60),
        name="values",
    )(got, w_uv)
    chunks = 4
    partial = pl.pallas_call(
        functools.partial(project_kernel, n_sub),
        out_shape=jax.ShapeDtypeStruct((n_dp, n_sub, wide_half), f32),
        in_specs=[VMEM, VMEM, HBM],
        out_specs=VMEM,
        scratch_shapes=[
            pltpu.VMEM((chunks, share * vh, wide_half // chunks), bf16),
            pltpu.SemaphoreType.DMA((chunks,)),
        ],
        compiler_params=params(60),
        name="project",
    )(values, swap(values, n_sub), w_out)
    summed = exchange(partial)
    routed = pl.pallas_call(
        functools.partial(sum_kernel, n_sub),
        out_shape=jax.ShapeDtypeStruct((n_dp, 16 + rows, width), bf16),
        in_specs=[SMEM] + [VMEM] * 4,
        out_specs=VMEM,
        compiler_params=params(60),
        name="sum",
    )(moves, summed, resid, theirs, got)
    landed = exchange(routed)
    x_half, spare = pl.pallas_call(
        functools.partial(unpack_kernel, n_sub),
        out_shape=(
            jax.ShapeDtypeStruct((requests, wide_half), bf16),
            jax.ShapeDtypeStruct((half, width), bf16),
        ),
        in_specs=[VMEM],
        out_specs=(VMEM, VMEM),
        compiler_params=params(60),
        name="unpack",
    )(landed)
    chunks = 3
    hidden, base = pl.pallas_call(
        functools.partial(gate_up_kernel, n_sub),
        out_shape=(
            jax.ShapeDtypeStruct((n_dp, requests, units), bf16),
            jax.ShapeDtypeStruct((requests, cols), bf16),
        ),
        in_specs=[VMEM] * 3 + [HBM] * 2,
        out_specs=(VMEM, VMEM),
        scratch_shapes=[
            pltpu.VMEM((requests, dim), f32),
            pltpu.VMEM((2 * chunks, units // chunks, dim), bf16),
            pltpu.SemaphoreType.DMA((2 * chunks,)),
        ],
        compiler_params=params(60),
        name="gate_up",
    )(x_half, swap(x_half, n_sub), norm_gain[None], w_gate.T, w_up.T)
    every = exchange(hidden)
    chunks = 4
    mixed = pl.pallas_call(
        functools.partial(down_kernel, n_sub),
        out_shape=jax.ShapeDtypeStruct((requests, cols), bf16),
        in_specs=[VMEM] * 3 + [HBM],
        out_specs=VMEM,
        scratch_shapes=[
            pltpu.VMEM((requests, n_dp * n_sub * units), bf16),
            pltpu.VMEM((chunks, cols // chunks, w_down.shape[0]), bf16),
            pltpu.SemaphoreType.DMA((chunks,)),
        ],
        compiler_params=params(60),
        name="down",
    )(every, swap(every, n_sub), base, w_down.T)
    return (kept.T[None], spare[None], mixed)


def per_device(*args):
    queries, cache, w_uv, w_out = args[0], args[2], args[6], args[7]
    w_gate, w_down = args[9], args[11]
    n_dp = lax.axis_size("dp")
    n_sub = lax.axis_size("sub")
    fits = (
        n_sub == 2
        and n_dp == 8
        and cache.shape[1] % (2 * 8 * n_dp) == 0
        and queries.shape[1] // n_dp == 16
        and w_uv.shape[1] == 512
        and w_out.shape[1] % (n_sub * 4 * 128) == 0
        and w_gate.shape[1] % 96 == 0
        and w_down.shape[1] % 64 == 0
    )
    return per_device_fast(*args) if fits else per_device_any(*args)


def solution(mesh):
    return jax.shard_map(
        per_device,
        mesh=mesh,
        in_specs=(
            P(("groups", "dp", "sub"), None, None),
            P(("groups", "dp", "sub"), None),
            P(("groups", "dp", "sub"), None, None),
            P("groups"),
            P("groups", None),
            P(("groups", "dp", "sub"), None),
            P("dp", None, None),
            P("dp", None),
            P(),
            P(None, ("dp", "sub")),
            P(None, ("dp", "sub")),
            P(None, ("dp", "sub")),
        ),
        out_specs=(
            P(("groups", "dp", "sub"), None, None),
            P(("groups", "dp", "sub"), None, None),
            P("groups", ("dp", "sub")),
        ),
        check_vma=False,
    )
```

```python
import functools

import jax
import jax.numpy as jnp
from jax import lax
from jax.experimental import pallas as pl
from jax.experimental.pallas import tpu as pltpu
from jax.sharding import PartitionSpec as P


def partial_attend(query, keys, live, scale, latent):
    scores = jnp.einsum("hw,pw->hp", query, keys, preferred_element_type=jnp.float32) * scale
    scores = jnp.where(live[None, :], scores, -1e30)
    top = jnp.max(scores, axis=1)
    weights = jnp.where(live[None, :], jnp.exp(scores - top[:, None]), 0.0)
    total = jnp.sum(weights, axis=1)
    acc = jnp.dot(
        weights.astype(jnp.bfloat16), keys[:, :latent], preferred_element_type=jnp.float32
    )
    return (top, total, acc)


def route(spread, partner, present):
    shape = (spread.shape[0],) + (1,) * (spread.ndim - 1)
    picked = jnp.take(spread, partner, axis=0)
    return jnp.where(present.reshape(shape), picked, jnp.zeros((), spread.dtype))


def per_device_any(
    queries, new_latent, cache, lengths, moves, resid, w_uv, w_out, norm_gain, w_gate, w_up, w_down
):
    n_dp = lax.axis_size("dp")
    n_sub = lax.axis_size("sub")
    rank = lax.axis_index("dp")
    core = lax.axis_index("sub")
    device = rank * n_sub + core
    cap = cache.shape[1]
    half = cap // 2
    width = cache.shape[2]
    heads = queries.shape[1]
    latent = w_uv.shape[1]
    scale = (w_uv.shape[2] + width - latent) ** (-0.5)
    length = lax.dynamic_index_in_dim(lengths, device, 0, keepdims=False)
    positions = jnp.arange(cap, dtype=jnp.int32)
    appended = jnp.where((positions == length)[:, None], new_latent[0][None, :], cache[0])
    moved_req = moves[:, 0]
    sources = moves[:, 1]
    targets = moves[:, 2]
    same_core = moved_req % n_sub == core
    sending = jnp.any(moved_req == device)
    peers = jnp.arange(n_dp, dtype=jnp.int32)
    to_match = same_core[None, :] & (peers[:, None] == targets[None, :])
    from_of = jnp.sum(jnp.where(to_match, sources[None, :], 0), axis=1)
    to_has = jnp.any(to_match, axis=1)
    zero_bf = jnp.zeros((), jnp.bfloat16)
    upper = jnp.where(sending, appended[half:], zero_bf).reshape(n_dp, -1)
    spread = lax.all_to_all(upper, "dp", split_axis=0, concat_axis=0, tiled=True)
    landed = lax.all_to_all(
        route(spread, from_of, to_has), "dp", split_axis=0, concat_axis=0, tiled=True
    )
    spare = landed.reshape(half, width)
    kept = jnp.where(sending & (positions >= half)[:, None], zero_bf, appended)
    top, total, acc = partial_attend(queries[0], appended, positions <= length, scale, latent)
    o_lat = (acc / total[:, None]).astype(jnp.bfloat16)
    owners = lax.all_to_all(
        o_lat.reshape(n_dp, heads // n_dp, latent), "dp", split_axis=0, concat_axis=0, tiled=True
    )
    values = jnp.einsum("rhl,hlv->rhv", owners, w_uv, preferred_element_type=jnp.float32).astype(
        jnp.bfloat16
    )
    values = values.reshape(n_dp, -1)
    cols = w_down.shape[1]
    units = w_gate.shape[1]
    col_start = device * cols
    gain = norm_gain.astype(jnp.float32)
    summed = lax.psum_scatter(
        jnp.dot(values, w_out, preferred_element_type=jnp.float32),
        "dp",
        scatter_dimension=0,
        tiled=True,
    )
    x_rows = (resid.astype(jnp.float32) + summed).astype(jnp.bfloat16)
    piece = lax.all_gather(x_rows, ("dp", "sub"), axis=0, tiled=True)
    xf = piece.astype(jnp.float32)
    normed = (xf * lax.rsqrt(jnp.mean(xf * xf, axis=1, keepdims=True) + 1e-06) * gain).astype(
        jnp.bfloat16
    )
    gate = jnp.dot(normed, w_gate, preferred_element_type=jnp.float32)
    up_part = jnp.dot(normed, w_up, preferred_element_type=jnp.float32)
    hidden_part = (jax.nn.silu(gate) * up_part).astype(jnp.bfloat16)
    own_cols = lax.dynamic_slice_in_dim(piece, col_start, cols, 1)
    joined = jnp.concatenate([hidden_part, own_cols], axis=1)
    hidden = joined[:, :units]
    base = joined[:, units:]
    down = jnp.dot(
        lax.all_gather(hidden, ("dp", "sub"), axis=1, tiled=True),
        w_down,
        preferred_element_type=jnp.float32,
    )
    mixed = (base.astype(jnp.float32) + down).astype(jnp.bfloat16)
    return (kept[None], spare[None], mixed)


VMEM = pl.BlockSpec(memory_space=pltpu.VMEM)
SMEM = pl.BlockSpec(memory_space=pltpu.SMEM)
HBM = pl.BlockSpec(memory_space=pl.ANY)
NT = (((1,), (1,)), ((), ()))
TN = (((0,), (0,)), ((), ()))


def cost(mib):
    return pl.CostEstimate(flops=300 * (mib << 20), bytes_accessed=mib << 20, transcendentals=0)


def params(mib):
    return pltpu.CompilerParams(vmem_limit_bytes=mib << 20)


def place(n_sub):
    rank = lax.axis_index("dp")
    core = lax.axis_index("sub")
    return rank, core, rank * n_sub + core


def position_kernel(out_ref):
    out_ref[...] = lax.broadcasted_iota(jnp.int32, out_ref.shape, 1)


def attend_kernel(
    scale, n_dp, n_sub, latent, lengths, moves, at_ref, q_ref, fresh_ref, cache_ref, kept_ref, out_ref
):
    width, cap = cache_ref.shape
    half = cap // 2
    heads = q_ref.shape[1]
    _, _, device = place(n_sub)
    length = lengths[device]
    sending = moves[0, 0] == device
    for row in range(1, moves.shape[0]):
        sending = sending | (moves[row, 0] == device)
    fresh = jnp.broadcast_to(fresh_ref[...].astype(jnp.float32), (128, width)).T
    fresh = jnp.concatenate([fresh] * (cap // 128), axis=1)
    positions = at_ref[...]
    positions = jnp.concatenate([positions] * (width // positions.shape[0]), axis=0)
    appended = jnp.where(positions == length, fresh, cache_ref[...].astype(jnp.float32))
    drop = jnp.where(sending, half, cap)
    kept_ref[...] = jnp.where(positions >= drop, 0.0, appended).astype(jnp.bfloat16)
    keys = appended.astype(jnp.bfloat16)
    scores = lax.dot_general(q_ref[...], keys, TN, preferred_element_type=jnp.float32) * scale
    live = positions[:heads] <= length
    scores = jnp.where(live, scores, -1e30)
    top = jnp.max(scores, axis=1, keepdims=True)
    weights = jnp.where(live, jnp.exp(scores - top), 0.0)
    total = jnp.sum(weights, axis=1, keepdims=True)
    acc = lax.dot_general(
        weights.astype(jnp.bfloat16), keys[:latent], NT, preferred_element_type=jnp.float32
    )
    o_lat = (acc / total).astype(jnp.bfloat16)
    share = heads // n_dp
    rows = half // n_dp
    upper = jnp.where(sending, appended.T[half:], 0.0)
    for peer in range(n_dp):
        out_ref[peer, 0:share, 0:latent] = o_lat[peer * share : (peer + 1) * share]
        out_ref[peer, 0:share, latent:width] = jnp.zeros((share, width - latent), jnp.bfloat16)
        out_ref[peer, share : share + rows, :] = upper[peer * rows : (peer + 1) * rows].astype(
            jnp.bfloat16
        )


def values_kernel(got_ref, uv_ref, resid_ref, out_ref, wide):
    n_dp = got_ref.shape[0]
    share, latent, vh = uv_ref.shape
    for src in range(n_dp):
        for k in range(latent // 128):
            wide[k, src * share : (src + 1) * share, :] = got_ref[
                src, 0:share, 128 * k : 128 * (k + 1)
            ].astype(jnp.float32)
    piece = resid_ref.shape[1] // n_dp
    for src in range(n_dp):
        out_ref[src : src + 1, share * vh :] = resid_ref[:, src * piece : (src + 1) * piece]
    for head in range(share):
        rows = jnp.concatenate(
            [wide[k, pl.ds(head, n_dp, stride=share), :] for k in range(latent // 128)], axis=1
        ).astype(jnp.bfloat16)
        out_ref[:, head * vh : (head + 1) * vh] = jnp.dot(
            rows, uv_ref[head], preferred_element_type=jnp.float32
        ).astype(jnp.bfloat16)


def interleave(first, second):
    n = first.shape[0]
    row = lax.broadcasted_iota(jnp.int32, (2 * n, 2 * n), 0)
    col = lax.broadcasted_iota(jnp.int32, (2 * n, 2 * n), 1)
    pick = (col == (row % 2) * n + row // 2).astype(jnp.bfloat16)
    both = jnp.concatenate([first, second], axis=0)
    return jnp.dot(pick, both, preferred_element_type=jnp.float32).astype(jnp.bfloat16)


def project_kernel(n_sub, own_ref, peer_ref, w_ref, out_ref, weights, sems):
    n_dp, per, half = out_ref.shape
    depth = w_ref.shape[0]
    chunks = sems.shape[0]
    wide = half // chunks
    _, core, _ = place(n_sub)

    def fetch(i):
        start = pl.multiple_of(core * half + i * wide, 128)
        return pltpu.make_async_copy(
            w_ref.at[:, pl.ds(start, wide)], weights.at[i], sems.at[i]
        )

    for i in range(chunks):
        fetch(i).start()
    own = own_ref[:, :depth].astype(jnp.float32)
    peer = peer_ref[:, :depth].astype(jnp.float32)
    first = jnp.where(core == 0, own, peer).astype(jnp.bfloat16)
    second = jnp.where(core == 0, peer, own).astype(jnp.bfloat16)
    values = interleave(first, second)
    for i in range(chunks):
        fetch(i).wait()
        part = jnp.dot(values, weights[i], preferred_element_type=jnp.float32)
        for dst in range(n_dp):
            out_ref[dst, :, i * wide : (i + 1) * wide] = part[dst * per : (dst + 1) * per]


def sum_kernel(n_sub, moves, part_ref, own_ref, peer_ref, got_ref, out_ref):
    n_dp, per, half = part_ref.shape
    rows_at = 16
    rows = out_ref.shape[1] - rows_at
    _, core, _ = place(n_sub)
    piece = n_sub * half // n_dp
    at = own_ref.shape[1] - piece

    def row_of(ref):
        every = ref[:, at:].astype(jnp.float32)
        near = jnp.where(core == 0, every[: n_dp // 2], every[n_dp // 2 :])
        return jnp.concatenate([near[i : i + 1] for i in range(n_dp // 2)], axis=1)

    mine = row_of(own_ref)
    theirs = row_of(peer_ref)
    row = lax.broadcasted_iota(jnp.int32, (per, half), 0)
    total = jnp.where(row == core, mine, theirs)
    for src in range(n_dp):
        total = total + part_ref[src]
    x = total.astype(jnp.bfloat16)
    for dst in range(n_dp):
        for k in range(half // 512):
            out_ref[dst, per * k : per * (k + 1), 0:512] = x[:, 512 * k : 512 * (k + 1)]
        source = jnp.int32(0)
        found = jnp.int32(0)
        for row in range(moves.shape[0]):
            hit = (moves[row, 2] == dst) & (moves[row, 0] % n_sub == core)
            source = jnp.where(hit, moves[row, 1], source)
            found = jnp.where(hit, 1, found)

        @pl.when(found == 1)
        def _():
            out_ref[dst, rows_at : rows_at + rows, :] = got_ref[source, rows_at : rows_at + rows, :]

        @pl.when(found == 0)
        def _():
            out_ref[dst, rows_at : rows_at + rows, :] = jnp.zeros(
                (rows, out_ref.shape[2]), jnp.bfloat16
            )


def unpack_kernel(n_sub, got_ref, x_ref, spare_ref):
    n_dp = got_ref.shape[0]
    rows = spare_ref.shape[0] // n_dp
    half = x_ref.shape[1]
    for k in range(half // 512):
        x_ref[:, 512 * k : 512 * (k + 1)] = jnp.concatenate(
            [
                got_ref[src, n_sub * k : n_sub * (k + 1), 0:512].astype(jnp.float32)
                for src in range(n_dp)
            ],
            axis=0,
        ).astype(jnp.bfloat16)
    for src in range(n_dp):
        spare_ref[src * rows : (src + 1) * rows, :] = got_ref[src, 16 : 16 + rows, :]


def gate_up_kernel(
    n_sub, own_ref, peer_ref, gain_ref, gate_ref, up_ref, out_ref, base_ref, whole
):
    half = own_ref.shape[1]
    cols = base_ref.shape[1]
    rank, core, _ = place(n_sub)

    own = own_ref[...].astype(jnp.float32)
    peer = peer_ref[...].astype(jnp.float32)
    whole[:, :half] = jnp.where(core == 0, own, peer)
    whole[:, half:] = jnp.where(core == 0, peer, own)
    xf = whole[...]
    inverse = lax.rsqrt(jnp.mean(xf * xf, axis=1, keepdims=True) + 1e-06)
    normed = (xf * inverse * gain_ref[...].astype(jnp.float32).reshape(1, -1)).astype(jnp.bfloat16)
    start = pl.multiple_of(rank * n_sub * cols + core * (cols // 128 * 128), 128)
    near = whole[:, pl.ds(start, cols + 64)]
    base_ref[...] = jnp.where(core == 0, near[:, :cols], near[:, 64:]).astype(jnp.bfloat16)
    gate = lax.dot_general(gate_ref[...], normed, NT, preferred_element_type=jnp.float32)
    up = lax.dot_general(up_ref[...], normed, NT, preferred_element_type=jnp.float32)
    hidden = (gate * jax.nn.sigmoid(gate) * up).T.astype(jnp.bfloat16)
    for dst in range(out_ref.shape[0]):
        out_ref[dst] = hidden


def down_kernel(n_sub, own_ref, peer_ref, base_ref, down_ref, out_ref, hidden):
    units = own_ref.shape[2]
    _, core, _ = place(n_sub)

    for src in range(own_ref.shape[0]):
        own = own_ref[src].astype(jnp.float32)
        peer = peer_ref[src].astype(jnp.float32)
        first = jnp.where(core == 0, own, peer)
        second = jnp.where(core == 0, peer, own)
        hidden[:, src * n_sub * units : (src + 1) * n_sub * units] = jnp.concatenate(
            [first, second], axis=1
        ).astype(jnp.bfloat16)
    down = lax.dot_general(
        down_ref[...], hidden[...], NT, preferred_element_type=jnp.float32
    ).T
    out_ref[...] = (base_ref[...].astype(jnp.float32) + down).astype(jnp.bfloat16)


def swap(x, n_sub):
    return lax.ppermute(x, "sub", [(i, (i + 1) % n_sub) for i in range(n_sub)])


def exchange(x):
    return lax.all_to_all(x, "dp", split_axis=0, concat_axis=0, tiled=True)


def per_device_fast(
    queries, new_latent, cache, lengths, moves, resid, w_uv, w_out, norm_gain, w_gate, w_up, w_down
):
    n_dp = lax.axis_size("dp")
    n_sub = lax.axis_size("sub")
    cap, width = cache.shape[1:]
    heads = queries.shape[1]
    share, latent, vh = w_uv.shape
    half = cap // 2
    rows = half // n_dp
    dim = w_out.shape[1]
    requests = n_dp * n_sub
    units = w_gate.shape[1]
    cols = w_down.shape[1]
    scale = (vh + width - latent) ** (-0.5)
    bf16, f32 = jnp.bfloat16, jnp.float32

    positions = pl.pallas_call(
        position_kernel,
        out_shape=jax.ShapeDtypeStruct((8, cap), jnp.int32),
        out_specs=VMEM,
        compiler_params=params(8),
        cost_estimate=cost(40),
        name="positions",
    )()
    kept, sent = pl.pallas_call(
        functools.partial(attend_kernel, scale, n_dp, n_sub, latent),
        out_shape=(
            jax.ShapeDtypeStruct((width, cap), bf16),
            jax.ShapeDtypeStruct((n_dp, share + rows, width), bf16),
        ),
        in_specs=[SMEM] * 2 + [VMEM] * 4,
        out_specs=(VMEM, VMEM),
        compiler_params=params(8),
        cost_estimate=cost(24),
        name="attend",
    )(lengths, moves, positions, queries[0].T, new_latent, cache[0].T)
    got = exchange(sent)
    wide_half = dim // n_sub
    values = pl.pallas_call(
        values_kernel,
        out_shape=jax.ShapeDtypeStruct((n_dp, share * vh + dim // n_dp), bf16),
        in_specs=[VMEM] * 3,
        out_specs=VMEM,
        scratch_shapes=[pltpu.VMEM((latent // 128, n_dp * share, 128), f32)],
        compiler_params=params(8),
        cost_estimate=cost(1),
        name="values",
    )(got, w_uv, resid)
    peer_values = swap(values, n_sub)
    partial = pl.pallas_call(
        functools.partial(project_kernel, n_sub),
        out_shape=jax.ShapeDtypeStruct((n_dp, n_sub, wide_half), f32),
        in_specs=[VMEM, VMEM, HBM],
        out_specs=VMEM,
        scratch_shapes=[
            pltpu.VMEM((4, share * vh, wide_half // 4), bf16),
            pltpu.SemaphoreType.DMA((4,)),
        ],
        compiler_params=params(38),
        cost_estimate=cost(24),
        name="project",
    )(values, peer_values, w_out)
    summed = exchange(partial)
    routed = pl.pallas_call(
        functools.partial(sum_kernel, n_sub),
        out_shape=jax.ShapeDtypeStruct((n_dp, 16 + rows, width), bf16),
        in_specs=[SMEM] + [VMEM] * 4,
        out_specs=VMEM,
        compiler_params=params(8),
        cost_estimate=cost(64),
        name="sum",
    )(moves, summed, values, peer_values, got)
    landed = exchange(routed)
    x_half, spare = pl.pallas_call(
        functools.partial(unpack_kernel, n_sub),
        out_shape=(
            jax.ShapeDtypeStruct((requests, wide_half), bf16),
            jax.ShapeDtypeStruct((half, width), bf16),
        ),
        in_specs=[VMEM],
        out_specs=(VMEM, VMEM),
        compiler_params=params(8),
        cost_estimate=cost(1),
        name="unpack",
    )(landed)
    hidden, base = pl.pallas_call(
        functools.partial(gate_up_kernel, n_sub),
        out_shape=(
            jax.ShapeDtypeStruct((n_dp, requests, units), bf16),
            jax.ShapeDtypeStruct((requests, cols), bf16),
        ),
        in_specs=[VMEM] * 5,
        out_specs=(VMEM, VMEM),
        scratch_shapes=[
            pltpu.VMEM((requests, dim), f32),
        ],
        compiler_params=params(24),
        cost_estimate=cost(1),
        name="gate_up",
    )(x_half, swap(x_half, n_sub), norm_gain, w_gate.T, w_up.T)
    every = exchange(hidden)
    mixed = pl.pallas_call(
        functools.partial(down_kernel, n_sub),
        out_shape=jax.ShapeDtypeStruct((requests, cols), bf16),
        in_specs=[VMEM] * 4,
        out_specs=VMEM,
        scratch_shapes=[
            pltpu.VMEM((requests, n_dp * n_sub * units), bf16),
        ],
        compiler_params=params(16),
        cost_estimate=cost(1),
        name="down",
    )(every, swap(every, n_sub), base, w_down.T)
    return (kept.T[None], spare[None], mixed)


def per_device(*args):
    queries, cache, w_uv, w_out = args[0], args[2], args[6], args[7]
    w_gate, w_down = args[9], args[11]
    n_dp = lax.axis_size("dp")
    n_sub = lax.axis_size("sub")
    fits = (
        n_sub == 2
        and n_dp == 8
        and cache.shape[1] % (2 * 8 * n_dp) == 0
        and queries.shape[1] // n_dp == 16
        and w_uv.shape[1] == 512
        and w_out.shape[1] % (n_sub * 4 * 128) == 0
        and w_gate.shape[1] % 96 == 0
        and w_down.shape[1] % 64 == 0
    )
    return per_device_fast(*args) if fits else per_device_any(*args)


def solution(mesh):
    return jax.shard_map(
        per_device,
        mesh=mesh,
        in_specs=(
            P(("groups", "dp", "sub"), None, None),
            P(("groups", "dp", "sub"), None),
            P(("groups", "dp", "sub"), None, None),
            P("groups"),
            P("groups", None),
            P(("groups", "dp", "sub"), None),
            P("dp", None, None),
            P("dp", None),
            P(),
            P(None, ("dp", "sub")),
            P(None, ("dp", "sub")),
            P(None, ("dp", "sub")),
        ),
        out_specs=(
            P(("groups", "dp", "sub"), None, None),
            P(("groups", "dp", "sub"), None, None),
            P("groups", ("dp", "sub")),
        ),
        check_vma=False,
    )
```

```python
import functools

import jax
import jax.numpy as jnp
from jax import lax
from jax.experimental import pallas as pl
from jax.experimental.pallas import tpu as pltpu
from jax.sharding import PartitionSpec as P


def partial_attend(query, keys, live, scale, latent):
    scores = jnp.einsum("hw,pw->hp", query, keys, preferred_element_type=jnp.float32) * scale
    scores = jnp.where(live[None, :], scores, -1e30)
    top = jnp.max(scores, axis=1)
    weights = jnp.where(live[None, :], jnp.exp(scores - top[:, None]), 0.0)
    total = jnp.sum(weights, axis=1)
    acc = jnp.dot(
        weights.astype(jnp.bfloat16), keys[:, :latent], preferred_element_type=jnp.float32
    )
    return (top, total, acc)


def route(spread, partner, present):
    shape = (spread.shape[0],) + (1,) * (spread.ndim - 1)
    picked = jnp.take(spread, partner, axis=0)
    return jnp.where(present.reshape(shape), picked, jnp.zeros((), spread.dtype))


def per_device_any(
    queries, new_latent, cache, lengths, moves, resid, w_uv, w_out, norm_gain, w_gate, w_up, w_down
):
    n_dp = lax.axis_size("dp")
    n_sub = lax.axis_size("sub")
    rank = lax.axis_index("dp")
    core = lax.axis_index("sub")
    device = rank * n_sub + core
    cap = cache.shape[1]
    half = cap // 2
    width = cache.shape[2]
    heads = queries.shape[1]
    latent = w_uv.shape[1]
    scale = (w_uv.shape[2] + width - latent) ** (-0.5)
    length = lax.dynamic_index_in_dim(lengths, device, 0, keepdims=False)
    positions = jnp.arange(cap, dtype=jnp.int32)
    appended = jnp.where((positions == length)[:, None], new_latent[0][None, :], cache[0])
    moved_req = moves[:, 0]
    sources = moves[:, 1]
    targets = moves[:, 2]
    same_core = moved_req % n_sub == core
    sending = jnp.any(moved_req == device)
    peers = jnp.arange(n_dp, dtype=jnp.int32)
    to_match = same_core[None, :] & (peers[:, None] == targets[None, :])
    from_of = jnp.sum(jnp.where(to_match, sources[None, :], 0), axis=1)
    to_has = jnp.any(to_match, axis=1)
    zero_bf = jnp.zeros((), jnp.bfloat16)
    upper = jnp.where(sending, appended[half:], zero_bf).reshape(n_dp, -1)
    spread = lax.all_to_all(upper, "dp", split_axis=0, concat_axis=0, tiled=True)
    landed = lax.all_to_all(
        route(spread, from_of, to_has), "dp", split_axis=0, concat_axis=0, tiled=True
    )
    spare = landed.reshape(half, width)
    kept = jnp.where(sending & (positions >= half)[:, None], zero_bf, appended)
    top, total, acc = partial_attend(queries[0], appended, positions <= length, scale, latent)
    o_lat = (acc / total[:, None]).astype(jnp.bfloat16)
    owners = lax.all_to_all(
        o_lat.reshape(n_dp, heads // n_dp, latent), "dp", split_axis=0, concat_axis=0, tiled=True
    )
    values = jnp.einsum("rhl,hlv->rhv", owners, w_uv, preferred_element_type=jnp.float32).astype(
        jnp.bfloat16
    )
    values = values.reshape(n_dp, -1)
    cols = w_down.shape[1]
    units = w_gate.shape[1]
    col_start = device * cols
    gain = norm_gain.astype(jnp.float32)
    summed = lax.psum_scatter(
        jnp.dot(values, w_out, preferred_element_type=jnp.float32),
        "dp",
        scatter_dimension=0,
        tiled=True,
    )
    x_rows = (resid.astype(jnp.float32) + summed).astype(jnp.bfloat16)
    piece = lax.all_gather(x_rows, ("dp", "sub"), axis=0, tiled=True)
    xf = piece.astype(jnp.float32)
    normed = (xf * lax.rsqrt(jnp.mean(xf * xf, axis=1, keepdims=True) + 1e-06) * gain).astype(
        jnp.bfloat16
    )
    gate = jnp.dot(normed, w_gate, preferred_element_type=jnp.float32)
    up_part = jnp.dot(normed, w_up, preferred_element_type=jnp.float32)
    hidden_part = (jax.nn.silu(gate) * up_part).astype(jnp.bfloat16)
    own_cols = lax.dynamic_slice_in_dim(piece, col_start, cols, 1)
    joined = jnp.concatenate([hidden_part, own_cols], axis=1)
    hidden = joined[:, :units]
    base = joined[:, units:]
    down = jnp.dot(
        lax.all_gather(hidden, ("dp", "sub"), axis=1, tiled=True),
        w_down,
        preferred_element_type=jnp.float32,
    )
    mixed = (base.astype(jnp.float32) + down).astype(jnp.bfloat16)
    return (kept[None], spare[None], mixed)


VMEM = pl.BlockSpec(memory_space=pltpu.VMEM)
SMEM = pl.BlockSpec(memory_space=pltpu.SMEM)
HBM = pl.BlockSpec(memory_space=pl.ANY)
NT = (((1,), (1,)), ((), ()))
TN = (((0,), (0,)), ((), ()))


def cost(mib):
    return pl.CostEstimate(flops=300 * (mib << 20), bytes_accessed=mib << 20, transcendentals=0)


def params(mib):
    return pltpu.CompilerParams(vmem_limit_bytes=mib << 20)


def place(n_sub):
    rank = lax.axis_index("dp")
    core = lax.axis_index("sub")
    return rank, core, rank * n_sub + core


def position_kernel(out_ref):
    out_ref[...] = lax.broadcasted_iota(jnp.int32, out_ref.shape, 1)


def attend_kernel(
    scale, n_dp, n_sub, latent, lengths, moves, at_ref, q_ref, fresh_ref, cache_ref, kept_ref, out_ref
):
    width, cap = cache_ref.shape
    half = cap // 2
    heads = q_ref.shape[1]
    _, _, device = place(n_sub)
    length = lengths[device]
    sending = moves[0, 0] == device
    for row in range(1, moves.shape[0]):
        sending = sending | (moves[row, 0] == device)
    fresh = jnp.broadcast_to(fresh_ref[...].astype(jnp.float32), (128, width)).T
    fresh = jnp.concatenate([fresh] * (cap // 128), axis=1)
    positions = at_ref[...]
    positions = jnp.concatenate([positions] * (width // positions.shape[0]), axis=0)
    appended = jnp.where(positions == length, fresh, cache_ref[...].astype(jnp.float32))
    drop = jnp.where(sending, half, cap)
    kept_ref[...] = jnp.where(positions >= drop, 0.0, appended).astype(jnp.bfloat16)
    keys = appended.astype(jnp.bfloat16)
    scores = lax.dot_general(q_ref[...], keys, TN, preferred_element_type=jnp.float32) * scale
    live = positions[:heads] <= length
    scores = jnp.where(live, scores, -1e30)
    top = jnp.max(scores, axis=1, keepdims=True)
    weights = jnp.where(live, jnp.exp(scores - top), 0.0)
    total = jnp.sum(weights, axis=1, keepdims=True)
    acc = lax.dot_general(
        weights.astype(jnp.bfloat16), keys[:latent], NT, preferred_element_type=jnp.float32
    )
    o_lat = (acc / total).astype(jnp.bfloat16)
    share = heads // n_dp
    rows = half // n_dp
    upper = jnp.where(sending, appended.T[half:], 0.0)
    for peer in range(n_dp):
        out_ref[peer, 0:share, 0:latent] = o_lat[peer * share : (peer + 1) * share]
        out_ref[peer, 0:share, latent:width] = jnp.zeros((share, width - latent), jnp.bfloat16)
        out_ref[peer, share : share + rows, :] = upper[peer * rows : (peer + 1) * rows].astype(
            jnp.bfloat16
        )


def values_kernel(got_ref, uv_ref, resid_ref, out_ref, wide):
    n_dp = got_ref.shape[0]
    share, latent, vh = uv_ref.shape
    for src in range(n_dp):
        for k in range(latent // 128):
            wide[k, src * share : (src + 1) * share, :] = got_ref[
                src, 0:share, 128 * k : 128 * (k + 1)
            ].astype(jnp.float32)
    piece = resid_ref.shape[1] // n_dp
    for src in range(n_dp):
        out_ref[src : src + 1, share * vh :] = resid_ref[:, src * piece : (src + 1) * piece]
    for head in range(share):
        rows = jnp.concatenate(
            [wide[k, pl.ds(head, n_dp, stride=share), :] for k in range(latent // 128)], axis=1
        ).astype(jnp.bfloat16)
        out_ref[:, head * vh : (head + 1) * vh] = jnp.dot(
            rows, uv_ref[head], preferred_element_type=jnp.float32
        ).astype(jnp.bfloat16)


def interleave(first, second):
    n = first.shape[0]
    row = lax.broadcasted_iota(jnp.int32, (2 * n, 2 * n), 0)
    col = lax.broadcasted_iota(jnp.int32, (2 * n, 2 * n), 1)
    pick = (col == (row % 2) * n + row // 2).astype(jnp.bfloat16)
    both = jnp.concatenate([first, second], axis=0)
    return jnp.dot(pick, both, preferred_element_type=jnp.float32).astype(jnp.bfloat16)


def project_kernel(n_sub, own_ref, peer_ref, w_ref, out_ref, weights, sems):
    requests, half = out_ref.shape
    n_dp = requests // n_sub
    depth = w_ref.shape[0]
    chunks = sems.shape[0]
    wide = half // chunks
    rank, core, _ = place(n_sub)

    def fetch(i):
        start = pl.multiple_of(core * half + i * wide, 128)
        return pltpu.make_async_copy(
            w_ref.at[:, pl.ds(start, wide)], weights.at[i], sems.at[i]
        )

    for i in range(chunks):
        fetch(i).start()
    own = own_ref[:, :depth].astype(jnp.float32)
    peer = peer_ref[:, :depth].astype(jnp.float32)
    first = jnp.where(core == 0, own, peer).astype(jnp.bfloat16)
    second = jnp.where(core == 0, peer, own).astype(jnp.bfloat16)
    values = interleave(first, second)

    def resid_of(ref):
        every = ref[:, depth:].astype(jnp.float32)
        near = jnp.where(core == 0, every[: n_dp // 2], every[n_dp // 2 :])
        return jnp.concatenate([near[i : i + 1] for i in range(n_dp // 2)], axis=1)

    mine = resid_of(own_ref)
    theirs = resid_of(peer_ref)
    row = lax.broadcasted_iota(jnp.int32, (requests, wide), 0)
    for i in range(chunks):
        fetch(i).wait()
        span = slice(i * wide, (i + 1) * wide)
        part = jnp.dot(values, weights[i], preferred_element_type=jnp.float32)
        near = jnp.where(row % n_sub == core, mine[:, span], theirs[:, span])
        part = part + jnp.where(row // n_sub == rank, near, 0.0)
        out_ref[:, span] = part.astype(jnp.bfloat16)


def add_kernel(a_ref, b_ref, out_ref):
    out_ref[...] = (a_ref[...].astype(jnp.float32) + b_ref[...].astype(jnp.float32)).astype(
        jnp.bfloat16
    )


def unpack_kernel(got_ref, hidden_ref, spare_ref):
    n_dp, share, _ = hidden_ref.shape
    rows = spare_ref.shape[0] // n_dp
    for src in range(n_dp):
        hidden_ref[src] = got_ref[src, 0:share, :]
        spare_ref[src * rows : (src + 1) * rows, :] = got_ref[src, share : share + rows, :]


def gate_up_kernel(
    n_sub, moves, own_ref, peer_ref, gain_ref, got_ref, gate_ref, up_ref, out_ref, base_ref, whole
):
    half = own_ref.shape[1]
    cols = base_ref.shape[1]
    rank, core, _ = place(n_sub)

    own = own_ref[...].astype(jnp.float32)
    peer = peer_ref[...].astype(jnp.float32)
    whole[:, :half] = jnp.where(core == 0, own, peer)
    whole[:, half:] = jnp.where(core == 0, peer, own)
    xf = whole[...]
    inverse = lax.rsqrt(jnp.mean(xf * xf, axis=1, keepdims=True) + 1e-06)
    normed = (xf * inverse * gain_ref[...].astype(jnp.float32).reshape(1, -1)).astype(jnp.bfloat16)
    start = pl.multiple_of(rank * n_sub * cols + core * (cols // 128 * 128), 128)
    near = whole[:, pl.ds(start, cols + 64)]
    base_ref[...] = jnp.where(core == 0, near[:, :cols], near[:, 64:]).astype(jnp.bfloat16)
    gate = lax.dot_general(gate_ref[...], normed, NT, preferred_element_type=jnp.float32)
    up = lax.dot_general(up_ref[...], normed, NT, preferred_element_type=jnp.float32)
    hidden = (gate * jax.nn.sigmoid(gate) * up).T.astype(jnp.bfloat16)
    requests = hidden.shape[0]
    rows = out_ref.shape[1] - requests
    from_row = got_ref.shape[1] - rows
    for dst in range(out_ref.shape[0]):
        out_ref[dst, 0:requests, :] = hidden
        source = jnp.int32(0)
        found = jnp.int32(0)
        for row in range(moves.shape[0]):
            hit = (moves[row, 2] == dst) & (moves[row, 0] % n_sub == core)
            source = jnp.where(hit, moves[row, 1], source)
            found = jnp.where(hit, 1, found)

        @pl.when(found == 1)
        def _():
            out_ref[dst, requests:, :] = got_ref[source, from_row:, :]

        @pl.when(found == 0)
        def _():
            out_ref[dst, requests:, :] = jnp.zeros((rows, out_ref.shape[2]), jnp.bfloat16)


def down_kernel(n_sub, own_ref, peer_ref, base_ref, down_ref, out_ref, hidden):
    units = own_ref.shape[2]
    _, core, _ = place(n_sub)

    for src in range(own_ref.shape[0]):
        own = own_ref[src].astype(jnp.float32)
        peer = peer_ref[src].astype(jnp.float32)
        first = jnp.where(core == 0, own, peer)
        second = jnp.where(core == 0, peer, own)
        hidden[:, src * n_sub * units : (src + 1) * n_sub * units] = jnp.concatenate(
            [first, second], axis=1
        ).astype(jnp.bfloat16)
    down = lax.dot_general(
        down_ref[...], hidden[...], NT, preferred_element_type=jnp.float32
    ).T
    out_ref[...] = (base_ref[...].astype(jnp.float32) + down).astype(jnp.bfloat16)


def swap(x, n_sub):
    return lax.ppermute(x, "sub", [(i, (i + 1) % n_sub) for i in range(n_sub)])


def exchange(x):
    return lax.all_to_all(x, "dp", split_axis=0, concat_axis=0, tiled=True)


def per_device_fast(
    queries, new_latent, cache, lengths, moves, resid, w_uv, w_out, norm_gain, w_gate, w_up, w_down
):
    n_dp = lax.axis_size("dp")
    n_sub = lax.axis_size("sub")
    cap, width = cache.shape[1:]
    heads = queries.shape[1]
    share, latent, vh = w_uv.shape
    half = cap // 2
    rows = half // n_dp
    dim = w_out.shape[1]
    requests = n_dp * n_sub
    units = w_gate.shape[1]
    cols = w_down.shape[1]
    scale = (vh + width - latent) ** (-0.5)
    bf16, f32 = jnp.bfloat16, jnp.float32

    positions = pl.pallas_call(
        position_kernel,
        out_shape=jax.ShapeDtypeStruct((8, cap), jnp.int32),
        out_specs=VMEM,
        compiler_params=params(8),
        cost_estimate=cost(40),
        name="positions",
    )()
    kept, sent = pl.pallas_call(
        functools.partial(attend_kernel, scale, n_dp, n_sub, latent),
        out_shape=(
            jax.ShapeDtypeStruct((width, cap), bf16),
            jax.ShapeDtypeStruct((n_dp, share + rows, width), bf16),
        ),
        in_specs=[SMEM] * 2 + [VMEM] * 4,
        out_specs=(VMEM, VMEM),
        compiler_params=params(8),
        cost_estimate=cost(24),
        name="attend",
    )(lengths, moves, positions, queries[0].T, new_latent, cache[0].T)
    got = exchange(sent)
    wide_half = dim // n_sub
    values = pl.pallas_call(
        values_kernel,
        out_shape=jax.ShapeDtypeStruct((n_dp, share * vh + dim // n_dp), bf16),
        in_specs=[VMEM] * 3,
        out_specs=VMEM,
        scratch_shapes=[pltpu.VMEM((latent // 128, n_dp * share, 128), f32)],
        compiler_params=params(8),
        cost_estimate=cost(1),
        name="values",
    )(got, w_uv, resid)
    peer_values = swap(values, n_sub)
    x_half = pl.pallas_call(
        functools.partial(project_kernel, n_sub),
        out_shape=jax.ShapeDtypeStruct((requests, wide_half), bf16),
        in_specs=[VMEM, VMEM, HBM],
        out_specs=VMEM,
        scratch_shapes=[
            pltpu.VMEM((4, share * vh, wide_half // 4), bf16),
            pltpu.SemaphoreType.DMA((4,)),
        ],
        compiler_params=params(38),
        cost_estimate=cost(24),
        name="project",
    )(values, peer_values, w_out)
    step = 1
    while step < n_dp:
        other = lax.ppermute(x_half, "dp", [(i, i ^ step) for i in range(n_dp)])
        x_half = pl.pallas_call(
            add_kernel,
            out_shape=jax.ShapeDtypeStruct((requests, wide_half), bf16),
            in_specs=[VMEM] * 2,
            out_specs=VMEM,
            compiler_params=params(8),
            cost_estimate=cost(24),
            name="add",
        )(x_half, other)
        step *= 2
    sent, base = pl.pallas_call(
        functools.partial(gate_up_kernel, n_sub),
        out_shape=(
            jax.ShapeDtypeStruct((n_dp, requests + rows, units), bf16),
            jax.ShapeDtypeStruct((requests, cols), bf16),
        ),
        in_specs=[SMEM] + [VMEM] * 6,
        out_specs=(VMEM, VMEM),
        scratch_shapes=[pltpu.VMEM((requests, dim), f32)],
        compiler_params=params(24),
        cost_estimate=cost(24),
        name="gate_up",
    )(moves, x_half, swap(x_half, n_sub), norm_gain, got, w_gate.T, w_up.T)
    every, spare = pl.pallas_call(
        unpack_kernel,
        out_shape=(
            jax.ShapeDtypeStruct((n_dp, requests, units), bf16),
            jax.ShapeDtypeStruct((half, width), bf16),
        ),
        in_specs=[VMEM],
        out_specs=(VMEM, VMEM),
        compiler_params=params(8),
        cost_estimate=cost(1),
        name="unpack",
    )(exchange(sent))
    mixed = pl.pallas_call(
        functools.partial(down_kernel, n_sub),
        out_shape=jax.ShapeDtypeStruct((requests, cols), bf16),
        in_specs=[VMEM] * 4,
        out_specs=VMEM,
        scratch_shapes=[pltpu.VMEM((requests, n_dp * n_sub * units), bf16)],
        compiler_params=params(16),
        cost_estimate=cost(1),
        name="down",
    )(every, swap(every, n_sub), base, w_down.T)
    return (kept.T[None], spare[None], mixed)


def per_device(*args):
    queries, cache, w_uv, w_out = args[0], args[2], args[6], args[7]
    w_gate, w_down = args[9], args[11]
    n_dp = lax.axis_size("dp")
    n_sub = lax.axis_size("sub")
    fits = (
        n_sub == 2
        and n_dp == 8
        and cache.shape[1] % (2 * 8 * n_dp) == 0
        and queries.shape[1] // n_dp == 16
        and w_uv.shape[1] == 512
        and w_out.shape[1] % (n_sub * 4 * 128) == 0
        and w_gate.shape[1] == cache.shape[2]
        and w_down.shape[1] % 64 == 0
    )
    return per_device_fast(*args) if fits else per_device_any(*args)


def solution(mesh):
    return jax.shard_map(
        per_device,
        mesh=mesh,
        in_specs=(
            P(("groups", "dp", "sub"), None, None),
            P(("groups", "dp", "sub"), None),
            P(("groups", "dp", "sub"), None, None),
            P("groups"),
            P("groups", None),
            P(("groups", "dp", "sub"), None),
            P("dp", None, None),
            P("dp", None),
            P(),
            P(None, ("dp", "sub")),
            P(None, ("dp", "sub")),
            P(None, ("dp", "sub")),
        ),
        out_specs=(
            P(("groups", "dp", "sub"), None, None),
            P(("groups", "dp", "sub"), None, None),
            P("groups", ("dp", "sub")),
        ),
        check_vma=False,
    )
```

```python
import functools

import jax
import jax.numpy as jnp
from jax import lax
from jax.experimental import pallas as pl
from jax.experimental.pallas import tpu as pltpu
from jax.sharding import PartitionSpec as P


def partial_attend(query, keys, live, scale, latent):
    scores = jnp.einsum("hw,pw->hp", query, keys, preferred_element_type=jnp.float32) * scale
    scores = jnp.where(live[None, :], scores, -1e30)
    top = jnp.max(scores, axis=1)
    weights = jnp.where(live[None, :], jnp.exp(scores - top[:, None]), 0.0)
    total = jnp.sum(weights, axis=1)
    acc = jnp.dot(
        weights.astype(jnp.bfloat16), keys[:, :latent], preferred_element_type=jnp.float32
    )
    return (top, total, acc)


def route(spread, partner, present):
    shape = (spread.shape[0],) + (1,) * (spread.ndim - 1)
    picked = jnp.take(spread, partner, axis=0)
    return jnp.where(present.reshape(shape), picked, jnp.zeros((), spread.dtype))


def per_device_any(
    queries, new_latent, cache, lengths, moves, resid, w_uv, w_out, norm_gain, w_gate, w_up, w_down
):
    n_dp = lax.axis_size("dp")
    n_sub = lax.axis_size("sub")
    rank = lax.axis_index("dp")
    core = lax.axis_index("sub")
    device = rank * n_sub + core
    cap = cache.shape[1]
    half = cap // 2
    width = cache.shape[2]
    heads = queries.shape[1]
    latent = w_uv.shape[1]
    scale = (w_uv.shape[2] + width - latent) ** (-0.5)
    length = lax.dynamic_index_in_dim(lengths, device, 0, keepdims=False)
    positions = jnp.arange(cap, dtype=jnp.int32)
    appended = jnp.where((positions == length)[:, None], new_latent[0][None, :], cache[0])
    moved_req = moves[:, 0]
    sources = moves[:, 1]
    targets = moves[:, 2]
    same_core = moved_req % n_sub == core
    sending = jnp.any(moved_req == device)
    peers = jnp.arange(n_dp, dtype=jnp.int32)
    to_match = same_core[None, :] & (peers[:, None] == targets[None, :])
    from_of = jnp.sum(jnp.where(to_match, sources[None, :], 0), axis=1)
    to_has = jnp.any(to_match, axis=1)
    zero_bf = jnp.zeros((), jnp.bfloat16)
    upper = jnp.where(sending, appended[half:], zero_bf).reshape(n_dp, -1)
    spread = lax.all_to_all(upper, "dp", split_axis=0, concat_axis=0, tiled=True)
    landed = lax.all_to_all(
        route(spread, from_of, to_has), "dp", split_axis=0, concat_axis=0, tiled=True
    )
    spare = landed.reshape(half, width)
    kept = jnp.where(sending & (positions >= half)[:, None], zero_bf, appended)
    top, total, acc = partial_attend(queries[0], appended, positions <= length, scale, latent)
    o_lat = (acc / total[:, None]).astype(jnp.bfloat16)
    owners = lax.all_to_all(
        o_lat.reshape(n_dp, heads // n_dp, latent), "dp", split_axis=0, concat_axis=0, tiled=True
    )
    values = jnp.einsum("rhl,hlv->rhv", owners, w_uv, preferred_element_type=jnp.float32).astype(
        jnp.bfloat16
    )
    values = values.reshape(n_dp, -1)
    cols = w_down.shape[1]
    units = w_gate.shape[1]
    col_start = device * cols
    gain = norm_gain.astype(jnp.float32)
    summed = lax.psum_scatter(
        jnp.dot(values, w_out, preferred_element_type=jnp.float32),
        "dp",
        scatter_dimension=0,
        tiled=True,
    )
    x_rows = (resid.astype(jnp.float32) + summed).astype(jnp.bfloat16)
    piece = lax.all_gather(x_rows, ("dp", "sub"), axis=0, tiled=True)
    xf = piece.astype(jnp.float32)
    normed = (xf * lax.rsqrt(jnp.mean(xf * xf, axis=1, keepdims=True) + 1e-06) * gain).astype(
        jnp.bfloat16
    )
    gate = jnp.dot(normed, w_gate, preferred_element_type=jnp.float32)
    up_part = jnp.dot(normed, w_up, preferred_element_type=jnp.float32)
    hidden_part = (jax.nn.silu(gate) * up_part).astype(jnp.bfloat16)
    own_cols = lax.dynamic_slice_in_dim(piece, col_start, cols, 1)
    joined = jnp.concatenate([hidden_part, own_cols], axis=1)
    hidden = joined[:, :units]
    base = joined[:, units:]
    down = jnp.dot(
        lax.all_gather(hidden, ("dp", "sub"), axis=1, tiled=True),
        w_down,
        preferred_element_type=jnp.float32,
    )
    mixed = (base.astype(jnp.float32) + down).astype(jnp.bfloat16)
    return (kept[None], spare[None], mixed)


VMEM = pl.BlockSpec(memory_space=pltpu.VMEM)
SMEM = pl.BlockSpec(memory_space=pltpu.SMEM)
HBM = pl.BlockSpec(memory_space=pl.ANY)
NT = (((1,), (1,)), ((), ()))
TN = (((0,), (0,)), ((), ()))


def cost(mib):
    return pl.CostEstimate(flops=300 * (mib << 20), bytes_accessed=mib << 20, transcendentals=0)


def params(mib):
    return pltpu.CompilerParams(vmem_limit_bytes=mib << 20)


def place(n_sub):
    rank = lax.axis_index("dp")
    core = lax.axis_index("sub")
    return rank, core, rank * n_sub + core


def position_kernel(out_ref):
    out_ref[...] = lax.broadcasted_iota(jnp.int32, out_ref.shape, 1)


def attend_kernel(
    scale, n_dp, n_sub, latent, lengths, moves, at_ref, q_ref, fresh_ref, cache_ref, kept_ref, out_ref, near_ref, far_ref
):
    width, cap = cache_ref.shape
    half = cap // 2
    heads = q_ref.shape[1]
    _, _, device = place(n_sub)
    length = lengths[device]
    sending = moves[0, 0] == device
    for row in range(1, moves.shape[0]):
        sending = sending | (moves[row, 0] == device)
    fresh = jnp.broadcast_to(fresh_ref[...].astype(jnp.float32), (128, width)).T
    fresh = jnp.concatenate([fresh] * (cap // 128), axis=1)
    positions = at_ref[...]
    positions = jnp.concatenate([positions] * (width // positions.shape[0]), axis=0)
    appended = jnp.where(positions == length, fresh, cache_ref[...].astype(jnp.float32))
    drop = jnp.where(sending, half, cap)
    kept_ref[...] = jnp.where(positions >= drop, 0.0, appended).astype(jnp.bfloat16)
    keys = appended.astype(jnp.bfloat16)
    scores = lax.dot_general(q_ref[...], keys, TN, preferred_element_type=jnp.float32) * scale
    live = positions[:heads] <= length
    scores = jnp.where(live, scores, -1e30)
    top = jnp.max(scores, axis=1, keepdims=True)
    weights = jnp.where(live, jnp.exp(scores - top), 0.0)
    total = jnp.sum(weights, axis=1, keepdims=True)
    acc = lax.dot_general(
        weights.astype(jnp.bfloat16), keys[:latent], NT, preferred_element_type=jnp.float32
    )
    o_lat = (acc / total).astype(jnp.bfloat16)
    share = heads // n_dp
    upper = appended.T[half:].astype(jnp.bfloat16)
    near_ref[...] = upper[: half // 2]
    far_ref[...] = upper[half // 2 :]
    for peer in range(n_dp):
        out_ref[peer] = o_lat[peer * share : (peer + 1) * share]


def values_kernel(got_ref, uv_ref, resid_ref, out_ref, wide):
    n_dp = got_ref.shape[0]
    share, latent, vh = uv_ref.shape
    for src in range(n_dp):
        for k in range(latent // 128):
            wide[k, src * share : (src + 1) * share, :] = got_ref[
                src, 0:share, 128 * k : 128 * (k + 1)
            ].astype(jnp.float32)
    piece = resid_ref.shape[1] // n_dp
    for src in range(n_dp):
        out_ref[src : src + 1, share * vh :] = resid_ref[:, src * piece : (src + 1) * piece]
    for head in range(share):
        rows = jnp.concatenate(
            [wide[k, pl.ds(head, n_dp, stride=share), :] for k in range(latent // 128)], axis=1
        ).astype(jnp.bfloat16)
        out_ref[:, head * vh : (head + 1) * vh] = jnp.dot(
            rows, uv_ref[head], preferred_element_type=jnp.float32
        ).astype(jnp.bfloat16)


def interleave(first, second):
    n = first.shape[0]
    row = lax.broadcasted_iota(jnp.int32, (2 * n, 2 * n), 0)
    col = lax.broadcasted_iota(jnp.int32, (2 * n, 2 * n), 1)
    pick = (col == (row % 2) * n + row // 2).astype(jnp.bfloat16)
    both = jnp.concatenate([first, second], axis=0)
    return jnp.dot(pick, both, preferred_element_type=jnp.float32).astype(jnp.bfloat16)


def project_kernel(n_sub, own_ref, peer_ref, w_ref, sum_ref, out_ref, weights, sems):
    requests, half = out_ref.shape
    n_dp = requests // n_sub
    depth = w_ref.shape[0]
    chunks = sems.shape[0]
    wide = half // chunks
    rank, core, _ = place(n_sub)

    def fetch(i):
        start = pl.multiple_of(core * half + i * wide, 128)
        return pltpu.make_async_copy(
            w_ref.at[:, pl.ds(start, wide)], weights.at[i], sems.at[i]
        )

    for i in range(chunks):
        fetch(i).start()
    own = own_ref[:, :depth].astype(jnp.float32)
    peer = peer_ref[:, :depth].astype(jnp.float32)
    first = jnp.where(core == 0, own, peer).astype(jnp.bfloat16)
    second = jnp.where(core == 0, peer, own).astype(jnp.bfloat16)
    values = interleave(first, second)

    def resid_of(ref):
        every = ref[:, depth:].astype(jnp.float32)
        near = jnp.where(core == 0, every[: n_dp // 2], every[n_dp // 2 :])
        return jnp.concatenate([near[i : i + 1] for i in range(n_dp // 2)], axis=1)

    mine = resid_of(own_ref)
    theirs = resid_of(peer_ref)
    row = lax.broadcasted_iota(jnp.int32, (requests, wide), 0)
    for i in range(chunks):
        fetch(i).wait()
        span = slice(i * wide, (i + 1) * wide)
        part = jnp.dot(values, weights[i], preferred_element_type=jnp.float32)
        near = jnp.where(row % n_sub == core, mine[:, span], theirs[:, span])
        part = part + jnp.where(row // n_sub == rank, near, 0.0)
        sum_ref[:, span] = part
        out_ref[:, span] = part.astype(jnp.bfloat16)


def add_kernel(own_ref, peer_ref, sum_ref, send_ref):
    total = own_ref[...] + peer_ref[...].astype(jnp.float32)
    sum_ref[...] = total
    send_ref[...] = total.astype(jnp.bfloat16)


def last_add_kernel(own_ref, peer_ref, out_ref):
    out_ref[...] = (own_ref[...] + peer_ref[...].astype(jnp.float32)).astype(jnp.bfloat16)


def crosses(moves, core, step):
    return (moves[core, 1] // step) % 2 != (moves[core, 2] // step) % 2


def hop_kernel(n_sub, step, moves, kept_ref, come_ref, out_ref):
    _, core, _ = place(n_sub)
    crossing = crosses(moves, core, step)

    @pl.when(crossing)
    def _():
        out_ref[...] = come_ref[...]

    @pl.when(jnp.logical_not(crossing))
    def _():
        out_ref[...] = kept_ref[...]


def finish_kernel(n_sub, steps, moves, near_ref, near_come_ref, far_ref, far_come_ref, out_ref):
    rank, core, _ = place(n_sub)
    rows = near_ref.shape[0]
    wanted = rank == moves[core, 2]
    pairs = ((near_ref, near_come_ref), (far_ref, far_come_ref))
    for part, (step, (kept_ref, come_ref)) in enumerate(zip(steps, pairs)):
        crossing = crosses(moves, core, step)
        span = slice(part * rows, (part + 1) * rows)

        @pl.when(wanted & crossing)
        def _():
            out_ref[span, :] = come_ref[...]

        @pl.when(wanted & jnp.logical_not(crossing))
        def _():
            out_ref[span, :] = kept_ref[...]

        @pl.when(jnp.logical_not(wanted))
        def _():
            out_ref[span, :] = jnp.zeros_like(kept_ref)


def gate_up_kernel(
    n_sub, own_ref, peer_ref, gain_ref, gate_ref, up_ref, out_ref, base_ref, whole
):
    half = own_ref.shape[1]
    cols = base_ref.shape[1]
    rank, core, _ = place(n_sub)

    own = own_ref[...].astype(jnp.float32)
    peer = peer_ref[...].astype(jnp.float32)
    whole[:, :half] = jnp.where(core == 0, own, peer)
    whole[:, half:] = jnp.where(core == 0, peer, own)
    xf = whole[...]
    inverse = lax.rsqrt(jnp.mean(xf * xf, axis=1, keepdims=True) + 1e-06)
    normed = (xf * inverse * gain_ref[...].astype(jnp.float32).reshape(1, -1)).astype(jnp.bfloat16)
    start = pl.multiple_of(rank * n_sub * cols + core * (cols // 128 * 128), 128)
    near = whole[:, pl.ds(start, cols + 64)]
    base_ref[...] = jnp.where(core == 0, near[:, :cols], near[:, 64:]).astype(jnp.bfloat16)
    gate = lax.dot_general(gate_ref[...], normed, NT, preferred_element_type=jnp.float32)
    up = lax.dot_general(up_ref[...], normed, NT, preferred_element_type=jnp.float32)
    hidden = (gate * jax.nn.sigmoid(gate) * up).T.astype(jnp.bfloat16)
    for dst in range(out_ref.shape[0]):
        out_ref[dst] = hidden


def down_kernel(n_sub, own_ref, peer_ref, base_ref, down_ref, out_ref, hidden):
    units = own_ref.shape[2]
    _, core, _ = place(n_sub)

    for src in range(own_ref.shape[0]):
        own = own_ref[src].astype(jnp.float32)
        peer = peer_ref[src].astype(jnp.float32)
        first = jnp.where(core == 0, own, peer)
        second = jnp.where(core == 0, peer, own)
        hidden[:, src * n_sub * units : (src + 1) * n_sub * units] = jnp.concatenate(
            [first, second], axis=1
        ).astype(jnp.bfloat16)
    down = lax.dot_general(
        down_ref[...], hidden[...], NT, preferred_element_type=jnp.float32
    ).T
    out_ref[...] = (base_ref[...].astype(jnp.float32) + down).astype(jnp.bfloat16)


def swap(x, n_sub):
    return lax.ppermute(x, "sub", [(i, (i + 1) % n_sub) for i in range(n_sub)])


def exchange(x):
    return lax.all_to_all(x, "dp", split_axis=0, concat_axis=0, tiled=True)


def per_device_fast(
    queries, new_latent, cache, lengths, moves, resid, w_uv, w_out, norm_gain, w_gate, w_up, w_down
):
    n_dp = lax.axis_size("dp")
    n_sub = lax.axis_size("sub")
    cap, width = cache.shape[1:]
    heads = queries.shape[1]
    share, latent, vh = w_uv.shape
    half = cap // 2
    dim = w_out.shape[1]
    requests = n_dp * n_sub
    units = w_gate.shape[1]
    cols = w_down.shape[1]
    scale = (vh + width - latent) ** (-0.5)
    bf16, f32 = jnp.bfloat16, jnp.float32

    positions = pl.pallas_call(
        position_kernel,
        out_shape=jax.ShapeDtypeStruct((8, cap), jnp.int32),
        out_specs=VMEM,
        compiler_params=params(8),
        cost_estimate=cost(40),
        name="positions",
    )()
    kept, sent, near, far = pl.pallas_call(
        functools.partial(attend_kernel, scale, n_dp, n_sub, latent),
        out_shape=(
            jax.ShapeDtypeStruct((width, cap), bf16),
            jax.ShapeDtypeStruct((n_dp, share, latent), bf16),
            jax.ShapeDtypeStruct((half // 2, width), bf16),
            jax.ShapeDtypeStruct((half // 2, width), bf16),
        ),
        in_specs=[SMEM] * 2 + [VMEM] * 4,
        out_specs=(VMEM,) * 4,
        compiler_params=params(8),
        cost_estimate=cost(24),
        name="attend",
    )(lengths, moves, positions, queries[0].T, new_latent, cache[0].T)
    got, near, far = lax.optimization_barrier((exchange(sent), near, far))
    wide_half = dim // n_sub
    values = pl.pallas_call(
        values_kernel,
        out_shape=jax.ShapeDtypeStruct((n_dp, share * vh + dim // n_dp), bf16),
        in_specs=[VMEM] * 3,
        out_specs=VMEM,
        scratch_shapes=[pltpu.VMEM((latent // 128, n_dp * share, 128), f32)],
        compiler_params=params(8),
        cost_estimate=cost(1),
        name="values",
    )(got, w_uv, resid)
    peer_values = swap(values, n_sub)
    def cross(x, step):
        return lax.ppermute(x, "dp", [(i, i ^ step) for i in range(n_dp)])

    def hop(step, here, come):
        return pl.pallas_call(
            functools.partial(hop_kernel, n_sub, step),
            out_shape=jax.ShapeDtypeStruct((half // 2, width), bf16),
            in_specs=[SMEM, VMEM, VMEM],
            out_specs=VMEM,
            compiler_params=params(8),
            cost_estimate=cost(1),
            name="hop",
        )(moves, here, come)

    def add(total, come):
        return pl.pallas_call(
            add_kernel,
            out_shape=(
                jax.ShapeDtypeStruct((requests, wide_half), f32),
                jax.ShapeDtypeStruct((requests, wide_half), bf16),
            ),
            in_specs=[VMEM] * 2,
            out_specs=(VMEM, VMEM),
            compiler_params=params(8),
            cost_estimate=cost(1),
            name="add",
        )(total, come)

    near_come = cross(near, 4)
    far_come = cross(far, 2)
    total, part = pl.pallas_call(
        functools.partial(project_kernel, n_sub),
        out_shape=(
            jax.ShapeDtypeStruct((requests, wide_half), f32),
            jax.ShapeDtypeStruct((requests, wide_half), bf16),
        ),
        in_specs=[VMEM, VMEM, HBM],
        out_specs=(VMEM, VMEM),
        scratch_shapes=[
            pltpu.VMEM((4, share * vh, wide_half // 4), bf16),
            pltpu.SemaphoreType.DMA((4,)),
        ],
        compiler_params=params(38),
        cost_estimate=cost(24),
        name="project",
    )(values, peer_values, w_out)
    near_come, far_come, part = lax.optimization_barrier((near_come, far_come, part))
    near = hop(4, near, near_come)
    far = hop(2, far, far_come)
    near_come = cross(near, 2)
    total, part = add(total, cross(part, 1))
    near_come, part = lax.optimization_barrier((near_come, part))
    near = hop(2, near, near_come)
    near_come = cross(near, 1)
    far_come = cross(far, 1)
    total, part = add(total, cross(part, 2))
    far = hop(1, far, far_come)
    come, near_come, far = lax.optimization_barrier((cross(part, 4), near_come, far))
    x_half = pl.pallas_call(
        last_add_kernel,
        out_shape=jax.ShapeDtypeStruct((requests, wide_half), bf16),
        in_specs=[VMEM] * 2,
        out_specs=VMEM,
        compiler_params=params(8),
        cost_estimate=cost(1),
        name="last_add",
    )(total, come)
    far_come = cross(far, 4)
    hidden, base = pl.pallas_call(
        functools.partial(gate_up_kernel, n_sub),
        out_shape=(
            jax.ShapeDtypeStruct((n_dp, requests, units), bf16),
            jax.ShapeDtypeStruct((requests, cols), bf16),
        ),
        in_specs=[VMEM] * 5,
        out_specs=(VMEM, VMEM),
        scratch_shapes=[pltpu.VMEM((requests, dim), f32)],
        compiler_params=params(24),
        cost_estimate=cost(24),
        name="gate_up",
    )(x_half, swap(x_half, n_sub), norm_gain, w_gate.T, w_up.T)
    hidden, far_come = lax.optimization_barrier((hidden, far_come))
    every = exchange(hidden)
    mixed = pl.pallas_call(
        functools.partial(down_kernel, n_sub),
        out_shape=jax.ShapeDtypeStruct((requests, cols), bf16),
        in_specs=[VMEM] * 4,
        out_specs=VMEM,
        scratch_shapes=[pltpu.VMEM((requests, n_dp * n_sub * units), bf16)],
        compiler_params=params(16),
        cost_estimate=cost(1),
        name="down",
    )(every, swap(every, n_sub), base, w_down.T)
    spare = pl.pallas_call(
        functools.partial(finish_kernel, n_sub, (1, 4)),
        out_shape=jax.ShapeDtypeStruct((half, width), bf16),
        in_specs=[SMEM] + [VMEM] * 4,
        out_specs=VMEM,
        compiler_params=params(8),
        cost_estimate=cost(1),
        name="finish",
    )(moves, near, near_come, far, far_come)
    return (kept.T[None], spare[None], mixed)


def per_device(*args):
    queries, cache, moves, w_uv, w_out = args[0], args[2], args[4], args[6], args[7]
    w_gate, w_down = args[9], args[11]
    n_dp = lax.axis_size("dp")
    n_sub = lax.axis_size("sub")
    fits = (
        n_sub == 2
        and n_dp == 8
        and moves.shape[0] == n_sub
        and cache.shape[1] % 128 == 0
        and queries.shape[1] // n_dp == 16
        and w_uv.shape[1] == 512
        and w_out.shape[1] % (n_sub * 4 * 128) == 0
        and w_gate.shape[1] == cache.shape[2]
        and w_down.shape[1] % 64 == 0
    )
    return per_device_fast(*args) if fits else per_device_any(*args)


def solution(mesh):
    return jax.shard_map(
        per_device,
        mesh=mesh,
        in_specs=(
            P(("groups", "dp", "sub"), None, None),
            P(("groups", "dp", "sub"), None),
            P(("groups", "dp", "sub"), None, None),
            P("groups"),
            P("groups", None),
            P(("groups", "dp", "sub"), None),
            P("dp", None, None),
            P("dp", None),
            P(),
            P(None, ("dp", "sub")),
            P(None, ("dp", "sub")),
            P(None, ("dp", "sub")),
        ),
        out_specs=(
            P(("groups", "dp", "sub"), None, None),
            P(("groups", "dp", "sub"), None, None),
            P("groups", ("dp", "sub")),
        ),
        check_vma=False,
    )
```

```python
import functools

import jax
import jax.numpy as jnp
from jax import lax
from jax.experimental import pallas as pl
from jax.experimental.pallas import tpu as pltpu
from jax.sharding import PartitionSpec as P


def partial_attend(query, keys, live, scale, latent):
    scores = jnp.einsum("hw,pw->hp", query, keys, preferred_element_type=jnp.float32) * scale
    scores = jnp.where(live[None, :], scores, -1e30)
    top = jnp.max(scores, axis=1)
    weights = jnp.where(live[None, :], jnp.exp(scores - top[:, None]), 0.0)
    total = jnp.sum(weights, axis=1)
    acc = jnp.dot(
        weights.astype(jnp.bfloat16), keys[:, :latent], preferred_element_type=jnp.float32
    )
    return (top, total, acc)


def route(spread, partner, present):
    shape = (spread.shape[0],) + (1,) * (spread.ndim - 1)
    picked = jnp.take(spread, partner, axis=0)
    return jnp.where(present.reshape(shape), picked, jnp.zeros((), spread.dtype))


def per_device_any(
    queries, new_latent, cache, lengths, moves, resid, w_uv, w_out, norm_gain, w_gate, w_up, w_down
):
    n_dp = lax.axis_size("dp")
    n_sub = lax.axis_size("sub")
    rank = lax.axis_index("dp")
    core = lax.axis_index("sub")
    device = rank * n_sub + core
    cap = cache.shape[1]
    half = cap // 2
    width = cache.shape[2]
    heads = queries.shape[1]
    latent = w_uv.shape[1]
    scale = (w_uv.shape[2] + width - latent) ** (-0.5)
    length = lax.dynamic_index_in_dim(lengths, device, 0, keepdims=False)
    positions = jnp.arange(cap, dtype=jnp.int32)
    appended = jnp.where((positions == length)[:, None], new_latent[0][None, :], cache[0])
    moved_req = moves[:, 0]
    sources = moves[:, 1]
    targets = moves[:, 2]
    same_core = moved_req % n_sub == core
    sending = jnp.any(moved_req == device)
    peers = jnp.arange(n_dp, dtype=jnp.int32)
    to_match = same_core[None, :] & (peers[:, None] == targets[None, :])
    from_of = jnp.sum(jnp.where(to_match, sources[None, :], 0), axis=1)
    to_has = jnp.any(to_match, axis=1)
    zero_bf = jnp.zeros((), jnp.bfloat16)
    upper = jnp.where(sending, appended[half:], zero_bf).reshape(n_dp, -1)
    spread = lax.all_to_all(upper, "dp", split_axis=0, concat_axis=0, tiled=True)
    landed = lax.all_to_all(
        route(spread, from_of, to_has), "dp", split_axis=0, concat_axis=0, tiled=True
    )
    spare = landed.reshape(half, width)
    kept = jnp.where(sending & (positions >= half)[:, None], zero_bf, appended)
    top, total, acc = partial_attend(queries[0], appended, positions <= length, scale, latent)
    o_lat = (acc / total[:, None]).astype(jnp.bfloat16)
    owners = lax.all_to_all(
        o_lat.reshape(n_dp, heads // n_dp, latent), "dp", split_axis=0, concat_axis=0, tiled=True
    )
    values = jnp.einsum("rhl,hlv->rhv", owners, w_uv, preferred_element_type=jnp.float32).astype(
        jnp.bfloat16
    )
    values = values.reshape(n_dp, -1)
    cols = w_down.shape[1]
    units = w_gate.shape[1]
    col_start = device * cols
    gain = norm_gain.astype(jnp.float32)
    summed = lax.psum_scatter(
        jnp.dot(values, w_out, preferred_element_type=jnp.float32),
        "dp",
        scatter_dimension=0,
        tiled=True,
    )
    x_rows = (resid.astype(jnp.float32) + summed).astype(jnp.bfloat16)
    piece = lax.all_gather(x_rows, ("dp", "sub"), axis=0, tiled=True)
    xf = piece.astype(jnp.float32)
    normed = (xf * lax.rsqrt(jnp.mean(xf * xf, axis=1, keepdims=True) + 1e-06) * gain).astype(
        jnp.bfloat16
    )
    gate = jnp.dot(normed, w_gate, preferred_element_type=jnp.float32)
    up_part = jnp.dot(normed, w_up, preferred_element_type=jnp.float32)
    hidden_part = (jax.nn.silu(gate) * up_part).astype(jnp.bfloat16)
    own_cols = lax.dynamic_slice_in_dim(piece, col_start, cols, 1)
    joined = jnp.concatenate([hidden_part, own_cols], axis=1)
    hidden = joined[:, :units]
    base = joined[:, units:]
    down = jnp.dot(
        lax.all_gather(hidden, ("dp", "sub"), axis=1, tiled=True),
        w_down,
        preferred_element_type=jnp.float32,
    )
    mixed = (base.astype(jnp.float32) + down).astype(jnp.bfloat16)
    return (kept[None], spare[None], mixed)


VMEM = pl.BlockSpec(memory_space=pltpu.VMEM)
SMEM = pl.BlockSpec(memory_space=pltpu.SMEM)
HBM = pl.BlockSpec(memory_space=pl.ANY)
NT = (((1,), (1,)), ((), ()))
TN = (((0,), (0,)), ((), ()))


def cost(mib):
    return pl.CostEstimate(flops=300 * (mib << 20), bytes_accessed=mib << 20, transcendentals=0)


def params(mib):
    return pltpu.CompilerParams(vmem_limit_bytes=mib << 20)


def place(n_sub):
    rank = lax.axis_index("dp")
    core = lax.axis_index("sub")
    return rank, core, rank * n_sub + core


def position_kernel(out_ref):
    out_ref[...] = lax.broadcasted_iota(jnp.int32, out_ref.shape, 1)


def pack(x):
    rows, width = x.shape
    whole = width // 128 * 128
    pieces = [x[:, i : i + 128] for i in range(0, whole, 128)]
    rest = jnp.concatenate([x[: rows // 2, whole:], x[rows // 2 :, whole:]], axis=1)
    return jnp.concatenate(pieces + [rest], axis=0)


def unpack(x, rows, width):
    whole = width // 128 * 128
    pieces = [x[rows * i : rows * (i + 1)] for i in range(whole // 128)]
    rest = x[rows * (whole // 128) :]
    tail = jnp.concatenate([rest[:, : width - whole], rest[:, width - whole :]], axis=0)
    return jnp.concatenate(pieces + [tail], axis=1)


def attend_kernel(
    scale, n_dp, n_sub, latent, lengths, moves, at_ref, q_ref, fresh_ref, cache_ref, kept_ref, out_ref, near_ref, far_ref
):
    width, cap = cache_ref.shape
    half = cap // 2
    heads = q_ref.shape[1]
    _, _, device = place(n_sub)
    length = lengths[device]
    sending = moves[0, 0] == device
    for row in range(1, moves.shape[0]):
        sending = sending | (moves[row, 0] == device)
    fresh = jnp.broadcast_to(fresh_ref[...].astype(jnp.float32), (128, width)).T
    fresh = jnp.concatenate([fresh] * (cap // 128), axis=1)
    positions = at_ref[...]
    positions = jnp.concatenate([positions] * (width // positions.shape[0]), axis=0)
    appended = jnp.where(positions == length, fresh, cache_ref[...].astype(jnp.float32))
    drop = jnp.where(sending, half, cap)
    kept_ref[...] = jnp.where(positions >= drop, 0.0, appended).astype(jnp.bfloat16)
    keys = appended.astype(jnp.bfloat16)
    scores = lax.dot_general(q_ref[...], keys, TN, preferred_element_type=jnp.float32) * scale
    live = positions[:heads] <= length
    scores = jnp.where(live, scores, -1e30)
    top = jnp.max(scores, axis=1, keepdims=True)
    weights = jnp.where(live, jnp.exp(scores - top), 0.0)
    total = jnp.sum(weights, axis=1, keepdims=True)
    acc = lax.dot_general(
        weights.astype(jnp.bfloat16), keys[:latent], NT, preferred_element_type=jnp.float32
    )
    o_lat = (acc / total).astype(jnp.bfloat16)
    share = heads // n_dp
    upper = appended.T[half:]
    near_ref[...] = pack(upper[: half // 2]).astype(jnp.bfloat16)
    far_ref[...] = pack(upper[half // 2 :]).astype(jnp.bfloat16)
    for peer in range(n_dp):
        out_ref[peer] = o_lat[peer * share : (peer + 1) * share]


def values_kernel(got_ref, uv_ref, resid_ref, out_ref, wide):
    n_dp = got_ref.shape[0]
    share, latent, vh = uv_ref.shape
    for src in range(n_dp):
        for k in range(latent // 128):
            wide[k, src * share : (src + 1) * share, :] = got_ref[
                src, 0:share, 128 * k : 128 * (k + 1)
            ].astype(jnp.float32)
    piece = resid_ref.shape[1] // n_dp
    for src in range(n_dp):
        out_ref[src : src + 1, share * vh :] = resid_ref[:, src * piece : (src + 1) * piece]
    for head in range(share):
        rows = jnp.concatenate(
            [wide[k, pl.ds(head, n_dp, stride=share), :] for k in range(latent // 128)], axis=1
        ).astype(jnp.bfloat16)
        out_ref[:, head * vh : (head + 1) * vh] = jnp.dot(
            rows, uv_ref[head], preferred_element_type=jnp.float32
        ).astype(jnp.bfloat16)


def interleave(first, second):
    n = first.shape[0]
    row = lax.broadcasted_iota(jnp.int32, (2 * n, 2 * n), 0)
    col = lax.broadcasted_iota(jnp.int32, (2 * n, 2 * n), 1)
    pick = (col == (row % 2) * n + row // 2).astype(jnp.bfloat16)
    both = jnp.concatenate([first, second], axis=0)
    return jnp.dot(pick, both, preferred_element_type=jnp.float32).astype(jnp.bfloat16)


def project_kernel(n_sub, own_ref, peer_ref, w_ref, sum_ref, out_ref, weights, sems):
    requests, half = out_ref.shape
    n_dp = requests // n_sub
    depth = w_ref.shape[0]
    chunks = sems.shape[0]
    wide = half // chunks
    rank, core, _ = place(n_sub)

    def fetch(i):
        start = pl.multiple_of(core * half + i * wide, 128)
        return pltpu.make_async_copy(
            w_ref.at[:, pl.ds(start, wide)], weights.at[i], sems.at[i]
        )

    for i in range(chunks):
        fetch(i).start()
    own = own_ref[:, :depth].astype(jnp.float32)
    peer = peer_ref[:, :depth].astype(jnp.float32)
    first = jnp.where(core == 0, own, peer).astype(jnp.bfloat16)
    second = jnp.where(core == 0, peer, own).astype(jnp.bfloat16)
    values = interleave(first, second)

    def resid_of(ref):
        every = ref[:, depth:].astype(jnp.float32)
        near = jnp.where(core == 0, every[: n_dp // 2], every[n_dp // 2 :])
        return jnp.concatenate([near[i : i + 1] for i in range(n_dp // 2)], axis=1)

    mine = resid_of(own_ref)
    theirs = resid_of(peer_ref)
    row = lax.broadcasted_iota(jnp.int32, (requests, wide), 0)
    for i in range(chunks):
        fetch(i).wait()
        span = slice(i * wide, (i + 1) * wide)
        part = jnp.dot(values, weights[i], preferred_element_type=jnp.float32)
        near = jnp.where(row % n_sub == core, mine[:, span], theirs[:, span])
        part = part + jnp.where(row // n_sub == rank, near, 0.0)
        sum_ref[:, span] = part
        out_ref[:, span] = part.astype(jnp.bfloat16)


def add_kernel(own_ref, peer_ref, sum_ref, send_ref):
    total = own_ref[...] + peer_ref[...].astype(jnp.float32)
    sum_ref[...] = total
    send_ref[...] = total.astype(jnp.bfloat16)


def last_add_kernel(own_ref, peer_ref, out_ref):
    out_ref[...] = (own_ref[...] + peer_ref[...].astype(jnp.float32)).astype(jnp.bfloat16)


def crosses(moves, core, step):
    source, target = moves[core, 1], moves[core, 2]
    bits = {1: (1,), 2: (2, 4), 6: (4,)}[step]
    return sum(source // bit + target // bit for bit in bits) % 2 != 0


def hop_kernel(n_sub, step, moves, kept_ref, come_ref, out_ref):
    _, core, _ = place(n_sub)
    crossing = crosses(moves, core, step)

    @pl.when(crossing)
    def _():
        out_ref[...] = come_ref[...]

    @pl.when(jnp.logical_not(crossing))
    def _():
        out_ref[...] = kept_ref[...]


def finish_kernel(n_sub, steps, moves, near_ref, near_come_ref, far_ref, far_come_ref, out_ref):
    rank, core, _ = place(n_sub)
    rows = out_ref.shape[0] // 2
    width = out_ref.shape[1]
    wanted = rank == moves[core, 2]
    pairs = ((near_ref, near_come_ref), (far_ref, far_come_ref))

    @pl.when(jnp.logical_not(wanted))
    def _():
        out_ref[...] = jnp.zeros_like(out_ref)

    @pl.when(wanted)
    def _():
        for part, (step, (kept_ref, come_ref)) in enumerate(zip(steps, pairs)):
            kept = kept_ref[...].astype(jnp.float32)
            come = come_ref[...].astype(jnp.float32)
            picked = jnp.where(crosses(moves, core, step), come, kept)
            out_ref[part * rows : (part + 1) * rows, :] = unpack(picked, rows, width).astype(
                jnp.bfloat16
            )


def gate_up_kernel(
    n_sub, own_ref, peer_ref, gain_ref, gate_ref, up_ref, out_ref, base_ref, whole
):
    half = own_ref.shape[1]
    cols = base_ref.shape[1]
    rank, core, _ = place(n_sub)

    own = own_ref[...].astype(jnp.float32)
    peer = peer_ref[...].astype(jnp.float32)
    whole[:, :half] = jnp.where(core == 0, own, peer)
    whole[:, half:] = jnp.where(core == 0, peer, own)
    xf = whole[...]
    inverse = lax.rsqrt(jnp.mean(xf * xf, axis=1, keepdims=True) + 1e-06)
    normed = (xf * inverse * gain_ref[...].astype(jnp.float32).reshape(1, -1)).astype(jnp.bfloat16)
    start = pl.multiple_of(rank * n_sub * cols + core * (cols // 128 * 128), 128)
    near = whole[:, pl.ds(start, cols + 64)]
    base_ref[...] = jnp.where(core == 0, near[:, :cols], near[:, 64:]).astype(jnp.bfloat16)
    gate = lax.dot_general(gate_ref[...], normed, NT, preferred_element_type=jnp.float32)
    up = lax.dot_general(up_ref[...], normed, NT, preferred_element_type=jnp.float32)
    hidden = pack((gate * jax.nn.sigmoid(gate) * up).T).astype(jnp.bfloat16)
    for dst in range(out_ref.shape[0]):
        out_ref[dst] = hidden


def down_kernel(n_sub, own_ref, peer_ref, base_ref, down_ref, out_ref, hidden):
    requests = out_ref.shape[0]
    units = own_ref.shape[1] * 128 // requests
    _, core, _ = place(n_sub)

    for src in range(own_ref.shape[0]):
        own = unpack(own_ref[src].astype(jnp.float32), requests, units)
        peer = unpack(peer_ref[src].astype(jnp.float32), requests, units)
        first = jnp.where(core == 0, own, peer)
        second = jnp.where(core == 0, peer, own)
        hidden[:, src * n_sub * units : (src + 1) * n_sub * units] = jnp.concatenate(
            [first, second], axis=1
        ).astype(jnp.bfloat16)
    down = lax.dot_general(
        down_ref[...], hidden[...], NT, preferred_element_type=jnp.float32
    ).T
    out_ref[...] = (base_ref[...].astype(jnp.float32) + down).astype(jnp.bfloat16)


def swap(x, n_sub):
    return lax.ppermute(x, "sub", [(i, (i + 1) % n_sub) for i in range(n_sub)])


def exchange(x):
    return lax.all_to_all(x, "dp", split_axis=0, concat_axis=0, tiled=True)


def per_device_fast(
    queries, new_latent, cache, lengths, moves, resid, w_uv, w_out, norm_gain, w_gate, w_up, w_down
):
    n_dp = lax.axis_size("dp")
    n_sub = lax.axis_size("sub")
    cap, width = cache.shape[1:]
    heads = queries.shape[1]
    share, latent, vh = w_uv.shape
    half = cap // 2
    dim = w_out.shape[1]
    requests = n_dp * n_sub
    units = w_gate.shape[1]
    cols = w_down.shape[1]
    scale = (vh + width - latent) ** (-0.5)
    bf16, f32 = jnp.bfloat16, jnp.float32

    positions = pl.pallas_call(
        position_kernel,
        out_shape=jax.ShapeDtypeStruct((8, cap), jnp.int32),
        out_specs=VMEM,
        compiler_params=params(8),
        cost_estimate=cost(40),
        name="positions",
    )()
    kept, sent, near, far = pl.pallas_call(
        functools.partial(attend_kernel, scale, n_dp, n_sub, latent),
        out_shape=(
            jax.ShapeDtypeStruct((width, cap), bf16),
            jax.ShapeDtypeStruct((n_dp, share, latent), bf16),
            jax.ShapeDtypeStruct((half // 2 * width // 128, 128), bf16),
            jax.ShapeDtypeStruct((half // 2 * width // 128, 128), bf16),
        ),
        in_specs=[SMEM] * 2 + [VMEM] * 4,
        out_specs=(VMEM,) * 4,
        compiler_params=params(8),
        cost_estimate=cost(24),
        name="attend",
    )(lengths, moves, positions, queries[0].T, new_latent, cache[0].T)
    got, near, far = lax.optimization_barrier((exchange(sent), near, far))
    wide_half = dim // n_sub
    values = pl.pallas_call(
        values_kernel,
        out_shape=jax.ShapeDtypeStruct((n_dp, share * vh + dim // n_dp), bf16),
        in_specs=[VMEM] * 3,
        out_specs=VMEM,
        scratch_shapes=[pltpu.VMEM((latent // 128, n_dp * share, 128), f32)],
        compiler_params=params(8),
        cost_estimate=cost(1),
        name="values",
    )(got, w_uv, resid)
    peer_values = swap(values, n_sub)
    def cross(x, step):
        return lax.ppermute(x, "dp", [(i, i ^ step) for i in range(n_dp)])

    def hop(step, here, come):
        return pl.pallas_call(
            functools.partial(hop_kernel, n_sub, step),
            out_shape=jax.ShapeDtypeStruct(here.shape, bf16),
            in_specs=[SMEM, VMEM, VMEM],
            out_specs=VMEM,
            compiler_params=params(8),
            cost_estimate=cost(1),
            name="hop",
        )(moves, here, come)

    def add(total, come):
        return pl.pallas_call(
            add_kernel,
            out_shape=(
                jax.ShapeDtypeStruct((requests, wide_half), f32),
                jax.ShapeDtypeStruct((requests, wide_half), bf16),
            ),
            in_specs=[VMEM] * 2,
            out_specs=(VMEM, VMEM),
            compiler_params=params(8),
            cost_estimate=cost(1),
            name="add",
        )(total, come)

    near_come = cross(near, 6)
    far_come = cross(far, 2)
    total, part = pl.pallas_call(
        functools.partial(project_kernel, n_sub),
        out_shape=(
            jax.ShapeDtypeStruct((requests, wide_half), f32),
            jax.ShapeDtypeStruct((requests, wide_half), bf16),
        ),
        in_specs=[VMEM, VMEM, HBM],
        out_specs=(VMEM, VMEM),
        scratch_shapes=[
            pltpu.VMEM((4, share * vh, wide_half // 4), bf16),
            pltpu.SemaphoreType.DMA((4,)),
        ],
        compiler_params=params(38),
        cost_estimate=cost(24),
        name="project",
    )(values, peer_values, w_out)
    near_come, far_come, part = lax.optimization_barrier((near_come, far_come, part))
    near = hop(6, near, near_come)
    far = hop(2, far, far_come)
    near_come = cross(near, 2)
    total, part = add(total, cross(part, 1))
    near = hop(2, near, near_come)
    near_come = cross(near, 1)
    far_come = cross(far, 1)
    total, part = add(total, cross(part, 2))
    far = hop(1, far, far_come)
    come, near_come, far = lax.optimization_barrier((cross(part, 6), near_come, far))
    x_half = pl.pallas_call(
        last_add_kernel,
        out_shape=jax.ShapeDtypeStruct((requests, wide_half), bf16),
        in_specs=[VMEM] * 2,
        out_specs=VMEM,
        compiler_params=params(8),
        cost_estimate=cost(1),
        name="last_add",
    )(total, come)
    far_come = cross(far, 6)
    hidden, base = pl.pallas_call(
        functools.partial(gate_up_kernel, n_sub),
        out_shape=(
            jax.ShapeDtypeStruct((n_dp, requests * units // 128, 128), bf16),
            jax.ShapeDtypeStruct((requests, cols), bf16),
        ),
        in_specs=[VMEM] * 5,
        out_specs=(VMEM, VMEM),
        scratch_shapes=[pltpu.VMEM((requests, dim), f32)],
        compiler_params=params(24),
        cost_estimate=cost(24),
        name="gate_up",
    )(x_half, swap(x_half, n_sub), norm_gain, w_gate.T, w_up.T)
    hidden, far_come = lax.optimization_barrier((hidden, far_come))
    every = exchange(hidden)
    mixed = pl.pallas_call(
        functools.partial(down_kernel, n_sub),
        out_shape=jax.ShapeDtypeStruct((requests, cols), bf16),
        in_specs=[VMEM] * 4,
        out_specs=VMEM,
        scratch_shapes=[pltpu.VMEM((requests, n_dp * n_sub * units), bf16)],
        compiler_params=params(16),
        cost_estimate=cost(1),
        name="down",
    )(every, swap(every, n_sub), base, w_down.T)
    spare = pl.pallas_call(
        functools.partial(finish_kernel, n_sub, (1, 6)),
        out_shape=jax.ShapeDtypeStruct((half, width), bf16),
        in_specs=[SMEM] + [VMEM] * 4,
        out_specs=VMEM,
        compiler_params=params(8),
        cost_estimate=cost(1),
        name="finish",
    )(moves, near, near_come, far, far_come)
    return (kept.T[None], spare[None], mixed)


def per_device(*args):
    queries, cache, moves, w_uv, w_out = args[0], args[2], args[4], args[6], args[7]
    w_gate, w_down = args[9], args[11]
    n_dp = lax.axis_size("dp")
    n_sub = lax.axis_size("sub")
    fits = (
        n_sub == 2
        and n_dp == 8
        and moves.shape[0] == n_sub
        and cache.shape[1] % 128 == 0
        and queries.shape[1] // n_dp == 16
        and w_uv.shape[1] == 512
        and w_out.shape[1] % (n_sub * 4 * 128) == 0
        and w_gate.shape[1] % 128 == 64
        and cache.shape[2] % 128 == 64
        and w_down.shape[1] % 64 == 0
    )
    return per_device_fast(*args) if fits else per_device_any(*args)


def solution(mesh):
    return jax.shard_map(
        per_device,
        mesh=mesh,
        in_specs=(
            P(("groups", "dp", "sub"), None, None),
            P(("groups", "dp", "sub"), None),
            P(("groups", "dp", "sub"), None, None),
            P("groups"),
            P("groups", None),
            P(("groups", "dp", "sub"), None),
            P("dp", None, None),
            P("dp", None),
            P(),
            P(None, ("dp", "sub")),
            P(None, ("dp", "sub")),
            P(None, ("dp", "sub")),
        ),
        out_specs=(
            P(("groups", "dp", "sub"), None, None),
            P(("groups", "dp", "sub"), None, None),
            P("groups", ("dp", "sub")),
        ),
        check_vma=False,
    )
```

```python
import functools

import jax
import jax.numpy as jnp
from jax import lax
from jax.experimental import pallas as pl
from jax.experimental.pallas import tpu as pltpu
from jax.sharding import PartitionSpec as P


def partial_attend(query, keys, live, scale, latent):
    scores = jnp.einsum("hw,pw->hp", query, keys, preferred_element_type=jnp.float32) * scale
    scores = jnp.where(live[None, :], scores, -1e30)
    top = jnp.max(scores, axis=1)
    weights = jnp.where(live[None, :], jnp.exp(scores - top[:, None]), 0.0)
    total = jnp.sum(weights, axis=1)
    acc = jnp.dot(
        weights.astype(jnp.bfloat16), keys[:, :latent], preferred_element_type=jnp.float32
    )
    return (top, total, acc)


def route(spread, partner, present):
    shape = (spread.shape[0],) + (1,) * (spread.ndim - 1)
    picked = jnp.take(spread, partner, axis=0)
    return jnp.where(present.reshape(shape), picked, jnp.zeros((), spread.dtype))


def per_device_any(
    queries, new_latent, cache, lengths, moves, resid, w_uv, w_out, norm_gain, w_gate, w_up, w_down
):
    n_dp = lax.axis_size("dp")
    n_sub = lax.axis_size("sub")
    rank = lax.axis_index("dp")
    core = lax.axis_index("sub")
    device = rank * n_sub + core
    cap = cache.shape[1]
    half = cap // 2
    width = cache.shape[2]
    heads = queries.shape[1]
    latent = w_uv.shape[1]
    scale = (w_uv.shape[2] + width - latent) ** (-0.5)
    length = lax.dynamic_index_in_dim(lengths, device, 0, keepdims=False)
    positions = jnp.arange(cap, dtype=jnp.int32)
    appended = jnp.where((positions == length)[:, None], new_latent[0][None, :], cache[0])
    moved_req = moves[:, 0]
    sources = moves[:, 1]
    targets = moves[:, 2]
    same_core = moved_req % n_sub == core
    sending = jnp.any(moved_req == device)
    peers = jnp.arange(n_dp, dtype=jnp.int32)
    to_match = same_core[None, :] & (peers[:, None] == targets[None, :])
    from_of = jnp.sum(jnp.where(to_match, sources[None, :], 0), axis=1)
    to_has = jnp.any(to_match, axis=1)
    zero_bf = jnp.zeros((), jnp.bfloat16)
    upper = jnp.where(sending, appended[half:], zero_bf).reshape(n_dp, -1)
    spread = lax.all_to_all(upper, "dp", split_axis=0, concat_axis=0, tiled=True)
    landed = lax.all_to_all(
        route(spread, from_of, to_has), "dp", split_axis=0, concat_axis=0, tiled=True
    )
    spare = landed.reshape(half, width)
    kept = jnp.where(sending & (positions >= half)[:, None], zero_bf, appended)
    top, total, acc = partial_attend(queries[0], appended, positions <= length, scale, latent)
    o_lat = (acc / total[:, None]).astype(jnp.bfloat16)
    owners = lax.all_to_all(
        o_lat.reshape(n_dp, heads // n_dp, latent), "dp", split_axis=0, concat_axis=0, tiled=True
    )
    values = jnp.einsum("rhl,hlv->rhv", owners, w_uv, preferred_element_type=jnp.float32).astype(
        jnp.bfloat16
    )
    values = values.reshape(n_dp, -1)
    cols = w_down.shape[1]
    units = w_gate.shape[1]
    col_start = device * cols
    gain = norm_gain.astype(jnp.float32)
    summed = lax.psum_scatter(
        jnp.dot(values, w_out, preferred_element_type=jnp.float32),
        "dp",
        scatter_dimension=0,
        tiled=True,
    )
    x_rows = (resid.astype(jnp.float32) + summed).astype(jnp.bfloat16)
    piece = lax.all_gather(x_rows, ("dp", "sub"), axis=0, tiled=True)
    xf = piece.astype(jnp.float32)
    normed = (xf * lax.rsqrt(jnp.mean(xf * xf, axis=1, keepdims=True) + 1e-06) * gain).astype(
        jnp.bfloat16
    )
    gate = jnp.dot(normed, w_gate, preferred_element_type=jnp.float32)
    up_part = jnp.dot(normed, w_up, preferred_element_type=jnp.float32)
    hidden_part = (jax.nn.silu(gate) * up_part).astype(jnp.bfloat16)
    own_cols = lax.dynamic_slice_in_dim(piece, col_start, cols, 1)
    joined = jnp.concatenate([hidden_part, own_cols], axis=1)
    hidden = joined[:, :units]
    base = joined[:, units:]
    down = jnp.dot(
        lax.all_gather(hidden, ("dp", "sub"), axis=1, tiled=True),
        w_down,
        preferred_element_type=jnp.float32,
    )
    mixed = (base.astype(jnp.float32) + down).astype(jnp.bfloat16)
    return (kept[None], spare[None], mixed)


VMEM = pl.BlockSpec(memory_space=pltpu.VMEM)
SMEM = pl.BlockSpec(memory_space=pltpu.SMEM)
HBM = pl.BlockSpec(memory_space=pl.ANY)
NT = (((1,), (1,)), ((), ()))
TN = (((0,), (0,)), ((), ()))


def cost(mib):
    return pl.CostEstimate(flops=300 * (mib << 20), bytes_accessed=mib << 20, transcendentals=0)


def params(mib):
    return pltpu.CompilerParams(vmem_limit_bytes=mib << 20)


def place(n_sub):
    rank = lax.axis_index("dp")
    core = lax.axis_index("sub")
    return rank, core, rank * n_sub + core


def position_kernel(out_ref):
    out_ref[...] = lax.broadcasted_iota(jnp.int32, out_ref.shape, 1)


def pack(x):
    rows, width = x.shape
    whole = width // 128 * 128
    pieces = [x[:, i : i + 128] for i in range(0, whole, 128)]
    rest = jnp.concatenate([x[: rows // 2, whole:], x[rows // 2 :, whole:]], axis=1)
    return jnp.concatenate(pieces + [rest], axis=0)


def unpack(x, rows, width):
    whole = width // 128 * 128
    pieces = [x[rows * i : rows * (i + 1)] for i in range(whole // 128)]
    rest = x[rows * (whole // 128) :]
    tail = jnp.concatenate([rest[:, : width - whole], rest[:, width - whole :]], axis=0)
    return jnp.concatenate(pieces + [tail], axis=1)


def attend_kernel(
    scale, n_dp, n_sub, latent, lengths, moves, at_ref, q_ref, fresh_ref, cache_ref, kept_ref, out_ref, near_ref, far_ref
):
    width, cap = cache_ref.shape
    half = cap // 2
    heads = q_ref.shape[1]
    _, _, device = place(n_sub)
    length = lengths[device]
    sending = moves[0, 0] == device
    for row in range(1, moves.shape[0]):
        sending = sending | (moves[row, 0] == device)
    fresh = jnp.broadcast_to(fresh_ref[...].astype(jnp.float32), (128, width)).T
    fresh = jnp.concatenate([fresh] * (cap // 128), axis=1)
    positions = at_ref[...]
    positions = jnp.concatenate([positions] * (width // positions.shape[0]), axis=0)
    appended = jnp.where(positions == length, fresh, cache_ref[...].astype(jnp.float32))
    drop = jnp.where(sending, half, cap)
    kept_ref[...] = jnp.where(positions >= drop, 0.0, appended).astype(jnp.bfloat16)
    keys = appended.astype(jnp.bfloat16)
    scores = lax.dot_general(q_ref[...], keys, TN, preferred_element_type=jnp.float32) * scale
    live = positions[:heads] <= length
    scores = jnp.where(live, scores, -1e30)
    top = jnp.max(scores, axis=1, keepdims=True)
    weights = jnp.where(live, jnp.exp(scores - top), 0.0)
    total = jnp.sum(weights, axis=1, keepdims=True)
    acc = lax.dot_general(
        weights.astype(jnp.bfloat16), keys[:latent], NT, preferred_element_type=jnp.float32
    )
    o_lat = (acc / total).astype(jnp.bfloat16)
    share = heads // n_dp
    upper = appended.T[half:]
    cut = near_ref.shape[0] * 128 // width
    near_ref[...] = pack(upper[:cut]).astype(jnp.bfloat16)
    far_ref[...] = pack(upper[cut:]).astype(jnp.bfloat16)
    for peer in range(n_dp):
        out_ref[peer] = o_lat[peer * share : (peer + 1) * share]


def values_kernel(got_ref, uv_ref, resid_ref, out_ref, wide):
    n_dp = got_ref.shape[0]
    share, latent, vh = uv_ref.shape
    for src in range(n_dp):
        for k in range(latent // 128):
            wide[k, src * share : (src + 1) * share, :] = got_ref[
                src, 0:share, 128 * k : 128 * (k + 1)
            ].astype(jnp.float32)
    piece = resid_ref.shape[1] // n_dp
    for src in range(n_dp):
        out_ref[src : src + 1, share * vh :] = resid_ref[:, src * piece : (src + 1) * piece]
    for head in range(share):
        rows = jnp.concatenate(
            [wide[k, pl.ds(head, n_dp, stride=share), :] for k in range(latent // 128)], axis=1
        ).astype(jnp.bfloat16)
        out_ref[:, head * vh : (head + 1) * vh] = jnp.dot(
            rows, uv_ref[head], preferred_element_type=jnp.float32
        ).astype(jnp.bfloat16)


def interleave(first, second):
    n = first.shape[0]
    row = lax.broadcasted_iota(jnp.int32, (2 * n, 2 * n), 0)
    col = lax.broadcasted_iota(jnp.int32, (2 * n, 2 * n), 1)
    pick = (col == (row % 2) * n + row // 2).astype(jnp.bfloat16)
    both = jnp.concatenate([first, second], axis=0)
    return jnp.dot(pick, both, preferred_element_type=jnp.float32).astype(jnp.bfloat16)


def project_kernel(n_sub, own_ref, peer_ref, w_ref, sum_ref, out_ref, weights, sems):
    requests, half = out_ref.shape
    n_dp = requests // n_sub
    depth = w_ref.shape[0]
    chunks = sems.shape[0]
    wide = half // chunks
    rank, core, _ = place(n_sub)

    def fetch(i):
        start = pl.multiple_of(core * half + i * wide, 128)
        return pltpu.make_async_copy(
            w_ref.at[:, pl.ds(start, wide)], weights.at[i], sems.at[i]
        )

    for i in range(chunks):
        fetch(i).start()
    own = own_ref[:, :depth].astype(jnp.float32)
    peer = peer_ref[:, :depth].astype(jnp.float32)
    first = jnp.where(core == 0, own, peer).astype(jnp.bfloat16)
    second = jnp.where(core == 0, peer, own).astype(jnp.bfloat16)
    values = interleave(first, second)

    def resid_of(ref):
        every = ref[:, depth:].astype(jnp.float32)
        near = jnp.where(core == 0, every[: n_dp // 2], every[n_dp // 2 :])
        return jnp.concatenate([near[i : i + 1] for i in range(n_dp // 2)], axis=1)

    mine = resid_of(own_ref)
    theirs = resid_of(peer_ref)
    row = lax.broadcasted_iota(jnp.int32, (requests, wide), 0)
    for i in range(chunks):
        fetch(i).wait()
        span = slice(i * wide, (i + 1) * wide)
        part = jnp.dot(values, weights[i], preferred_element_type=jnp.float32)
        near = jnp.where(row % n_sub == core, mine[:, span], theirs[:, span])
        part = part + jnp.where(row // n_sub == rank, near, 0.0)
        sum_ref[:, span] = part
        out_ref[:, span] = part.astype(jnp.bfloat16)


def add_kernel(own_ref, peer_ref, sum_ref, send_ref):
    total = own_ref[...] + peer_ref[...].astype(jnp.float32)
    sum_ref[...] = total
    send_ref[...] = total.astype(jnp.bfloat16)


def last_add_kernel(own_ref, peer_ref, out_ref):
    out_ref[...] = (own_ref[...] + peer_ref[...].astype(jnp.float32)).astype(jnp.bfloat16)


def crosses(moves, core, step):
    source, target = moves[core, 1], moves[core, 2]
    bits = {1: (1,), 2: (2, 4), 6: (4,)}[step]
    return sum(source // bit + target // bit for bit in bits) % 2 != 0


def hop_kernel(n_sub, step, moves, kept_ref, come_ref, out_ref):
    _, core, _ = place(n_sub)
    crossing = crosses(moves, core, step)

    @pl.when(crossing)
    def _():
        out_ref[...] = come_ref[...]

    @pl.when(jnp.logical_not(crossing))
    def _():
        out_ref[...] = kept_ref[...]


def finish_kernel(n_sub, steps, moves, near_ref, near_come_ref, far_ref, far_come_ref, out_ref):
    rank, core, _ = place(n_sub)
    width = out_ref.shape[1]
    wanted = rank == moves[core, 2]
    pairs = ((near_ref, near_come_ref), (far_ref, far_come_ref))

    @pl.when(jnp.logical_not(wanted))
    def _():
        out_ref[...] = jnp.zeros_like(out_ref)

    @pl.when(wanted)
    def _():
        for part, (step, (kept_ref, come_ref)) in enumerate(zip(steps, pairs)):
            kept = kept_ref[...].astype(jnp.float32)
            come = come_ref[...].astype(jnp.float32)
            picked = jnp.where(crosses(moves, core, step), come, kept)
            rows = kept_ref.shape[0] * 128 // width
            first = part * (out_ref.shape[0] - rows)
            out_ref[first : first + rows, :] = unpack(picked, rows, width).astype(jnp.bfloat16)


def gate_up_kernel(
    n_sub, own_ref, peer_ref, gain_ref, gate_ref, up_ref, out_ref, base_ref, whole
):
    half = own_ref.shape[1]
    cols = base_ref.shape[1]
    rank, core, _ = place(n_sub)

    own = own_ref[...].astype(jnp.float32)
    peer = peer_ref[...].astype(jnp.float32)
    whole[:, :half] = jnp.where(core == 0, own, peer)
    whole[:, half:] = jnp.where(core == 0, peer, own)
    xf = whole[...]
    inverse = lax.rsqrt(jnp.mean(xf * xf, axis=1, keepdims=True) + 1e-06)
    normed = (xf * inverse * gain_ref[...].astype(jnp.float32).reshape(1, -1)).astype(jnp.bfloat16)
    start = pl.multiple_of(rank * n_sub * cols + core * (cols // 128 * 128), 128)
    near = whole[:, pl.ds(start, cols + 64)]
    base_ref[...] = jnp.where(core == 0, near[:, :cols], near[:, 64:]).astype(jnp.bfloat16)
    gate = lax.dot_general(gate_ref[...], normed, NT, preferred_element_type=jnp.float32)
    up = lax.dot_general(up_ref[...], normed, NT, preferred_element_type=jnp.float32)
    hidden = pack((gate * jax.nn.sigmoid(gate) * up).T).astype(jnp.bfloat16)
    for dst in range(out_ref.shape[0]):
        out_ref[dst] = hidden


def down_kernel(n_sub, own_ref, peer_ref, base_ref, down_ref, out_ref, hidden):
    requests = out_ref.shape[0]
    units = own_ref.shape[1] * 128 // requests
    _, core, _ = place(n_sub)

    for src in range(own_ref.shape[0]):
        own = unpack(own_ref[src].astype(jnp.float32), requests, units)
        peer = unpack(peer_ref[src].astype(jnp.float32), requests, units)
        first = jnp.where(core == 0, own, peer)
        second = jnp.where(core == 0, peer, own)
        hidden[:, src * n_sub * units : (src + 1) * n_sub * units] = jnp.concatenate(
            [first, second], axis=1
        ).astype(jnp.bfloat16)
    down = lax.dot_general(
        down_ref[...], hidden[...], NT, preferred_element_type=jnp.float32
    ).T
    out_ref[...] = (base_ref[...].astype(jnp.float32) + down).astype(jnp.bfloat16)


def swap(x, n_sub):
    return lax.ppermute(x, "sub", [(i, (i + 1) % n_sub) for i in range(n_sub)])


def exchange(x):
    return lax.all_to_all(x, "dp", split_axis=0, concat_axis=0, tiled=True)


def per_device_fast(
    queries, new_latent, cache, lengths, moves, resid, w_uv, w_out, norm_gain, w_gate, w_up, w_down
):
    n_dp = lax.axis_size("dp")
    n_sub = lax.axis_size("sub")
    cap, width = cache.shape[1:]
    heads = queries.shape[1]
    share, latent, vh = w_uv.shape
    half = cap // 2
    dim = w_out.shape[1]
    requests = n_dp * n_sub
    units = w_gate.shape[1]
    cols = w_down.shape[1]
    cut = half * 2//3 // 32 * 32
    scale = (vh + width - latent) ** (-0.5)
    bf16, f32 = jnp.bfloat16, jnp.float32

    positions = pl.pallas_call(
        position_kernel,
        out_shape=jax.ShapeDtypeStruct((8, cap), jnp.int32),
        out_specs=VMEM,
        compiler_params=params(8),
        cost_estimate=cost(40),
        name="positions",
    )()
    kept, sent, near, far = pl.pallas_call(
        functools.partial(attend_kernel, scale, n_dp, n_sub, latent),
        out_shape=(
            jax.ShapeDtypeStruct((width, cap), bf16),
            jax.ShapeDtypeStruct((n_dp, share, latent), bf16),
            jax.ShapeDtypeStruct((cut * width // 128, 128), bf16),
            jax.ShapeDtypeStruct(((half - cut) * width // 128, 128), bf16),
        ),
        in_specs=[SMEM] * 2 + [VMEM] * 4,
        out_specs=(VMEM,) * 4,
        compiler_params=params(8),
        cost_estimate=cost(24),
        name="attend",
    )(lengths, moves, positions, queries[0].T, new_latent, cache[0].T)
    got, near, far = lax.optimization_barrier((exchange(sent), near, far))
    wide_half = dim // n_sub
    values = pl.pallas_call(
        values_kernel,
        out_shape=jax.ShapeDtypeStruct((n_dp, share * vh + dim // n_dp), bf16),
        in_specs=[VMEM] * 3,
        out_specs=VMEM,
        scratch_shapes=[pltpu.VMEM((latent // 128, n_dp * share, 128), f32)],
        compiler_params=params(8),
        cost_estimate=cost(1),
        name="values",
    )(got, w_uv, resid)
    peer_values = swap(values, n_sub)
    def cross(x, step):
        return lax.ppermute(x, "dp", [(i, i ^ step) for i in range(n_dp)])

    def hop(step, here, come):
        return pl.pallas_call(
            functools.partial(hop_kernel, n_sub, step),
            out_shape=jax.ShapeDtypeStruct(here.shape, bf16),
            in_specs=[SMEM, VMEM, VMEM],
            out_specs=VMEM,
            compiler_params=params(8),
            cost_estimate=cost(1),
            name="hop",
        )(moves, here, come)

    def add(total, come):
        return pl.pallas_call(
            add_kernel,
            out_shape=(
                jax.ShapeDtypeStruct((requests, wide_half), f32),
                jax.ShapeDtypeStruct((requests, wide_half), bf16),
            ),
            in_specs=[VMEM] * 2,
            out_specs=(VMEM, VMEM),
            compiler_params=params(8),
            cost_estimate=cost(1),
            name="add",
        )(total, come)

    near_come = cross(near, 6)
    far_come = cross(far, 2)
    total, part = pl.pallas_call(
        functools.partial(project_kernel, n_sub),
        out_shape=(
            jax.ShapeDtypeStruct((requests, wide_half), f32),
            jax.ShapeDtypeStruct((requests, wide_half), bf16),
        ),
        in_specs=[VMEM, VMEM, HBM],
        out_specs=(VMEM, VMEM),
        scratch_shapes=[
            pltpu.VMEM((4, share * vh, wide_half // 4), bf16),
            pltpu.SemaphoreType.DMA((4,)),
        ],
        compiler_params=params(38),
        cost_estimate=cost(24),
        name="project",
    )(values, peer_values, w_out)
    near_come, far_come, part = lax.optimization_barrier((near_come, far_come, part))
    near = hop(6, near, near_come)
    far = hop(2, far, far_come)
    near_come = cross(near, 2)
    total, part = add(total, cross(part, 1))
    far, part = lax.optimization_barrier((far, part))
    near = hop(2, near, near_come)
    near_come = cross(near, 1)
    far_come = cross(far, 1)
    total, part = add(total, cross(part, 2))
    far = hop(1, far, far_come)
    come, near_come, far = lax.optimization_barrier((cross(part, 6), near_come, far))
    x_half = pl.pallas_call(
        last_add_kernel,
        out_shape=jax.ShapeDtypeStruct((requests, wide_half), bf16),
        in_specs=[VMEM] * 2,
        out_specs=VMEM,
        compiler_params=params(8),
        cost_estimate=cost(1),
        name="last_add",
    )(total, come)
    far_come = cross(far, 6)
    hidden, base = pl.pallas_call(
        functools.partial(gate_up_kernel, n_sub),
        out_shape=(
            jax.ShapeDtypeStruct((n_dp, requests * units // 128, 128), bf16),
            jax.ShapeDtypeStruct((requests, cols), bf16),
        ),
        in_specs=[VMEM] * 5,
        out_specs=(VMEM, VMEM),
        scratch_shapes=[pltpu.VMEM((requests, dim), f32)],
        compiler_params=params(24),
        cost_estimate=cost(24),
        name="gate_up",
    )(x_half, swap(x_half, n_sub), norm_gain, w_gate.T, w_up.T)
    hidden, far_come = lax.optimization_barrier((hidden, far_come))
    every = exchange(hidden)
    mixed = pl.pallas_call(
        functools.partial(down_kernel, n_sub),
        out_shape=jax.ShapeDtypeStruct((requests, cols), bf16),
        in_specs=[VMEM] * 4,
        out_specs=VMEM,
        scratch_shapes=[pltpu.VMEM((requests, n_dp * n_sub * units), bf16)],
        compiler_params=params(16),
        cost_estimate=cost(1),
        name="down",
    )(every, swap(every, n_sub), base, w_down.T)
    spare = pl.pallas_call(
        functools.partial(finish_kernel, n_sub, (1, 6)),
        out_shape=jax.ShapeDtypeStruct((half, width), bf16),
        in_specs=[SMEM] + [VMEM] * 4,
        out_specs=VMEM,
        compiler_params=params(8),
        cost_estimate=cost(1),
        name="finish",
    )(moves, near, near_come, far, far_come)
    return (kept.T[None], spare[None], mixed)


def per_device(*args):
    queries, cache, moves, w_uv, w_out = args[0], args[2], args[4], args[6], args[7]
    w_gate, w_down = args[9], args[11]
    n_dp = lax.axis_size("dp")
    n_sub = lax.axis_size("sub")
    fits = (
        n_sub == 2
        and n_dp == 8
        and moves.shape[0] == n_sub
        and cache.shape[1] % 128 == 0
        and queries.shape[1] // n_dp == 16
        and w_uv.shape[1] == 512
        and w_out.shape[1] % (n_sub * 4 * 128) == 0
        and w_gate.shape[1] % 128 == 64
        and cache.shape[2] % 128 == 64
        and w_down.shape[1] % 64 == 0
    )
    return per_device_fast(*args) if fits else per_device_any(*args)


def solution(mesh):
    return jax.shard_map(
        per_device,
        mesh=mesh,
        in_specs=(
            P(("groups", "dp", "sub"), None, None),
            P(("groups", "dp", "sub"), None),
            P(("groups", "dp", "sub"), None, None),
            P("groups"),
            P("groups", None),
            P(("groups", "dp", "sub"), None),
            P("dp", None, None),
            P("dp", None),
            P(),
            P(None, ("dp", "sub")),
            P(None, ("dp", "sub")),
            P(None, ("dp", "sub")),
        ),
        out_specs=(
            P(("groups", "dp", "sub"), None, None),
            P(("groups", "dp", "sub"), None, None),
            P("groups", ("dp", "sub")),
        ),
        check_vma=False,
    )
```

```python
import functools

import jax
import jax.numpy as jnp
from jax import lax
from jax.experimental import pallas as pl
from jax.experimental.pallas import tpu as pltpu
from jax.sharding import PartitionSpec as P


def partial_attend(query, keys, live, scale, latent):
    scores = jnp.einsum("hw,pw->hp", query, keys, preferred_element_type=jnp.float32) * scale
    scores = jnp.where(live[None, :], scores, -1e30)
    top = jnp.max(scores, axis=1)
    weights = jnp.where(live[None, :], jnp.exp(scores - top[:, None]), 0.0)
    total = jnp.sum(weights, axis=1)
    acc = jnp.dot(
        weights.astype(jnp.bfloat16), keys[:, :latent], preferred_element_type=jnp.float32
    )
    return (top, total, acc)


def route(spread, partner, present):
    shape = (spread.shape[0],) + (1,) * (spread.ndim - 1)
    picked = jnp.take(spread, partner, axis=0)
    return jnp.where(present.reshape(shape), picked, jnp.zeros((), spread.dtype))


def per_device_any(
    queries, new_latent, cache, lengths, moves, resid, w_uv, w_out, norm_gain, w_gate, w_up, w_down
):
    n_dp = lax.axis_size("dp")
    n_sub = lax.axis_size("sub")
    rank = lax.axis_index("dp")
    core = lax.axis_index("sub")
    device = rank * n_sub + core
    cap = cache.shape[1]
    half = cap // 2
    width = cache.shape[2]
    heads = queries.shape[1]
    latent = w_uv.shape[1]
    scale = (w_uv.shape[2] + width - latent) ** (-0.5)
    length = lax.dynamic_index_in_dim(lengths, device, 0, keepdims=False)
    positions = jnp.arange(cap, dtype=jnp.int32)
    appended = jnp.where((positions == length)[:, None], new_latent[0][None, :], cache[0])
    moved_req = moves[:, 0]
    sources = moves[:, 1]
    targets = moves[:, 2]
    same_core = moved_req % n_sub == core
    sending = jnp.any(moved_req == device)
    peers = jnp.arange(n_dp, dtype=jnp.int32)
    to_match = same_core[None, :] & (peers[:, None] == targets[None, :])
    from_of = jnp.sum(jnp.where(to_match, sources[None, :], 0), axis=1)
    to_has = jnp.any(to_match, axis=1)
    zero_bf = jnp.zeros((), jnp.bfloat16)
    upper = jnp.where(sending, appended[half:], zero_bf).reshape(n_dp, -1)
    spread = lax.all_to_all(upper, "dp", split_axis=0, concat_axis=0, tiled=True)
    landed = lax.all_to_all(
        route(spread, from_of, to_has), "dp", split_axis=0, concat_axis=0, tiled=True
    )
    spare = landed.reshape(half, width)
    kept = jnp.where(sending & (positions >= half)[:, None], zero_bf, appended)
    top, total, acc = partial_attend(queries[0], appended, positions <= length, scale, latent)
    o_lat = (acc / total[:, None]).astype(jnp.bfloat16)
    owners = lax.all_to_all(
        o_lat.reshape(n_dp, heads // n_dp, latent), "dp", split_axis=0, concat_axis=0, tiled=True
    )
    values = jnp.einsum("rhl,hlv->rhv", owners, w_uv, preferred_element_type=jnp.float32).astype(
        jnp.bfloat16
    )
    values = values.reshape(n_dp, -1)
    cols = w_down.shape[1]
    units = w_gate.shape[1]
    col_start = device * cols
    gain = norm_gain.astype(jnp.float32)
    summed = lax.psum_scatter(
        jnp.dot(values, w_out, preferred_element_type=jnp.float32),
        "dp",
        scatter_dimension=0,
        tiled=True,
    )
    x_rows = (resid.astype(jnp.float32) + summed).astype(jnp.bfloat16)
    piece = lax.all_gather(x_rows, ("dp", "sub"), axis=0, tiled=True)
    xf = piece.astype(jnp.float32)
    normed = (xf * lax.rsqrt(jnp.mean(xf * xf, axis=1, keepdims=True) + 1e-06) * gain).astype(
        jnp.bfloat16
    )
    gate = jnp.dot(normed, w_gate, preferred_element_type=jnp.float32)
    up_part = jnp.dot(normed, w_up, preferred_element_type=jnp.float32)
    hidden_part = (jax.nn.silu(gate) * up_part).astype(jnp.bfloat16)
    own_cols = lax.dynamic_slice_in_dim(piece, col_start, cols, 1)
    joined = jnp.concatenate([hidden_part, own_cols], axis=1)
    hidden = joined[:, :units]
    base = joined[:, units:]
    down = jnp.dot(
        lax.all_gather(hidden, ("dp", "sub"), axis=1, tiled=True),
        w_down,
        preferred_element_type=jnp.float32,
    )
    mixed = (base.astype(jnp.float32) + down).astype(jnp.bfloat16)
    return (kept[None], spare[None], mixed)


VMEM = pl.BlockSpec(memory_space=pltpu.VMEM)
SMEM = pl.BlockSpec(memory_space=pltpu.SMEM)
HBM = pl.BlockSpec(memory_space=pl.ANY)
NT = (((1,), (1,)), ((), ()))
TN = (((0,), (0,)), ((), ()))


def cost(mib):
    return pl.CostEstimate(flops=300 * (mib << 20), bytes_accessed=mib << 20, transcendentals=0)


def params(mib):
    return pltpu.CompilerParams(vmem_limit_bytes=mib << 20)


def place(n_sub):
    rank = lax.axis_index("dp")
    core = lax.axis_index("sub")
    return rank, core, rank * n_sub + core


def position_kernel(out_ref):
    out_ref[...] = lax.broadcasted_iota(jnp.int32, out_ref.shape, 1)


def pack(x):
    rows, width = x.shape
    whole = width // 128 * 128
    pieces = [x[:, i : i + 128] for i in range(0, whole, 128)]
    rest = jnp.concatenate([x[: rows // 2, whole:], x[rows // 2 :, whole:]], axis=1)
    return jnp.concatenate(pieces + [rest], axis=0)


def unpack(x, rows, width):
    whole = width // 128 * 128
    pieces = [x[rows * i : rows * (i + 1)] for i in range(whole // 128)]
    rest = x[rows * (whole // 128) :]
    tail = jnp.concatenate([rest[:, : width - whole], rest[:, width - whole :]], axis=0)
    return jnp.concatenate(pieces + [tail], axis=1)


def attend_kernel(
    scale, n_dp, n_sub, latent, lengths, moves, at_ref, q_ref, fresh_ref, cache_ref, kept_ref, out_ref, near_ref, far_ref
):
    width, cap = cache_ref.shape
    half = cap // 2
    heads = q_ref.shape[1]
    _, _, device = place(n_sub)
    length = lengths[device]
    sending = moves[0, 0] == device
    for row in range(1, moves.shape[0]):
        sending = sending | (moves[row, 0] == device)
    fresh = jnp.broadcast_to(fresh_ref[...].astype(jnp.float32), (128, width)).T
    fresh = jnp.concatenate([fresh] * (cap // 128), axis=1)
    positions = at_ref[...]
    positions = jnp.concatenate([positions] * (width // positions.shape[0]), axis=0)
    appended = jnp.where(positions == length, fresh, cache_ref[...].astype(jnp.float32))
    drop = jnp.where(sending, half, cap)
    kept_ref[...] = jnp.where(positions >= drop, 0.0, appended).astype(jnp.bfloat16)
    keys = appended.astype(jnp.bfloat16)
    scores = lax.dot_general(q_ref[...], keys, TN, preferred_element_type=jnp.float32) * scale
    live = positions[:heads] <= length
    scores = jnp.where(live, scores, -1e30)
    top = jnp.max(scores, axis=1, keepdims=True)
    weights = jnp.where(live, jnp.exp(scores - top), 0.0)
    total = jnp.sum(weights, axis=1, keepdims=True)
    acc = lax.dot_general(
        weights.astype(jnp.bfloat16), keys[:latent], NT, preferred_element_type=jnp.float32
    )
    o_lat = (acc / total).astype(jnp.bfloat16)
    share = heads // n_dp
    upper = appended.T[half:]
    cut = near_ref.shape[0] * 128 // width
    near_ref[...] = pack(upper[:cut]).astype(jnp.bfloat16)
    far_ref[...] = pack(upper[cut:]).astype(jnp.bfloat16)
    for peer in range(n_dp):
        out_ref[peer] = o_lat[peer * share : (peer + 1) * share]


def values_kernel(got_ref, uv_ref, resid_ref, out_ref, wide):
    n_dp = got_ref.shape[0]
    share, latent, vh = uv_ref.shape
    for src in range(n_dp):
        for k in range(latent // 128):
            wide[k, src * share : (src + 1) * share, :] = got_ref[
                src, 0:share, 128 * k : 128 * (k + 1)
            ].astype(jnp.float32)
    piece = resid_ref.shape[1] // n_dp
    row = resid_ref[...].astype(jnp.float32)
    out_ref[:, share * vh :] = jnp.concatenate(
        [row[:, src * piece : (src + 1) * piece] for src in range(n_dp)], axis=0
    ).astype(jnp.bfloat16)
    for head in range(share):
        rows = jnp.concatenate(
            [wide[k, pl.ds(head, n_dp, stride=share), :] for k in range(latent // 128)], axis=1
        ).astype(jnp.bfloat16)
        out_ref[:, head * vh : (head + 1) * vh] = jnp.dot(
            rows, uv_ref[head], preferred_element_type=jnp.float32
        ).astype(jnp.bfloat16)


def interleave(first, second):
    n = first.shape[0]
    row = lax.broadcasted_iota(jnp.int32, (2 * n, 2 * n), 0)
    col = lax.broadcasted_iota(jnp.int32, (2 * n, 2 * n), 1)
    pick = (col == (row % 2) * n + row // 2).astype(jnp.bfloat16)
    both = jnp.concatenate([first, second], axis=0)
    return jnp.dot(pick, both, preferred_element_type=jnp.float32).astype(jnp.bfloat16)


def project_kernel(n_sub, own_ref, peer_ref, w_ref, sum_ref, out_ref, weights, sems):
    requests, half = out_ref.shape
    n_dp = requests // n_sub
    depth = w_ref.shape[0]
    chunks = sems.shape[0]
    wide = half // chunks
    rank, core, _ = place(n_sub)

    def fetch(i):
        start = pl.multiple_of(core * half + i * wide, 128)
        return pltpu.make_async_copy(
            w_ref.at[:, pl.ds(start, wide)], weights.at[i], sems.at[i]
        )

    for i in range(chunks):
        fetch(i).start()
    own = own_ref[:, :depth].astype(jnp.float32)
    peer = peer_ref[:, :depth].astype(jnp.float32)
    first = jnp.where(core == 0, own, peer).astype(jnp.bfloat16)
    second = jnp.where(core == 0, peer, own).astype(jnp.bfloat16)
    values = interleave(first, second)

    def resid_of(ref):
        every = ref[:, depth:].astype(jnp.float32)
        near = jnp.where(core == 0, every[: n_dp // 2], every[n_dp // 2 :])
        return jnp.concatenate([near[i : i + 1] for i in range(n_dp // 2)], axis=1)

    mine = resid_of(own_ref)
    theirs = resid_of(peer_ref)
    row = lax.broadcasted_iota(jnp.int32, (requests, wide), 0)
    for i in range(chunks):
        fetch(i).wait()
        span = slice(i * wide, (i + 1) * wide)
        part = jnp.dot(values, weights[i], preferred_element_type=jnp.float32)
        near = jnp.where(row % n_sub == core, mine[:, span], theirs[:, span])
        part = part + jnp.where(row // n_sub == rank, near, 0.0)
        sum_ref[:, span] = part
        out_ref[:, span] = part.astype(jnp.bfloat16)


def add_kernel(own_ref, peer_ref, sum_ref, send_ref):
    total = own_ref[...] + peer_ref[...].astype(jnp.float32)
    sum_ref[...] = total
    send_ref[...] = total.astype(jnp.bfloat16)


def last_add_kernel(own_ref, peer_ref, out_ref):
    out_ref[...] = (own_ref[...] + peer_ref[...].astype(jnp.float32)).astype(jnp.bfloat16)


def crosses(moves, core, step):
    source, target = moves[core, 1], moves[core, 2]
    bits = {1: (1,), 2: (2, 4), 6: (4,)}[step]
    return sum(source // bit + target // bit for bit in bits) % 2 != 0


def hop_kernel(n_sub, step, moves, kept_ref, come_ref, out_ref):
    _, core, _ = place(n_sub)
    crossing = crosses(moves, core, step)

    @pl.when(crossing)
    def _():
        out_ref[...] = come_ref[...]

    @pl.when(jnp.logical_not(crossing))
    def _():
        out_ref[...] = kept_ref[...]


def finish_kernel(n_sub, steps, moves, near_ref, near_come_ref, far_ref, far_come_ref, out_ref):
    rank, core, _ = place(n_sub)
    width = out_ref.shape[1]
    wanted = rank == moves[core, 2]
    pairs = ((near_ref, near_come_ref), (far_ref, far_come_ref))

    @pl.when(jnp.logical_not(wanted))
    def _():
        out_ref[...] = jnp.zeros_like(out_ref)

    @pl.when(wanted)
    def _():
        for part, (step, (kept_ref, come_ref)) in enumerate(zip(steps, pairs)):
            kept = kept_ref[...].astype(jnp.float32)
            come = come_ref[...].astype(jnp.float32)
            picked = jnp.where(crosses(moves, core, step), come, kept)
            rows = kept_ref.shape[0] * 128 // width
            first = part * (out_ref.shape[0] - rows)
            out_ref[first : first + rows, :] = unpack(picked, rows, width).astype(jnp.bfloat16)


def gate_up_kernel(
    n_sub, own_ref, peer_ref, gain_ref, gate_ref, up_ref, out_ref, base_ref, whole
):
    half = own_ref.shape[1]
    cols = base_ref.shape[1]
    rank, core, _ = place(n_sub)

    own = own_ref[...].astype(jnp.float32)
    peer = peer_ref[...].astype(jnp.float32)
    whole[:, :half] = jnp.where(core == 0, own, peer)
    whole[:, half:] = jnp.where(core == 0, peer, own)
    xf = whole[...]
    inverse = lax.rsqrt(jnp.mean(xf * xf, axis=1, keepdims=True) + 1e-06)
    normed = (xf * inverse * gain_ref[...].astype(jnp.float32).reshape(1, -1)).astype(jnp.bfloat16)
    start = pl.multiple_of(rank * n_sub * cols + core * (cols // 128 * 128), 128)
    near = whole[:, pl.ds(start, cols + 64)]
    base_ref[...] = jnp.where(core == 0, near[:, :cols], near[:, 64:]).astype(jnp.bfloat16)
    gate = lax.dot_general(gate_ref[...], normed, NT, preferred_element_type=jnp.float32)
    up = lax.dot_general(up_ref[...], normed, NT, preferred_element_type=jnp.float32)
    hidden = pack((gate * jax.nn.sigmoid(gate) * up).T).astype(jnp.bfloat16)
    for dst in range(out_ref.shape[0]):
        out_ref[dst] = hidden


def down_kernel(n_sub, own_ref, peer_ref, base_ref, down_ref, out_ref, hidden):
    requests = out_ref.shape[0]
    units = own_ref.shape[1] * 128 // requests
    _, core, _ = place(n_sub)

    for src in range(own_ref.shape[0]):
        own = unpack(own_ref[src].astype(jnp.float32), requests, units)
        peer = unpack(peer_ref[src].astype(jnp.float32), requests, units)
        first = jnp.where(core == 0, own, peer)
        second = jnp.where(core == 0, peer, own)
        hidden[:, src * n_sub * units : (src + 1) * n_sub * units] = jnp.concatenate(
            [first, second], axis=1
        ).astype(jnp.bfloat16)
    down = lax.dot_general(
        down_ref[...], hidden[...], NT, preferred_element_type=jnp.float32
    ).T
    out_ref[...] = (base_ref[...].astype(jnp.float32) + down).astype(jnp.bfloat16)


def swap(x, n_sub):
    return lax.ppermute(x, "sub", [(i, (i + 1) % n_sub) for i in range(n_sub)])


def exchange(x):
    return lax.all_to_all(x, "dp", split_axis=0, concat_axis=0, tiled=True)


def per_device_fast(
    queries, new_latent, cache, lengths, moves, resid, w_uv, w_out, norm_gain, w_gate, w_up, w_down
):
    n_dp = lax.axis_size("dp")
    n_sub = lax.axis_size("sub")
    cap, width = cache.shape[1:]
    heads = queries.shape[1]
    share, latent, vh = w_uv.shape
    half = cap // 2
    dim = w_out.shape[1]
    requests = n_dp * n_sub
    units = w_gate.shape[1]
    cols = w_down.shape[1]
    cut = half * 2//3 // 32 * 32
    scale = (vh + width - latent) ** (-0.5)
    bf16, f32 = jnp.bfloat16, jnp.float32

    positions = pl.pallas_call(
        position_kernel,
        out_shape=jax.ShapeDtypeStruct((8, cap), jnp.int32),
        out_specs=VMEM,
        compiler_params=params(8),
        cost_estimate=cost(40),
        name="positions",
    )()
    kept, sent, near, far = pl.pallas_call(
        functools.partial(attend_kernel, scale, n_dp, n_sub, latent),
        out_shape=(
            jax.ShapeDtypeStruct((width, cap), bf16),
            jax.ShapeDtypeStruct((n_dp, share, latent), bf16),
            jax.ShapeDtypeStruct((cut * width // 128, 128), bf16),
            jax.ShapeDtypeStruct(((half - cut) * width // 128, 128), bf16),
        ),
        in_specs=[SMEM] * 2 + [VMEM] * 4,
        out_specs=(VMEM,) * 4,
        compiler_params=params(8),
        cost_estimate=cost(24),
        name="attend",
    )(lengths, moves, positions, queries[0].T, new_latent, cache[0].T)
    got, near, far = lax.optimization_barrier((exchange(sent), near, far))
    wide_half = dim // n_sub
    values = pl.pallas_call(
        values_kernel,
        out_shape=jax.ShapeDtypeStruct((n_dp, share * vh + dim // n_dp), bf16),
        in_specs=[VMEM] * 3,
        out_specs=VMEM,
        scratch_shapes=[pltpu.VMEM((latent // 128, n_dp * share, 128), f32)],
        compiler_params=params(8),
        cost_estimate=cost(1),
        name="values",
    )(got, w_uv, resid)
    peer_values = swap(values, n_sub)
    def cross(x, step):
        return lax.ppermute(x, "dp", [(i, i ^ step) for i in range(n_dp)])

    def hop(step, here, come):
        return pl.pallas_call(
            functools.partial(hop_kernel, n_sub, step),
            out_shape=jax.ShapeDtypeStruct(here.shape, bf16),
            in_specs=[SMEM, VMEM, VMEM],
            out_specs=VMEM,
            compiler_params=params(8),
            cost_estimate=cost(1),
            name="hop",
        )(moves, here, come)

    def add(total, come):
        return pl.pallas_call(
            add_kernel,
            out_shape=(
                jax.ShapeDtypeStruct((requests, wide_half), f32),
                jax.ShapeDtypeStruct((requests, wide_half), bf16),
            ),
            in_specs=[VMEM] * 2,
            out_specs=(VMEM, VMEM),
            compiler_params=params(8),
            cost_estimate=cost(1),
            name="add",
        )(total, come)

    near_come = cross(near, 6)
    far_come = cross(far, 2)
    total, part = pl.pallas_call(
        functools.partial(project_kernel, n_sub),
        out_shape=(
            jax.ShapeDtypeStruct((requests, wide_half), f32),
            jax.ShapeDtypeStruct((requests, wide_half), bf16),
        ),
        in_specs=[VMEM, VMEM, HBM],
        out_specs=(VMEM, VMEM),
        scratch_shapes=[
            pltpu.VMEM((4, share * vh, wide_half // 4), bf16),
            pltpu.SemaphoreType.DMA((4,)),
        ],
        compiler_params=params(38),
        cost_estimate=cost(24),
        name="project",
    )(values, peer_values, w_out)
    near_come, far_come, part = lax.optimization_barrier((near_come, far_come, part))
    near = hop(6, near, near_come)
    far = hop(2, far, far_come)
    near_come = cross(near, 2)
    total, part = add(total, cross(part, 1))
    far, part = lax.optimization_barrier((far, part))
    near = hop(2, near, near_come)
    near_come = cross(near, 1)
    far_come = cross(far, 1)
    total, part = add(total, cross(part, 2))
    far = hop(1, far, far_come)
    come, near_come, far = lax.optimization_barrier((cross(part, 6), near_come, far))
    x_half = pl.pallas_call(
        last_add_kernel,
        out_shape=jax.ShapeDtypeStruct((requests, wide_half), bf16),
        in_specs=[VMEM] * 2,
        out_specs=VMEM,
        compiler_params=params(8),
        cost_estimate=cost(1),
        name="last_add",
    )(total, come)
    far_come = cross(far, 6)
    hidden, base = pl.pallas_call(
        functools.partial(gate_up_kernel, n_sub),
        out_shape=(
            jax.ShapeDtypeStruct((n_dp, requests * units // 128, 128), bf16),
            jax.ShapeDtypeStruct((requests, cols), bf16),
        ),
        in_specs=[VMEM] * 5,
        out_specs=(VMEM, VMEM),
        scratch_shapes=[pltpu.VMEM((requests, dim), f32)],
        compiler_params=params(24),
        cost_estimate=cost(24),
        name="gate_up",
    )(x_half, swap(x_half, n_sub), norm_gain, w_gate.T, w_up.T)
    hidden, far_come = lax.optimization_barrier((hidden, far_come))
    every = exchange(hidden)
    mixed = pl.pallas_call(
        functools.partial(down_kernel, n_sub),
        out_shape=jax.ShapeDtypeStruct((requests, cols), bf16),
        in_specs=[VMEM] * 4,
        out_specs=VMEM,
        scratch_shapes=[pltpu.VMEM((requests, n_dp * n_sub * units), bf16)],
        compiler_params=params(16),
        cost_estimate=cost(1),
        name="down",
    )(every, swap(every, n_sub), base, w_down.T)
    spare = pl.pallas_call(
        functools.partial(finish_kernel, n_sub, (1, 6)),
        out_shape=jax.ShapeDtypeStruct((half, width), bf16),
        in_specs=[SMEM] + [VMEM] * 4,
        out_specs=VMEM,
        compiler_params=params(8),
        cost_estimate=cost(1),
        name="finish",
    )(moves, near, near_come, far, far_come)
    return (kept.T[None], spare[None], mixed)


def per_device(*args):
    queries, cache, moves, w_uv, w_out = args[0], args[2], args[4], args[6], args[7]
    w_gate, w_down = args[9], args[11]
    n_dp = lax.axis_size("dp")
    n_sub = lax.axis_size("sub")
    fits = (
        n_sub == 2
        and n_dp == 8
        and moves.shape[0] == n_sub
        and cache.shape[1] % 128 == 0
        and queries.shape[1] // n_dp == 16
        and w_uv.shape[1] == 512
        and w_out.shape[1] % (n_sub * 4 * 128) == 0
        and w_gate.shape[1] % 128 == 64
        and cache.shape[2] % 128 == 64
        and w_down.shape[1] % 64 == 0
    )
    return per_device_fast(*args) if fits else per_device_any(*args)


def solution(mesh):
    return jax.shard_map(
        per_device,
        mesh=mesh,
        in_specs=(
            P(("groups", "dp", "sub"), None, None),
            P(("groups", "dp", "sub"), None),
            P(("groups", "dp", "sub"), None, None),
            P("groups"),
            P("groups", None),
            P(("groups", "dp", "sub"), None),
            P("dp", None, None),
            P("dp", None),
            P(),
            P(None, ("dp", "sub")),
            P(None, ("dp", "sub")),
            P(None, ("dp", "sub")),
        ),
        out_specs=(
            P(("groups", "dp", "sub"), None, None),
            P(("groups", "dp", "sub"), None, None),
            P("groups", ("dp", "sub")),
        ),
        check_vma=False,
    )
```

```python
import functools

import jax
import jax.numpy as jnp
from jax import lax
from jax.experimental import pallas as pl
from jax.experimental.pallas import tpu as pltpu
from jax.sharding import PartitionSpec as P


def partial_attend(query, keys, live, scale, latent):
    scores = jnp.einsum("hw,pw->hp", query, keys, preferred_element_type=jnp.float32) * scale
    scores = jnp.where(live[None, :], scores, -1e30)
    top = jnp.max(scores, axis=1)
    weights = jnp.where(live[None, :], jnp.exp(scores - top[:, None]), 0.0)
    total = jnp.sum(weights, axis=1)
    acc = jnp.dot(
        weights.astype(jnp.bfloat16), keys[:, :latent], preferred_element_type=jnp.float32
    )
    return (top, total, acc)


def route(spread, partner, present):
    shape = (spread.shape[0],) + (1,) * (spread.ndim - 1)
    picked = jnp.take(spread, partner, axis=0)
    return jnp.where(present.reshape(shape), picked, jnp.zeros((), spread.dtype))


def per_device_any(
    queries, new_latent, cache, lengths, moves, resid, w_uv, w_out, norm_gain, w_gate, w_up, w_down
):
    n_dp = lax.axis_size("dp")
    n_sub = lax.axis_size("sub")
    rank = lax.axis_index("dp")
    core = lax.axis_index("sub")
    device = rank * n_sub + core
    cap = cache.shape[1]
    half = cap // 2
    width = cache.shape[2]
    heads = queries.shape[1]
    latent = w_uv.shape[1]
    scale = (w_uv.shape[2] + width - latent) ** (-0.5)
    length = lax.dynamic_index_in_dim(lengths, device, 0, keepdims=False)
    positions = jnp.arange(cap, dtype=jnp.int32)
    appended = jnp.where((positions == length)[:, None], new_latent[0][None, :], cache[0])
    moved_req = moves[:, 0]
    sources = moves[:, 1]
    targets = moves[:, 2]
    same_core = moved_req % n_sub == core
    sending = jnp.any(moved_req == device)
    peers = jnp.arange(n_dp, dtype=jnp.int32)
    to_match = same_core[None, :] & (peers[:, None] == targets[None, :])
    from_of = jnp.sum(jnp.where(to_match, sources[None, :], 0), axis=1)
    to_has = jnp.any(to_match, axis=1)
    zero_bf = jnp.zeros((), jnp.bfloat16)
    upper = jnp.where(sending, appended[half:], zero_bf).reshape(n_dp, -1)
    spread = lax.all_to_all(upper, "dp", split_axis=0, concat_axis=0, tiled=True)
    landed = lax.all_to_all(
        route(spread, from_of, to_has), "dp", split_axis=0, concat_axis=0, tiled=True
    )
    spare = landed.reshape(half, width)
    kept = jnp.where(sending & (positions >= half)[:, None], zero_bf, appended)
    top, total, acc = partial_attend(queries[0], appended, positions <= length, scale, latent)
    o_lat = (acc / total[:, None]).astype(jnp.bfloat16)
    owners = lax.all_to_all(
        o_lat.reshape(n_dp, heads // n_dp, latent), "dp", split_axis=0, concat_axis=0, tiled=True
    )
    values = jnp.einsum("rhl,hlv->rhv", owners, w_uv, preferred_element_type=jnp.float32).astype(
        jnp.bfloat16
    )
    values = values.reshape(n_dp, -1)
    cols = w_down.shape[1]
    units = w_gate.shape[1]
    col_start = device * cols
    gain = norm_gain.astype(jnp.float32)
    summed = lax.psum_scatter(
        jnp.dot(values, w_out, preferred_element_type=jnp.float32),
        "dp",
        scatter_dimension=0,
        tiled=True,
    )
    x_rows = (resid.astype(jnp.float32) + summed).astype(jnp.bfloat16)
    piece = lax.all_gather(x_rows, ("dp", "sub"), axis=0, tiled=True)
    xf = piece.astype(jnp.float32)
    normed = (xf * lax.rsqrt(jnp.mean(xf * xf, axis=1, keepdims=True) + 1e-06) * gain).astype(
        jnp.bfloat16
    )
    gate = jnp.dot(normed, w_gate, preferred_element_type=jnp.float32)
    up_part = jnp.dot(normed, w_up, preferred_element_type=jnp.float32)
    hidden_part = (jax.nn.silu(gate) * up_part).astype(jnp.bfloat16)
    own_cols = lax.dynamic_slice_in_dim(piece, col_start, cols, 1)
    joined = jnp.concatenate([hidden_part, own_cols], axis=1)
    hidden = joined[:, :units]
    base = joined[:, units:]
    down = jnp.dot(
        lax.all_gather(hidden, ("dp", "sub"), axis=1, tiled=True),
        w_down,
        preferred_element_type=jnp.float32,
    )
    mixed = (base.astype(jnp.float32) + down).astype(jnp.bfloat16)
    return (kept[None], spare[None], mixed)


VMEM = pl.BlockSpec(memory_space=pltpu.VMEM)
SMEM = pl.BlockSpec(memory_space=pltpu.SMEM)
HBM = pl.BlockSpec(memory_space=pl.ANY)
NT = (((1,), (1,)), ((), ()))
TN = (((0,), (0,)), ((), ()))


def cost(mib):
    return pl.CostEstimate(flops=300 * (mib << 20), bytes_accessed=mib << 20, transcendentals=0)


def params(mib):
    return pltpu.CompilerParams(vmem_limit_bytes=mib << 20)


def place(n_sub):
    rank = lax.axis_index("dp")
    core = lax.axis_index("sub")
    return rank, core, rank * n_sub + core


def position_kernel(out_ref):
    out_ref[...] = lax.broadcasted_iota(jnp.int32, out_ref.shape, 1)


def pack(x):
    rows, width = x.shape
    whole = width // 128 * 128
    pieces = [x[:, i : i + 128] for i in range(0, whole, 128)]
    rest = jnp.concatenate([x[: rows // 2, whole:], x[rows // 2 :, whole:]], axis=1)
    return jnp.concatenate(pieces + [rest], axis=0)


def unpack(x, rows, width):
    whole = width // 128 * 128
    pieces = [x[rows * i : rows * (i + 1)] for i in range(whole // 128)]
    rest = x[rows * (whole // 128) :]
    tail = jnp.concatenate([rest[:, : width - whole], rest[:, width - whole :]], axis=0)
    return jnp.concatenate(pieces + [tail], axis=1)


def attend_kernel(
    scale, n_dp, n_sub, latent, lengths, moves, at_ref, q_ref, fresh_ref, cache_ref, kept_ref, out_ref, near_ref, far_ref
):
    width, cap = cache_ref.shape
    half = cap // 2
    heads = q_ref.shape[1]
    _, _, device = place(n_sub)
    length = lengths[device]
    sending = moves[0, 0] == device
    for row in range(1, moves.shape[0]):
        sending = sending | (moves[row, 0] == device)
    fresh = jnp.broadcast_to(fresh_ref[...].astype(jnp.float32), (128, width)).T
    fresh = jnp.concatenate([fresh] * (cap // 128), axis=1)
    positions = at_ref[...]
    positions = jnp.concatenate([positions] * (width // positions.shape[0]), axis=0)
    appended = jnp.where(positions == length, fresh, cache_ref[...].astype(jnp.float32))
    drop = jnp.where(sending, half, cap)
    kept_ref[...] = jnp.where(positions >= drop, 0.0, appended).astype(jnp.bfloat16)
    keys = appended.astype(jnp.bfloat16)
    scores = lax.dot_general(q_ref[...], keys, TN, preferred_element_type=jnp.float32) * scale
    live = positions[:heads] <= length
    scores = jnp.where(live, scores, -1e30)
    top = jnp.max(scores, axis=1, keepdims=True)
    weights = jnp.where(live, jnp.exp(scores - top), 0.0)
    total = jnp.sum(weights, axis=1, keepdims=True)
    acc = lax.dot_general(
        weights.astype(jnp.bfloat16), keys[:latent], NT, preferred_element_type=jnp.float32
    )
    o_lat = (acc / total).astype(jnp.bfloat16)
    share = heads // n_dp
    low = half // 128 * 128
    upper = appended[:, low:].T[half - low :]
    cut = near_ref.shape[0] * 128 // width
    near_ref[...] = pack(upper[:cut]).astype(jnp.bfloat16)
    far_ref[...] = pack(upper[cut:]).astype(jnp.bfloat16)
    for peer in range(n_dp):
        out_ref[peer] = o_lat[peer * share : (peer + 1) * share]


def values_kernel(got_ref, uv_ref, resid_ref, out_ref, wide):
    n_dp = got_ref.shape[0]
    share, latent, vh = uv_ref.shape
    for src in range(n_dp):
        for k in range(latent // 128):
            wide[k, src * share : (src + 1) * share, :] = got_ref[
                src, 0:share, 128 * k : 128 * (k + 1)
            ].astype(jnp.float32)
    piece = resid_ref.shape[1] // n_dp
    row = resid_ref[...].astype(jnp.float32)
    out_ref[:, share * vh :] = jnp.concatenate(
        [row[:, src * piece : (src + 1) * piece] for src in range(n_dp)], axis=0
    ).astype(jnp.bfloat16)
    for head in range(share):
        rows = jnp.concatenate(
            [wide[k, pl.ds(head, n_dp, stride=share), :] for k in range(latent // 128)], axis=1
        ).astype(jnp.bfloat16)
        out_ref[:, head * vh : (head + 1) * vh] = jnp.dot(
            rows, uv_ref[head], preferred_element_type=jnp.float32
        ).astype(jnp.bfloat16)


def interleave(first, second):
    n = first.shape[0]
    row = lax.broadcasted_iota(jnp.int32, (2 * n, 2 * n), 0)
    col = lax.broadcasted_iota(jnp.int32, (2 * n, 2 * n), 1)
    pick = (col == (row % 2) * n + row // 2).astype(jnp.bfloat16)
    both = jnp.concatenate([first, second], axis=0)
    return jnp.dot(pick, both, preferred_element_type=jnp.float32).astype(jnp.bfloat16)


def project_kernel(n_sub, own_ref, peer_ref, w_ref, sum_ref, out_ref, weights, sems):
    requests, half = out_ref.shape
    n_dp = requests // n_sub
    depth = w_ref.shape[0]
    chunks = sems.shape[0]
    wide = half // chunks
    rank, core, _ = place(n_sub)

    def fetch(i):
        start = pl.multiple_of(core * half + i * wide, 128)
        return pltpu.make_async_copy(
            w_ref.at[:, pl.ds(start, wide)], weights.at[i], sems.at[i]
        )

    for i in range(chunks):
        fetch(i).start()
    own = own_ref[:, :depth].astype(jnp.float32)
    peer = peer_ref[:, :depth].astype(jnp.float32)
    first = jnp.where(core == 0, own, peer).astype(jnp.bfloat16)
    second = jnp.where(core == 0, peer, own).astype(jnp.bfloat16)
    values = interleave(first, second)

    def resid_of(ref):
        every = ref[:, depth:].astype(jnp.float32)
        near = jnp.where(core == 0, every[: n_dp // 2], every[n_dp // 2 :])
        return jnp.concatenate([near[i : i + 1] for i in range(n_dp // 2)], axis=1)

    mine = resid_of(own_ref)
    theirs = resid_of(peer_ref)
    row = lax.broadcasted_iota(jnp.int32, (requests, wide), 0)
    for i in range(chunks):
        fetch(i).wait()
        span = slice(i * wide, (i + 1) * wide)
        part = jnp.dot(values, weights[i], preferred_element_type=jnp.float32)
        near = jnp.where(row % n_sub == core, mine[:, span], theirs[:, span])
        part = part + jnp.where(row // n_sub == rank, near, 0.0)
        sum_ref[:, span] = part
        out_ref[:, span] = part.astype(jnp.bfloat16)


def add_kernel(own_ref, peer_ref, sum_ref, send_ref):
    total = own_ref[...] + peer_ref[...].astype(jnp.float32)
    sum_ref[...] = total
    send_ref[...] = total.astype(jnp.bfloat16)


def last_add_kernel(own_ref, peer_ref, out_ref):
    out_ref[...] = (own_ref[...] + peer_ref[...].astype(jnp.float32)).astype(jnp.bfloat16)


def crosses(moves, core, step):
    source, target = moves[core, 1], moves[core, 2]
    bits = {1: (1,), 2: (2, 4), 6: (4,)}[step]
    return sum(source // bit + target // bit for bit in bits) % 2 != 0


def hop_kernel(n_sub, step, moves, kept_ref, come_ref, out_ref):
    _, core, _ = place(n_sub)
    crossing = crosses(moves, core, step)

    @pl.when(crossing)
    def _():
        out_ref[...] = come_ref[...]

    @pl.when(jnp.logical_not(crossing))
    def _():
        out_ref[...] = kept_ref[...]


def finish_kernel(n_sub, steps, moves, near_ref, near_come_ref, far_ref, far_come_ref, out_ref):
    rank, core, _ = place(n_sub)
    width = out_ref.shape[1]
    wanted = rank == moves[core, 2]
    pairs = ((near_ref, near_come_ref), (far_ref, far_come_ref))

    @pl.when(jnp.logical_not(wanted))
    def _():
        out_ref[...] = jnp.zeros_like(out_ref)

    @pl.when(wanted)
    def _():
        for part, (step, (kept_ref, come_ref)) in enumerate(zip(steps, pairs)):
            kept = kept_ref[...].astype(jnp.float32)
            come = come_ref[...].astype(jnp.float32)
            picked = jnp.where(crosses(moves, core, step), come, kept)
            rows = kept_ref.shape[0] * 128 // width
            first = part * (out_ref.shape[0] - rows)
            out_ref[first : first + rows, :] = unpack(picked, rows, width).astype(jnp.bfloat16)


def gate_up_kernel(
    n_sub, own_ref, peer_ref, gain_ref, gate_ref, up_ref, out_ref, base_ref, whole
):
    half = own_ref.shape[1]
    cols = base_ref.shape[1]
    rank, core, _ = place(n_sub)

    own = own_ref[...].astype(jnp.float32)
    peer = peer_ref[...].astype(jnp.float32)
    whole[:, :half] = jnp.where(core == 0, own, peer)
    whole[:, half:] = jnp.where(core == 0, peer, own)
    xf = whole[...]
    inverse = lax.rsqrt(jnp.mean(xf * xf, axis=1, keepdims=True) + 1e-06)
    normed = (xf * inverse * gain_ref[...].astype(jnp.float32).reshape(1, -1)).astype(jnp.bfloat16)
    start = pl.multiple_of(rank * n_sub * cols + core * (cols // 128 * 128), 128)
    near = whole[:, pl.ds(start, cols + 64)]
    base_ref[...] = jnp.where(core == 0, near[:, :cols], near[:, 64:]).astype(jnp.bfloat16)
    gate = lax.dot_general(gate_ref[...], normed, NT, preferred_element_type=jnp.float32)
    up = lax.dot_general(up_ref[...], normed, NT, preferred_element_type=jnp.float32)
    hidden = pack((gate * jax.nn.sigmoid(gate) * up).T).astype(jnp.bfloat16)
    for dst in range(out_ref.shape[0]):
        out_ref[dst] = hidden


def down_kernel(n_sub, own_ref, peer_ref, base_ref, down_ref, out_ref, hidden):
    requests = out_ref.shape[0]
    units = own_ref.shape[1] * 128 // requests
    _, core, _ = place(n_sub)

    for src in range(own_ref.shape[0]):
        own = unpack(own_ref[src].astype(jnp.float32), requests, units)
        peer = unpack(peer_ref[src].astype(jnp.float32), requests, units)
        first = jnp.where(core == 0, own, peer)
        second = jnp.where(core == 0, peer, own)
        hidden[:, src * n_sub * units : (src + 1) * n_sub * units] = jnp.concatenate(
            [first, second], axis=1
        ).astype(jnp.bfloat16)
    down = lax.dot_general(
        down_ref[...], hidden[...], NT, preferred_element_type=jnp.float32
    ).T
    out_ref[...] = (base_ref[...].astype(jnp.float32) + down).astype(jnp.bfloat16)


def swap(x, n_sub):
    return lax.ppermute(x, "sub", [(i, (i + 1) % n_sub) for i in range(n_sub)])


def exchange(x):
    return lax.all_to_all(x, "dp", split_axis=0, concat_axis=0, tiled=True)


def per_device_fast(
    queries, new_latent, cache, lengths, moves, resid, w_uv, w_out, norm_gain, w_gate, w_up, w_down
):
    n_dp = lax.axis_size("dp")
    n_sub = lax.axis_size("sub")
    cap, width = cache.shape[1:]
    heads = queries.shape[1]
    share, latent, vh = w_uv.shape
    half = cap // 2
    dim = w_out.shape[1]
    requests = n_dp * n_sub
    units = w_gate.shape[1]
    cols = w_down.shape[1]
    cut = half * 2//3 // 32 * 32
    scale = (vh + width - latent) ** (-0.5)
    bf16, f32 = jnp.bfloat16, jnp.float32

    positions = pl.pallas_call(
        position_kernel,
        out_shape=jax.ShapeDtypeStruct((8, cap), jnp.int32),
        out_specs=VMEM,
        compiler_params=params(8),
        cost_estimate=cost(40),
        name="positions",
    )()
    kept, sent, near, far = pl.pallas_call(
        functools.partial(attend_kernel, scale, n_dp, n_sub, latent),
        out_shape=(
            jax.ShapeDtypeStruct((width, cap), bf16),
            jax.ShapeDtypeStruct((n_dp, share, latent), bf16),
            jax.ShapeDtypeStruct((cut * width // 128, 128), bf16),
            jax.ShapeDtypeStruct(((half - cut) * width // 128, 128), bf16),
        ),
        in_specs=[SMEM] * 2 + [VMEM] * 4,
        out_specs=(VMEM,) * 4,
        compiler_params=params(8),
        cost_estimate=cost(24),
        name="attend",
    )(lengths, moves, positions, queries[0].T, new_latent, cache[0].T)
    got, near, far = lax.optimization_barrier((exchange(sent), near, far))
    wide_half = dim // n_sub
    values = pl.pallas_call(
        values_kernel,
        out_shape=jax.ShapeDtypeStruct((n_dp, share * vh + dim // n_dp), bf16),
        in_specs=[VMEM] * 3,
        out_specs=VMEM,
        scratch_shapes=[pltpu.VMEM((latent // 128, n_dp * share, 128), f32)],
        compiler_params=params(8),
        cost_estimate=cost(1),
        name="values",
    )(got, w_uv, resid)
    peer_values = swap(values, n_sub)
    def cross(x, step):
        return lax.ppermute(x, "dp", [(i, i ^ step) for i in range(n_dp)])

    def hop(step, here, come):
        return pl.pallas_call(
            functools.partial(hop_kernel, n_sub, step),
            out_shape=jax.ShapeDtypeStruct(here.shape, bf16),
            in_specs=[SMEM, VMEM, VMEM],
            out_specs=VMEM,
            compiler_params=params(8),
            cost_estimate=cost(1),
            name="hop",
        )(moves, here, come)

    def add(total, come):
        return pl.pallas_call(
            add_kernel,
            out_shape=(
                jax.ShapeDtypeStruct((requests, wide_half), f32),
                jax.ShapeDtypeStruct((requests, wide_half), bf16),
            ),
            in_specs=[VMEM] * 2,
            out_specs=(VMEM, VMEM),
            compiler_params=params(8),
            cost_estimate=cost(1),
            name="add",
        )(total, come)

    near_come = cross(near, 6)
    far_come = cross(far, 2)
    total, part = pl.pallas_call(
        functools.partial(project_kernel, n_sub),
        out_shape=(
            jax.ShapeDtypeStruct((requests, wide_half), f32),
            jax.ShapeDtypeStruct((requests, wide_half), bf16),
        ),
        in_specs=[VMEM, VMEM, HBM],
        out_specs=(VMEM, VMEM),
        scratch_shapes=[
            pltpu.VMEM((4, share * vh, wide_half // 4), bf16),
            pltpu.SemaphoreType.DMA((4,)),
        ],
        compiler_params=params(38),
        cost_estimate=cost(24),
        name="project",
    )(values, peer_values, w_out)
    near_come, far_come, part = lax.optimization_barrier((near_come, far_come, part))
    near = hop(6, near, near_come)
    far = hop(2, far, far_come)
    near_come = cross(near, 2)
    total, part = add(total, cross(part, 1))
    far, part = lax.optimization_barrier((far, part))
    near = hop(2, near, near_come)
    near_come = cross(near, 1)
    far_come = cross(far, 1)
    total, part = add(total, cross(part, 2))
    far = hop(1, far, far_come)
    come, near_come, far = lax.optimization_barrier((cross(part, 6), near_come, far))
    x_half = pl.pallas_call(
        last_add_kernel,
        out_shape=jax.ShapeDtypeStruct((requests, wide_half), bf16),
        in_specs=[VMEM] * 2,
        out_specs=VMEM,
        compiler_params=params(8),
        cost_estimate=cost(1),
        name="last_add",
    )(total, come)
    far_come = cross(far, 6)
    hidden, base = pl.pallas_call(
        functools.partial(gate_up_kernel, n_sub),
        out_shape=(
            jax.ShapeDtypeStruct((n_dp, requests * units // 128, 128), bf16),
            jax.ShapeDtypeStruct((requests, cols), bf16),
        ),
        in_specs=[VMEM] * 5,
        out_specs=(VMEM, VMEM),
        scratch_shapes=[pltpu.VMEM((requests, dim), f32)],
        compiler_params=params(24),
        cost_estimate=cost(24),
        name="gate_up",
    )(x_half, swap(x_half, n_sub), norm_gain, w_gate.T, w_up.T)
    hidden, far_come = lax.optimization_barrier((hidden, far_come))
    every = exchange(hidden)
    mixed = pl.pallas_call(
        functools.partial(down_kernel, n_sub),
        out_shape=jax.ShapeDtypeStruct((requests, cols), bf16),
        in_specs=[VMEM] * 4,
        out_specs=VMEM,
        scratch_shapes=[pltpu.VMEM((requests, n_dp * n_sub * units), bf16)],
        compiler_params=params(16),
        cost_estimate=cost(1),
        name="down",
    )(every, swap(every, n_sub), base, w_down.T)
    spare = pl.pallas_call(
        functools.partial(finish_kernel, n_sub, (1, 6)),
        out_shape=jax.ShapeDtypeStruct((half, width), bf16),
        in_specs=[SMEM] + [VMEM] * 4,
        out_specs=VMEM,
        compiler_params=params(8),
        cost_estimate=cost(1),
        name="finish",
    )(moves, near, near_come, far, far_come)
    return (kept.T[None], spare[None], mixed)


def per_device(*args):
    queries, cache, moves, w_uv, w_out = args[0], args[2], args[4], args[6], args[7]
    w_gate, w_down = args[9], args[11]
    n_dp = lax.axis_size("dp")
    n_sub = lax.axis_size("sub")
    fits = (
        n_sub == 2
        and n_dp == 8
        and moves.shape[0] == n_sub
        and cache.shape[1] % 128 == 0
        and queries.shape[1] // n_dp == 16
        and w_uv.shape[1] == 512
        and w_out.shape[1] % (n_sub * 4 * 128) == 0
        and w_gate.shape[1] % 128 == 64
        and cache.shape[2] % 128 == 64
        and w_down.shape[1] % 64 == 0
    )
    return per_device_fast(*args) if fits else per_device_any(*args)


def solution(mesh):
    return jax.shard_map(
        per_device,
        mesh=mesh,
        in_specs=(
            P(("groups", "dp", "sub"), None, None),
            P(("groups", "dp", "sub"), None),
            P(("groups", "dp", "sub"), None, None),
            P("groups"),
            P("groups", None),
            P(("groups", "dp", "sub"), None),
            P("dp", None, None),
            P("dp", None),
            P(),
            P(None, ("dp", "sub")),
            P(None, ("dp", "sub")),
            P(None, ("dp", "sub")),
        ),
        out_specs=(
            P(("groups", "dp", "sub"), None, None),
            P(("groups", "dp", "sub"), None, None),
            P("groups", ("dp", "sub")),
        ),
        check_vma=False,
    )
```
